32 devices in a mesh: gx: 4 (over z), gy: 4 (over y, x), gz: 2 (over core).
Axes of the slice: x: 2, y: 2, z: 4, core: 2. Of those that a mesh axis runs over, the one named last changes fastest.
Arguments:
- offsets: float32 [3, 16, 16, 4, 128], P(None, 'gx', 'gy', 'gz'), may hold values from -0.5 to 0.5
- burgers: float32 [3, 16, 16, 4, 128], P(None, 'gx', 'gy', 'gz'), may hold values from -4 to 4
- line: float32 [3, 16, 16, 4, 128], P(None, 'gx', 'gy', 'gz'), may hold values from -3 to 3
- block_fill: int32 [16, 16, 4], P('gx', 'gy', 'gz'), may hold values from 1 to 128, as said below
- near_pairs: int32 [6144], P(('gx', 'gy', 'gz')), may hold values from 0 to 447, as said below
- pair_count: int32 [32], P(('gx', 'gy', 'gz')), may hold values from 24 to 192, as said below
Outputs:
- forces: float32 [3, 16, 16, 4, 128], P(None, 'gx', 'gy', 'gz')
The draws below stay inside these ranges and needn't reach their ends.
Inputs may be any that keep to these rules, and one draw needn't show every extreme that they name: `block_fill`: some block in every draw holds exactly 128 live segments. `near_pairs`: within each device's 192 entries the codes are distinct; each device's first four entries are 5, 7, 9 and 447, and code 0 is among its entries. `pair_count`: some device has exactly 192 live entries.
All inputs are finite; a program needn't handle non-finite values.
Results may differ from the reference program's by a relative error of at most 0.0003.
Values sent between devices are 32-bit elements; how exact they have to be, the bound alone decides.
No kernel may reach another device: no remote copies, remote signals or barrier semaphores. Data moves between devices by JAX's collectives and lax.ppermute only.
A program may use at most 64 MiB of HBM per device.

```python
import math
import jax
import jax.numpy as jnp
import numpy as np
from jax import lax

BX = 4
BY = 4
BZ = 2
SLOT = 128
NBX = 16
NBY = 16
NBZ = 4
BLK_DEV = 32
PAIRS_DEV = 192
PAIRS_ALL = 6144
CGX = 8
CGY = 8
CGZ = 2
N_GY = 4
N_GZ = 2


def draw_block_fill(key, part):
    key = jax.random.fold_in(key, 11)
    first_key, second_key = jax.random.split(key)
    total_blocks = NBX * NBY * NBZ
    fills = jax.random.randint(first_key, (total_blocks,), 1, SLOT + 1)
    chosen = jax.random.randint(second_key, (), 0, total_blocks)
    fills = jnp.where(jnp.arange(total_blocks) == chosen, SLOT, fills)
    return fills.reshape(NBX, NBY, NBZ).astype(jnp.int32)


def draw_near_pairs(key, part):
    key = jax.random.fold_in(key, 23)
    device_count = PAIRS_ALL // PAIRS_DEV
    device_keys = jax.random.split(key, device_count)
    top_code = BLK_DEV * 14 - 1
    leading = np.array([5, 7, 9, top_code, 0], dtype=np.int32)
    others = np.array([c for c in range(1, top_code) if c not in (5, 7, 9)], dtype=np.int32)

    def one_device(device_key):
        picked = jax.random.permutation(device_key, jnp.asarray(others))[:PAIRS_DEV - 5]
        tail = jax.random.permutation(jax.random.fold_in(device_key, 1), jnp.concatenate([jnp.zeros((1,), jnp.int32), picked.astype(jnp.int32)]))
        return jnp.concatenate([jnp.asarray(leading[:4]), tail])
    return jax.vmap(one_device)(device_keys).reshape(-1).astype(jnp.int32)


def draw_pair_count(key, part):
    key = jax.random.fold_in(key, 37)
    base_key, heavy_key, pick_key = jax.random.split(key, 3)
    device_count = PAIRS_ALL // PAIRS_DEV
    counts = jax.random.randint(base_key, (device_count,), PAIRS_DEV // 8, PAIRS_DEV // 2 + 1)
    heavy = jax.random.randint(heavy_key, (device_count,), 0, 16) == 0
    chosen = jax.random.randint(pick_key, (), 0, device_count)
    full = heavy | (jnp.arange(device_count) == chosen)
    return jnp.where(full, PAIRS_DEV, counts).astype(jnp.int32)


def levels(key, dims, cuts, least, largest):
    def one(dim, shards_of):
        steps = jax.random.uniform(jax.random.fold_in(jax.random.fold_in(key, 6), dim), (shards_of,), jnp.float32, least / len(cuts), largest / len(cuts))
        return jnp.repeat(jnp.exp(steps), dims[dim] // shards_of).reshape((-1,) + (1,) * (len(dims) - dim - 1))

    level = one(*cuts[0])
    for cut in cuts[1:]:
        level = level * one(*cut)
    return level


def normal_values(own_key, shape, deviation, bound, pieces=(), kind=jnp.bfloat16):
    gain = levels(own_key, shape, pieces, -0.22, 0.18) if pieces else 1.0
    values = jax.random.normal(own_key, shape, jnp.float32) * deviation * gain
    return jnp.minimum(jnp.maximum(values, -bound), bound).astype(kind)


def setup_inputs(seed: int = 0) -> dict:
    key_of = jax.random.split(jax.random.key(seed), 7)
    return {
        "offsets": jnp.clip(jax.random.uniform(key_of[0], (3, NBX, NBY, NBZ, SLOT), jnp.float32, -0.5, 0.5) * levels(key_of[0], (3, NBX, NBY, NBZ, SLOT), ((1, 4), (2, 4), (3, 2)), -0.4, 0.0), -0.5, 0.5),
        "burgers": normal_values(key_of[1], (3, NBX, NBY, NBZ, SLOT), 1.0, 4.0, ((1, 4), (2, 4), (3, 2)), jnp.float32),
        "line": normal_values(key_of[2], (3, NBX, NBY, NBZ, SLOT), 0.5, 3.0, ((1, 4), (2, 4), (3, 2)), jnp.float32),
        "block_fill": draw_block_fill(jax.random.fold_in(key_of[6], 71), 0),
        "near_pairs": draw_near_pairs(jax.random.fold_in(key_of[6], 71), 0),
        "pair_count": draw_pair_count(jax.random.fold_in(key_of[6], 71), 0),
    }


stencil_table = np.array([[0, 0, 0], [1, 0, 0], [0, 1, 0], [0, 0, 1], [1, 1, 0], [-1, 1, 0], [1, 0, 1], [1, 0, -1], [0, 1, 1], [0, -1, 1], [1, 1, -1], [1, -1, 1], [-1, 1, 1], [1, 1, 1]], dtype=np.int32)
kernel_scale = 1.0 / (8.0 * math.pi)
core_square = 0.09


def cross_product(left, right):
    return jnp.stack([left[1] * right[2] - left[2] * right[1], left[2] * right[0] - left[0] * right[2], left[0] * right[1] - left[1] * right[0]])


def pair_terms(side_a, side_b, shift_vec):
    offset_a, burgers_a, line_a = side_a[0:3], side_a[3:6], side_a[6:9]
    offset_b, burgers_b, line_b = side_b[0:3], side_b[3:6], side_b[6:9]
    separation = offset_a[:, :, None] - offset_b[:, None, :] - shift_vec[:, None, None]
    weight = (jnp.sum(separation * separation, 0) + core_square) ** -1.5
    turn_b = cross_product(separation, burgers_b[:, None, :])
    along_b = jnp.sum(line_b[:, None, :] * burgers_a[:, :, None], 0)
    project_b = jnp.sum(burgers_a[:, :, None] * turn_b, 0)
    force_a = jnp.sum(weight * (along_b * turn_b + project_b * line_b[:, None, :]), 2)
    turn_a = -cross_product(separation, burgers_a[:, :, None])
    along_a = jnp.sum(line_a[:, :, None] * burgers_b[:, None, :], 0)
    project_a = jnp.sum(burgers_b[:, None, :] * turn_a, 0)
    force_b = jnp.sum(weight * (along_a * turn_a + project_a * line_a[:, :, None]), 1)
    return force_a, force_b


def far_terms(target_coords, source_coords, moments, grid_shape):
    deltas = []
    for which_dim in range(3):
        extent = grid_shape[which_dim]
        delta = target_coords[which_dim][:, None] - source_coords[which_dim][None, :]
        delta = (delta + extent // 2) % extent - extent // 2
        deltas.append(delta)
    close = (deltas[0] == 0) & (deltas[1] == 0) & (deltas[2] == 0)
    lengths = [2.0 * delta.astype(jnp.float32) for delta in deltas]
    radius = lengths[0] * lengths[0] + lengths[1] * lengths[1] + lengths[2] * lengths[2]
    weight = jnp.where(close, jnp.float32(0.0), (radius + core_square) ** -1.5)
    scaled = jnp.stack([weight * length for length in lengths])
    summed = jnp.einsum("mts,nks->mnkt", scaled, moments, precision=lax.Precision.HIGHEST)
    return jnp.stack([summed[1, 2] - summed[2, 1], summed[2, 0] - summed[0, 2], summed[0, 1] - summed[1, 0]])


def reference(offsets, burgers, line, block_fill, near_pairs, pair_count):
    nblocks = NBX * NBY * NBZ
    slot_live = (lax.broadcasted_iota(jnp.int32, (NBX, NBY, NBZ, SLOT), 3) < block_fill[..., None]).astype(jnp.float32)
    burgers_live = burgers * slot_live
    line_live = line * slot_live
    segments = jnp.concatenate([offsets, burgers_live, line_live], axis=0).reshape(9, nblocks, SLOT)
    stencil = jnp.asarray(stencil_table)
    ordinal = jnp.arange(PAIRS_ALL, dtype=jnp.int32)
    device = ordinal // PAIRS_DEV
    pair_live = ((ordinal % PAIRS_DEV) < pair_count[device]).astype(jnp.float32)
    dev_x = device // (N_GY * N_GZ)
    dev_y = (device // N_GZ) % N_GY
    dev_z = device % N_GZ
    block_no = near_pairs // 14
    code_no = near_pairs % 14
    first_x = dev_x * BX + block_no // (BY * BZ)
    first_y = dev_y * BY + (block_no // BZ) % BY
    first_z = dev_z * BZ + block_no % BZ
    shift_vec = stencil[code_no]
    second_x = (first_x + shift_vec[:, 0]) % NBX
    second_y = (first_y + shift_vec[:, 1]) % NBY
    second_z = (first_z + shift_vec[:, 2]) % NBZ
    first_block = (first_x * NBY + first_y) * NBZ + first_z
    second_block = (second_x * NBY + second_y) * NBZ + second_z
    self_free = (code_no != 0).astype(jnp.float32)

    def accumulate(totals, entry):
        block_a, block_b, shifts, live_now, free_now = entry
        side_a = jnp.moveaxis(segments[:, block_a], 0, 1)
        side_b = jnp.moveaxis(segments[:, block_b], 0, 1)
        force_a, force_b = jax.vmap(pair_terms)(side_a, side_b, shifts)
        force_a = force_a * live_now[:, None, None]
        force_b = force_b * (live_now * free_now)[:, None, None]
        totals = totals.at[:, block_a].add(jnp.moveaxis(force_a, 0, 1))
        totals = totals.at[:, block_b].add(jnp.moveaxis(force_b, 0, 1))
        return totals, None

    entries = (first_block.reshape(-1, 64), second_block.reshape(-1, 64), shift_vec.astype(jnp.float32).reshape(-1, 64, 3), pair_live.reshape(-1, 64), self_free.reshape(-1, 64))
    near_sum, _ = lax.scan(accumulate, jnp.zeros((3, nblocks, SLOT), jnp.float32), entries)
    near_sum = near_sum.reshape(3, NBX, NBY, NBZ, SLOT)

    moments = jnp.einsum("nxaybzcs,kxaybzcs->nkxyz", burgers_live.reshape(3, CGX, 2, CGY, 2, CGZ, 2, SLOT), line_live.reshape(3, CGX, 2, CGY, 2, CGZ, 2, SLOT), precision=lax.Precision.HIGHEST)
    flat_moments = moments.reshape(3, 3, CGX * CGY * CGZ)
    cells = jnp.arange(CGX * CGY * CGZ, dtype=jnp.int32)
    sources = jnp.stack([cells // (CGY * CGZ), (cells // CGZ) % CGY, cells % CGZ])
    plane_cells = jnp.arange(CGY * CGZ, dtype=jnp.int32)

    def per_plane(plane_x):
        targets = jnp.stack([jnp.zeros_like(plane_cells) + plane_x, plane_cells // CGZ, plane_cells % CGZ])
        return far_terms(targets, sources, flat_moments, (CGX, CGY, CGZ))

    far_field = lax.map(per_plane, jnp.arange(CGX, dtype=jnp.int32))
    far_field = jnp.moveaxis(far_field, 0, 2).reshape(3, 3, CGX, CGY, CGZ)
    stress = far_field + jnp.swapaxes(far_field, 0, 1)
    far_push = jnp.einsum("ikxyz,kxaybzcs->ixaybzcs", stress, burgers_live.reshape(3, CGX, 2, CGY, 2, CGZ, 2, SLOT), precision=lax.Precision.HIGHEST).reshape(3, NBX, NBY, NBZ, SLOT)
    return kernel_scale * cross_product(near_sum + far_push, line_live)
```

```python
import functools
import math

import jax
import jax.numpy as jnp
import numpy as np
from jax import lax
from jax.experimental import pallas as pl
from jax.experimental.pallas import tpu as pltpu
from jax.sharding import PartitionSpec as P

stencil_table = (
    (0, 0, 0),
    (1, 0, 0),
    (0, 1, 0),
    (0, 0, 1),
    (1, 1, 0),
    (-1, 1, 0),
    (1, 0, 1),
    (1, 0, -1),
    (0, 1, 1),
    (0, -1, 1),
    (1, 1, -1),
    (1, -1, 1),
    (-1, 1, 1),
    (1, 1, 1),
)
code_total = len(stencil_table)
kernel_scale = 1.0 / (8.0 * math.pi)
core_square = 0.09
lanes = 128
parts_sent = 10
unroll = 24
f32 = jnp.float32
bf16 = jnp.bfloat16


def block_layout(bx, by, bz):
    coords = []
    layers = [(z, z + 1) for z in range(bz)]
    beside = [(z, bz + 1 if z == 0 else 0) for z in range(bz)]
    for z_of in (layers, beside):
        group = [
            [(x + 1, y + 1, z) for x in range(bx) for y in range(by) for _, z in z_of],
            [(0, y + 1, z) for y in range(by) for _, z in z_of],
            [(bx + 1, y + 1, z) for y in range(by) for _, z in z_of],
            [(x, 0, z) for x in range(bx + 2) for _, z in z_of],
            [(x, by + 1, z) for x in range(bx + 2) for _, z in z_of],
        ]
        coords.extend(group)
    return coords


def work_tables(bx, by, bz):
    groups = block_layout(bx, by, bz)
    flat = [c for group in groups for c in group]
    number = {c: i for i, c in enumerate(flat)}
    own = bx * by * bz
    forward, backward, inbound = [], [], []
    for a in range(own):
        for code, o in enumerate(stencil_table):
            b = number[tuple(flat[a][d] + o[d] for d in range(3))]
            forward.append(a | b << 8)
            backward.append(b | a << 8 if b < own and code else -1)
    for h in range(own, len(flat)):
        for code, o in enumerate(stencil_table):
            b = number.get(tuple(flat[h][d] + o[d] for d in range(3)), own)
            if b < own:
                inbound.append(b | h << 8 | code << 16)
    while len(inbound) % 8:
        inbound.append(-1)
    return np.array(forward, np.int32), np.array(backward, np.int32), np.array(inbound, np.int32)


def position(group, rows, bx, by, bz):
    row = lax.broadcasted_iota(jnp.int32, (rows, lanes), 0)
    z = row % bz
    line = row // bz
    kind = group % 5
    if kind == 0:
        x, y = line // by + 1, line % by + 1
    elif kind <= 2:
        x, y = jnp.full_like(row, 0 if kind == 1 else bx + 1), line + 1
    else:
        x, y = line, jnp.full_like(row, 0 if kind == 3 else by + 1)
    if group < 5:
        z = z + 1
    else:
        z = jnp.where(z == 0, bz + 1, 0)
    sides = (bx + 1, by + 1, bz + 1)
    return [v.astype(f32) - 0.5 * side for v, side in zip((x, y, z), sides)]


def moment_rows(b, l):
    zz = b[2] * l[2]
    return [
        b[0] * l[1],
        b[0] * l[2],
        b[1] * l[0],
        b[1] * l[2],
        b[2] * l[0],
        b[2] * l[1],
        b[0] * l[0] - zz,
        b[1] * l[1] - zz,
    ]


def cross_rows(q, b, l):
    c = [q[1] * b[2] - q[2] * b[1], q[2] * b[0] - q[0] * b[2], q[0] * b[1] - q[1] * b[0]]
    return [
        2.0 * c[0] * l[0],
        2.0 * c[1] * l[1],
        2.0 * c[2] * l[2],
        c[0] * l[1] + c[1] * l[0],
        c[0] * l[2] + c[2] * l[0],
        c[1] * l[2] + c[2] * l[1],
    ]


def turn_rows(r, m):
    return [
        2.0 * (r[1] * m[4] - r[2] * m[2]),
        2.0 * (r[2] * m[0] - r[0] * m[5]),
        2.0 * (r[0] * m[3] - r[1] * m[1]),
        r[1] * m[5] - r[0] * m[4] + r[2] * (m[6] - m[7]),
        r[0] * m[2] - r[2] * m[3] - r[1] * m[6],
        r[2] * m[1] + r[0] * m[7] - r[1] * m[0],
    ]


def pieces(value):
    first = value.astype(bf16).astype(f32)
    rest = value - first
    second = rest.astype(bf16).astype(f32)
    return first, second, rest - second


def distance_rows(q):
    near = q[0] * q[0] + q[1] * q[1] + q[2] * q[2]
    one = jnp.ones_like(near)
    left, right = [], []
    for axis in q:
        p1, p2, p3 = pieces(axis)
        left += [p1, p1, p2, p2, p1, p3]
        right += [-2.0 * v for v in (p1, p2, p1, p2, p3, p1)]
    left += [*pieces(near), one, one, one]
    right += [one, one, one, *pieces(near + core_square)]
    return left, right


def pack_kernel(sizes, axes, fill, count, offsets, burgers, line, pairs, own, face_lo, face_hi, mom):
    bx, by, bz, cells = sizes
    total, face = bx * by * bz, by * bz
    lane = lax.broadcasted_iota(jnp.int32, (total, lanes), 1)
    row = lax.broadcasted_iota(jnp.int32, (total, lanes), 0)
    level = jnp.zeros((total, lanes), jnp.int32)
    for block in range(total):
        here = fill[block // (by * bz), block // bz % by, block % bz]
        level = jnp.where(row == block, here, level)
    live = lane < level
    b, l = [], []
    for d in range(3):
        own[d] = offsets[d]
        b.append(jnp.where(live, burgers[d], 0.0))
        l.append(jnp.where(live, line[d], 0.0))
        own[3 + d] = b[d]
        own[6 + d] = l[d]
    entries = pairs.shape[1]
    code = pairs[...]
    block_no = code // code_total
    code_no = code - block_no * code_total
    alive = lax.broadcasted_iota(jnp.int32, (1, entries), 1) < count[0]
    of_block = lax.broadcasted_iota(jnp.int32, (total, entries), 0) == block_no
    of_code = lax.broadcasted_iota(jnp.int32, (lanes, entries), 0) == code_no
    own[9] = lax.dot_general(
        jnp.where(of_block & alive, 1.0, 0.0).astype(bf16),
        jnp.where(of_code, 1.0, 0.0).astype(bf16),
        (((1,), (1,)), ((), ())),
        preferred_element_type=f32,
    )
    cx, cy, cz = bx // 2, by // 2, bz // 2
    here = lax.axis_index(axes[0])
    for axis in axes[1:]:
        here = here * lax.axis_size(axis) + lax.axis_index(axis)
    first_lane = here * (cx * cy * cz)
    wide = lax.broadcasted_iota(jnp.int32, (face, lanes), 1)
    deep = lax.broadcasted_iota(jnp.int32, (face, lanes), 0)
    local = deep // (2 * bz) * cz + deep % bz // 2
    sums = []
    for feature in moment_rows(b, l):
        column = []
        for x in range(cx):
            both = feature[2 * x * face : (2 * x + 1) * face] + feature[(2 * x + 1) * face : (2 * x + 2) * face]
            column.append(jnp.sum(both, 1, keepdims=True))
        sums.append(column)
    for chunk in range(cells // lanes):
        for f, column in enumerate(sums):
            placed = jnp.zeros((face, lanes), f32)
            for x in range(cx):
                lane_of = first_lane + x * cy * cz + local - chunk * lanes
                placed = placed + jnp.where(wide == lane_of, column[x], 0.0)
            mom[chunk * 8 + f : chunk * 8 + f + 1, :] = jnp.sum(placed, 0, keepdims=True)
    for d in range(parts_sent):
        face_lo[d * face : (d + 1) * face] = own[d, 0:face]
        face_hi[d * face : (d + 1) * face] = own[d, total - face : total]
    face_lo[parts_sent * face :] = mom[...]
    face_hi[parts_sent * face :] = mom[...]


def force_kernel(sizes, axes, grid, tables, pairs, count, *refs):
    bx, by, bz, cells = sizes
    groups = refs[:10]
    mom_own, mom_beside, cell_of, out = refs[10:14]
    stage, left, right, weighed, acc, flags, flags_s, todo, sem = refs[14:]
    own = bx * by * bz
    face, rim = by * bz, (bx + 2) * bz
    heights = [own, face, face, rim, rim] * 2
    starts = [sum(heights[:k]) for k in range(10)]
    codes = own * code_total

    def part(group, d):
        if group % 5 == 0:
            return groups[group][d]
        return groups[group][d * heights[group] : (d + 1) * heights[group], :]

    for group in range(1, 10):
        flags[starts[group] - own : starts[group] - own + heights[group], :] = part(group, 9)
    flag_copy = pltpu.make_async_copy(flags, flags_s, sem)
    flag_copy.start()

    acc[...] = jnp.zeros_like(acc)
    zero = {h: jnp.zeros((h, lanes), f32) for h in set(heights)}

    def put(base, which, group, value):
        stage[pl.ds(starts[group] * 80 + base + which, heights[group], stride=80), :] = value

    for group in range(10):
        h = heights[group]
        place = position(group, h, bx, by, bz)
        q = [part(group, d) + place[d] for d in range(3)]
        b = [part(group, 3 + d) for d in range(3)]
        l = [part(group, 6 + d) for d in range(3)]
        rows = moment_rows(b, l) + cross_rows(q, b, l)
        for f, value in enumerate(rows + [zero[h]] * (16 - len(rows))):
            put(0, f, group, value)
        lhs, rhs = distance_rows(q)
        for f, value in enumerate(rhs + [zero[h]] * (32 - len(rhs))):
            put(16, f, group, value)
        if group == 0:
            for f, value in enumerate(lhs + [zero[h]] * (32 - len(lhs))):
                put(48, f, group, value)

    def shape_block(block, carry):
        base = pl.multiple_of(block * 80, 16)
        product = stage[pl.ds(base, 16), :]
        high = product.astype(bf16)
        low = (product - high.astype(f32)).astype(bf16)
        weighed[block, 0:16, 0:lanes] = high
        weighed[block, 0:16, lanes : 2 * lanes] = high
        weighed[block, 16:32, 0:lanes] = low
        weighed[block, 16:32, lanes : 2 * lanes] = jnp.zeros_like(low)
        right[block] = stage[pl.ds(base + 16, 32), :].astype(bf16)
        return carry

    lax.fori_loop(0, sum(heights), shape_block, 0, unroll=8)
    for block in range(own):
        left[block] = stage[block * 80 + 48 : block * 80 + 80, :].astype(bf16)
    left[own] = left[0]

    live_count = count[0]

    def list_own(step, n):
        for k in range(8):
            at = step * 8 + k
            code = pairs[at]
            alive = (at < live_count).astype(jnp.int32)
            todo[n] = tables[code]
            n = n + alive
            back = tables[codes + code]
            todo[n] = back
            n = n + jnp.where(back >= 0, alive, 0)
        return n

    n = lax.fori_loop(0, (live_count + 7) // 8, list_own, 0)
    flag_copy.wait()
    inbound = tables.shape[0] - 2 * codes

    def list_inbound(step, n):
        for k in range(8):
            entry = tables[2 * codes + step * 8 + k]
            h = jnp.maximum(entry >> 8 & 255, own) - own
            on = flags_s[h, entry >> 16 & 15]
            todo[n] = entry & 65535
            n = n + jnp.where((entry >= 0) & (on > 0.5), 1, 0)
        return n

    n = lax.fori_loop(0, inbound // 8, list_inbound, n)
    for k in range(unroll):
        todo[n + k] = own

    def interact(step, carry):
        results = []
        for k in range(unroll):
            entry = todo[step * unroll + k]
            row, col = entry & 255, entry >> 8
            square = lax.dot_general(
                right[col], left[row], (((0,), (0,)), ((), ())), preferred_element_type=f32
            )
            root = lax.rsqrt(square)
            weight = root * root * root
            high = weight.astype(bf16)
            low = (weight - high.astype(f32)).astype(bf16)
            both = jnp.dot(
                weighed[col], jnp.concatenate([high, low], 0), preferred_element_type=f32
            )
            results.append((row, both[0:16] + both[16:32]))
        for row, value in results:
            at = pl.ds(pl.multiple_of(row * 16, 16), 16)
            acc[at, :] += value
        return carry

    lax.fori_loop(0, (n + unroll - 1) // unroll, interact, 0)

    cx, cy, cz = bx // 2, by // 2, bz // 2
    deep = lax.broadcasted_iota(jnp.int32, (face, lanes), 0)
    local = (None, deep // (2 * bz), deep % bz // 2)
    far = [[] for _ in range(6)]
    for x in range(cx):
        totals = [jnp.zeros((face, lanes), f32)] * 6
        for chunk in range(cells // lanes):
            lengths = []
            close = jnp.zeros((face, lanes), f32)
            for d, axis in enumerate(axes):
                at = lax.axis_index(axis) * (cx, cy, cz)[d] + (x if d == 0 else local[d])
                delta = at - cell_of[d : d + 1, chunk * lanes : (chunk + 1) * lanes]
                half = grid[d] // 2
                delta = jnp.where(delta >= grid[d] - half, delta - grid[d], delta)
                delta = jnp.where(delta < -half, delta + grid[d], delta)
                lengths.append(2.0 * delta.astype(f32))
            radius = lengths[0] * lengths[0] + lengths[1] * lengths[1] + lengths[2] * lengths[2]
            root = lax.rsqrt(radius + core_square)
            weight = jnp.where(radius == 0.0, 0.0, root * root * root)
            m = mom_own[chunk * 8 : chunk * 8 + 8, :] + mom_beside[chunk * 8 : chunk * 8 + 8, :]
            m = [m[f : f + 1, :] for f in range(8)]
            turned = turn_rows([weight * v for v in lengths], m)
            totals = [t + v for t, v in zip(totals, turned)]
        for f in range(6):
            far[f].append(jnp.sum(totals[f], 1, keepdims=True))

    place = position(0, own, bx, by, bz)
    p = [groups[0][d] + place[d] for d in range(3)]
    b = [groups[0][3 + d] for d in range(3)]
    l = [groups[0][6 + d] for d in range(3)]
    moment = [acc[pl.ds(f, own, stride=16), :] for f in range(8)]
    crossed = [acc[pl.ds(8 + f, own, stride=16), :] for f in range(6)]
    turned = turn_rows(p, moment)
    s = []
    for f in range(6):
        column = jnp.concatenate([far[f][x // 2] for x in range(bx)], 0)
        s.append(turned[f] - crossed[f] + column)
    push = [
        s[0] * b[0] + s[3] * b[1] + s[4] * b[2],
        s[3] * b[0] + s[1] * b[1] + s[5] * b[2],
        s[4] * b[0] + s[5] * b[1] + s[2] * b[2],
    ]
    out[0] = kernel_scale * (push[1] * l[2] - push[2] * l[1])
    out[1] = kernel_scale * (push[2] * l[0] - push[0] * l[2])
    out[2] = kernel_scale * (push[0] * l[1] - push[1] * l[0])


def shifted(value, axis, step):
    size = lax.axis_size(axis)
    return lax.ppermute(value, axis, [(i, (i + step) % size) for i in range(size)])


def gather_sum(own, low, high, axis):
    size = lax.axis_size(axis)
    total = own + low
    if size > 2:
        total = total + high
    for step in range(2, size - 1):
        total = total + shifted(own, axis, step)
    return total


def beside_z(value, layers):
    size = lax.axis_size("gz")
    if size == 2:
        return shifted(value, "gz", 1)
    head = value.shape
    split = value.reshape(-1, layers, lanes)
    above = shifted(split[:, :1], "gz", -1)
    below = shifted(split[:, layers - 1 :], "gz", 1)
    middle = split[:, 1 : layers - 1]
    return jnp.concatenate([above, middle, below], 1).reshape(head)


def body(offsets, burgers, line, block_fill, near_pairs, pair_count):
    _, bx, by, bz, slots = offsets.shape
    axes = ("gx", "gy", "gz")
    sizes = [lax.axis_size(axis) for axis in axes]
    own, face, rim = bx * by * bz, by * bz, (bx + 2) * bz
    blocks = 2 * (own + 2 * face + 2 * rim)
    coarse = (bx // 2, by // 2, bz // 2)
    grid = tuple(c * n for c, n in zip(coarse, sizes))
    per_device = coarse[0] * coarse[1] * coarse[2]
    cells = per_device * sizes[0] * sizes[1] * sizes[2]
    mom_rows = 8 * cells // lanes
    kinds = (bx, by, bz, cells)
    vmem = pl.BlockSpec(memory_space=pltpu.VMEM)
    smem = pl.BlockSpec(memory_space=pltpu.SMEM)
    flat = lambda v: v.reshape(3, own, slots)
    offsets, burgers, line = flat(offsets), flat(burgers), flat(line)

    mine, face_lo, face_hi, mom = pl.pallas_call(
        functools.partial(pack_kernel, kinds, axes),
        out_shape=[
            jax.ShapeDtypeStruct((parts_sent, own, lanes), f32),
            jax.ShapeDtypeStruct((parts_sent * face + mom_rows, lanes), f32),
            jax.ShapeDtypeStruct((parts_sent * face + mom_rows, lanes), f32),
            jax.ShapeDtypeStruct((mom_rows, lanes), f32),
        ],
        in_specs=[smem, smem, vmem, vmem, vmem, vmem],
        out_specs=[vmem] * 4,
        name="pack",
    )(block_fill, pair_count, offsets, burgers, line, near_pairs.reshape(1, -1))

    x_lo = shifted(face_hi, "gx", 1)
    x_hi = shifted(face_lo, "gx", -1)
    head = parts_sent * face
    mom_x = gather_sum(mom, x_lo[head:], x_hi[head:], "gx")
    cut = lambda v, y: v[:head].reshape(parts_sent, 1, by, bz, lanes)[:, :, y]
    whole = mine.reshape(parts_sent, bx, by, bz, lanes)
    sides = []
    for y in (0, by - 1):
        side = jnp.concatenate([cut(x_lo, y), whole[:, :, y], cut(x_hi, y)], 1)
        sides.append(jnp.concatenate([side.reshape(parts_sent * rim, lanes), mom_x], 0))
    y_lo = shifted(sides[1], "gy", 1)
    y_hi = shifted(sides[0], "gy", -1)
    head = parts_sent * rim
    mom_xy = gather_sum(mom_x, y_lo[head:], y_hi[head:], "gy")
    mom_z = shifted(mom_xy, "gz", 1)
    for step in range(2, sizes[2]):
        mom_z = mom_z + shifted(mom_xy, "gz", step)
    x_lo, x_hi = x_lo[: parts_sent * face], x_hi[: parts_sent * face]
    y_lo, y_hi = y_lo[:head], y_hi[:head]
    here = [mine, x_lo, x_hi, y_lo, y_hi]
    beside = [beside_z(v, bz) for v in here]

    forward, backward, inbound = work_tables(bx, by, bz)
    tables = jnp.asarray(np.concatenate([forward, backward, inbound]))
    number = np.arange(cells)
    device, local = number // per_device, number % per_device
    cell_of = np.zeros((8, cells), np.int32)
    cell_of[0] = device // (sizes[1] * sizes[2]) * coarse[0] + local // (coarse[1] * coarse[2])
    cell_of[1] = device // sizes[2] % sizes[1] * coarse[1] + local // coarse[2] % coarse[1]
    cell_of[2] = device % sizes[2] * coarse[2] + local % coarse[2]
    entries = near_pairs.shape[0]
    forces = pl.pallas_call(
        functools.partial(force_kernel, kinds, axes, grid),
        out_shape=jax.ShapeDtypeStruct((3, own, lanes), f32),
        in_specs=[smem, smem, smem] + [vmem] * 13,
        out_specs=vmem,
        scratch_shapes=[
            pltpu.VMEM((blocks * 80, lanes), f32),
            pltpu.VMEM((own + 1, 32, lanes), bf16),
            pltpu.VMEM((blocks, 32, lanes), bf16),
            pltpu.VMEM((blocks, 32, 2 * lanes), bf16),
            pltpu.VMEM(((own + 1) * 16, lanes), f32),
            pltpu.VMEM((blocks - own, lanes), f32),
            pltpu.SMEM((blocks - own, lanes), f32),
            pltpu.SMEM((2 * entries + inbound.shape[0] + unroll + 8,), jnp.int32),
            pltpu.SemaphoreType.DMA,
        ],
        compiler_params=pltpu.CompilerParams(vmem_limit_bytes=40 * 2**20),
        name="force",
    )(tables, near_pairs, pair_count, *here, *beside, mom_xy, mom_z, jnp.asarray(cell_of))
    return forces.reshape(3, bx, by, bz, slots)


def solution(mesh):
    in_specs = (
        P(None, "gx", "gy", "gz", None),
        P(None, "gx", "gy", "gz", None),
        P(None, "gx", "gy", "gz", None),
        P("gx", "gy", "gz"),
        P(("gx", "gy", "gz")),
        P(("gx", "gy", "gz")),
    )
    out_specs = P(None, "gx", "gy", "gz", None)
    return jax.shard_map(body, mesh=mesh, in_specs=in_specs, out_specs=out_specs, check_vma=False)
```

```python
import functools
import math

import jax
import jax.numpy as jnp
import numpy as np
from jax import lax
from jax.experimental import pallas as pl
from jax.experimental.pallas import tpu as pltpu
from jax.sharding import PartitionSpec as P

stencil_table = (
    (0, 0, 0),
    (1, 0, 0),
    (0, 1, 0),
    (0, 0, 1),
    (1, 1, 0),
    (-1, 1, 0),
    (1, 0, 1),
    (1, 0, -1),
    (0, 1, 1),
    (0, -1, 1),
    (1, 1, -1),
    (1, -1, 1),
    (-1, 1, 1),
    (1, 1, 1),
)
code_total = len(stencil_table)
kernel_scale = 1.0 / (8.0 * math.pi)
core_square = 0.09
lanes = 128
list_room = 640
parts_sent = 10
unroll = 32
f32 = jnp.float32
bf16 = jnp.bfloat16


group_set = (0, 1, 1, 2, 2, 1, 1, 1, 2, 2)


def set_groups(which):
    return [g for g in range(10) if group_set[g] == which]


def group_heights(bx, by, bz):
    return [bx * by * bz, by * bz, by * bz, (bx + 2) * bz, (bx + 2) * bz] * 2


def block_layout(bx, by, bz, odd_x, odd_y):
    x_at = (0, bx + 1) if odd_x else (bx + 1, 0)
    y_at = (0, by + 1) if odd_y else (by + 1, 0)
    x_row = [x_at[0], *range(1, bx + 1), x_at[1]]
    coords = []
    for z_of in ([z + 1 for z in range(bz)], [bz + 1 if z == 0 else 0 for z in range(bz)]):
        coords.append([(x + 1, y + 1, z) for x in range(bx) for y in range(by) for z in z_of])
        for x in x_at:
            coords.append([(x, y + 1, z) for y in range(by) for z in z_of])
        for y in y_at:
            coords.append([(x, y, z) for x in x_row for z in z_of])
    return coords


def work_tables(bx, by, bz, odd_x, odd_y):
    groups = block_layout(bx, by, bz, odd_x, odd_y)
    place = {}
    count = [0, 0, 0]
    for g, group in enumerate(groups):
        for c in group:
            place[c] = (group_set[g], count[group_set[g]])
            count[group_set[g]] += 1
    own = count[0]
    forward, backward, inbound = [], [], ([], [])
    for a, at in enumerate(groups[0]):
        for code, o in enumerate(stencil_table):
            which, b = place[tuple(at[d] + o[d] for d in range(3))]
            forward.append(a | b << 8 | which << 16)
            backward.append(b | a << 8 if which == 0 and code else own)
    for at, (which, h) in place.items():
        for code, o in enumerate(stencil_table):
            to, b = place.get(tuple(at[d] + o[d] for d in range(3)), (3, 0))
            if which and to == 0:
                inbound[which - 1].append((b | h << 8) << 16 | h * 16 + code)
    for column in inbound:
        while len(column) % 8:
            column.append(own << 16 | 15)
    spans = [len(column) for column in (forward, backward, *inbound)]
    flat = [*forward, *backward, *inbound[0], *inbound[1]]
    flat += [0] * (-len(flat) % 1024)
    return np.array(flat, np.int32), spans


def position(group, rows, bx, by, bz, odd):
    row = lax.broadcasted_iota(jnp.int32, (rows, lanes), 0)
    z = row % bz
    line = row // bz
    kind = group % 5
    first_x = jnp.where(odd[0] == 1, 0, bx + 1)
    first_y = jnp.where(odd[1] == 1, 0, by + 1)
    if kind == 0:
        x, y = line // by + 1, line % by + 1
    elif kind <= 2:
        x = jnp.zeros_like(row) + (first_x if kind == 1 else bx + 1 - first_x)
        y = line + 1
    else:
        x = jnp.where(line == 0, first_x, jnp.where(line == bx + 1, bx + 1 - first_x, line))
        y = jnp.zeros_like(row) + (first_y if kind == 3 else by + 1 - first_y)
    if group < 5:
        z = z + 1
    else:
        z = jnp.where(z == 0, bz + 1, 0)
    sides = (bx + 1, by + 1, bz + 1)
    return [v.astype(f32) - 0.5 * side for v, side in zip((x, y, z), sides)]


def moment_rows(b, l):
    zz = b[2] * l[2]
    return [
        b[0] * l[1],
        b[0] * l[2],
        b[1] * l[0],
        b[1] * l[2],
        b[2] * l[0],
        b[2] * l[1],
        b[0] * l[0] - zz,
        b[1] * l[1] - zz,
    ]


def cross_rows(q, b, l):
    c = [q[1] * b[2] - q[2] * b[1], q[2] * b[0] - q[0] * b[2], q[0] * b[1] - q[1] * b[0]]
    return [
        2.0 * c[0] * l[0],
        2.0 * c[1] * l[1],
        2.0 * c[2] * l[2],
        c[0] * l[1] + c[1] * l[0],
        c[0] * l[2] + c[2] * l[0],
        c[1] * l[2] + c[2] * l[1],
    ]


def turn_rows(r, m):
    return [
        2.0 * (r[1] * m[4] - r[2] * m[2]),
        2.0 * (r[2] * m[0] - r[0] * m[5]),
        2.0 * (r[0] * m[3] - r[1] * m[1]),
        r[1] * m[5] - r[0] * m[4] + r[2] * (m[6] - m[7]),
        r[0] * m[2] - r[2] * m[3] - r[1] * m[6],
        r[2] * m[1] + r[0] * m[7] - r[1] * m[0],
    ]


def pieces(value):
    first = value.astype(bf16).astype(f32)
    rest = value - first
    second = rest.astype(bf16).astype(f32)
    return first, second, rest - second


def distance_rows(q):
    near = q[0] * q[0] + q[1] * q[1] + q[2] * q[2]
    one = jnp.ones_like(near)
    left, right = [], []
    for axis in q:
        p1, p2, p3 = pieces(axis)
        left += [p1, p1, p2, p2, p1, p3]
        right += [-2.0 * v for v in (p1, p2, p1, p2, p3, p1)]
    left += [*pieces(near), one, one, one]
    right += [one, one, one, *pieces(near + core_square)]
    return left, right


def parities(axes):
    return [lax.rem(lax.axis_index(axis), 2) for axis in axes[:2]]


def pack_kernel(sizes, axes, count, fill_h, offsets_h, burgers_h, line_h, pairs_h, own, face_1, mom, fill, offsets, burgers, line, pairs, level, sems):
    bx, by, bz, cells = sizes
    total, face = bx * by * bz, by * bz
    moves = ((fill_h, fill), (pairs_h, pairs), (burgers_h, burgers), (line_h, line), (offsets_h, offsets))
    copies = [pltpu.make_async_copy(u, v, sems.at[k]) for k, (u, v) in enumerate(moves)]
    for copy in copies:
        copy.start()
    for copy in copies:
        copy.wait()
    for x in range(bx):
        for y in range(by):
            column = jnp.broadcast_to(fill[x][:, y : y + 1], (bz, lanes))
            level[x * face + y * bz : x * face + (y + 1) * bz, :] = column
    live = lax.broadcasted_iota(jnp.int32, (total, lanes), 1) < level[...]
    b, l = [], []
    for d in range(3):
        own[d] = offsets[d]
        b.append(jnp.where(live, burgers[d], 0.0))
        l.append(jnp.where(live, line[d], 0.0))
        own[3 + d] = b[d]
        own[6 + d] = l[d]
    entries = pairs.shape[1]
    code = pairs[...]
    block_no = code // code_total
    code_no = code - block_no * code_total
    alive = lax.broadcasted_iota(jnp.int32, (1, entries), 1) < count[0]
    of_block = lax.broadcasted_iota(jnp.int32, (total, entries), 0) == block_no
    of_code = lax.broadcasted_iota(jnp.int32, (lanes, entries), 0) == code_no
    own[9] = lax.dot_general(
        jnp.where(of_block & alive, 1.0, 0.0).astype(bf16),
        jnp.where(of_code, 1.0, 0.0).astype(bf16),
        (((1,), (1,)), ((), ())),
        preferred_element_type=f32,
    )
    cx, cy, cz = bx // 2, by // 2, bz // 2
    here = lax.axis_index(axes[0])
    for axis in axes[1:]:
        here = here * lax.axis_size(axis) + lax.axis_index(axis)
    first_lane = here * (cx * cy * cz)
    wide = lax.broadcasted_iota(jnp.int32, (face, lanes), 1)
    deep = lax.broadcasted_iota(jnp.int32, (face, lanes), 0)
    local = deep // (2 * bz) * cz + deep % bz // 2
    sums = []
    for feature in moment_rows(b, l):
        column = []
        for x in range(cx):
            both = feature[2 * x * face : (2 * x + 1) * face] + feature[(2 * x + 1) * face : (2 * x + 2) * face]
            column.append(jnp.sum(both, 1, keepdims=True))
        sums.append(column)
    for chunk in range(cells // lanes):
        for f, column in enumerate(sums):
            placed = jnp.zeros((face, lanes), f32)
            for x in range(cx):
                lane_of = first_lane + x * cy * cz + local - chunk * lanes
                placed = placed + jnp.where(wide == lane_of, column[x], 0.0)
            mom[chunk * 8 + f : chunk * 8 + f + 1, :] = jnp.sum(placed, 0, keepdims=True)
    x_face(sizes, axes, 0, own, face_1)
    face_1[parts_sent * face :] = mom[...]


def x_face(sizes, axes, turn, own, out):
    bx, by, bz, _ = sizes
    total, face = bx * by * bz, by * bz
    low = parities(axes)[0] != turn
    for d in range(parts_sent):
        out[d * face : (d + 1) * face] = jnp.where(low, own[d, 0:face], own[d, total - face : total])


def y_face(sizes, axes, turn, own, x_1, out):
    bx, by, bz, _ = sizes
    low = parities(axes)[1] != turn
    last = (by - 1) * bz
    for d in range(parts_sent):
        start = d * by * bz
        out[d, 0:bz] = jnp.where(low, x_1[start : start + bz], x_1[start + last : start + last + bz])
        for x in range(bx):
            start = x * by * bz
            lo, hi = own[d, start : start + bz], own[d, start + last : start + last + bz]
            out[d, (x + 1) * bz : (x + 2) * bz] = jnp.where(low, lo, hi)


def shape_blocks(sizes, odd, sources, stage, right, weighed, left=None):
    bx, by, bz, _ = sizes
    heights = group_heights(bx, by, bz)
    base = 0
    for group, part in sources:
        h = heights[group]
        zero = jnp.zeros((h, lanes), f32)
        place = position(group, h, bx, by, bz, odd)
        q = [part(d) + place[d] for d in range(3)]
        b = [part(3 + d) for d in range(3)]
        l = [part(6 + d) for d in range(3)]
        rows = moment_rows(b, l) + cross_rows(q, b, l)
        lhs, rhs = distance_rows(q)
        rows = rows + [zero] * (16 - len(rows)) + rhs + [zero] * (32 - len(rhs))
        if left is not None:
            rows = rows + lhs + [zero] * (32 - len(lhs))
        for f, value in enumerate(rows):
            stage[pl.ds(base * 80 + f, h, stride=80), :] = value
        base += h

    def shape_block(block, carry):
        at = pl.multiple_of(block * 80, 16)
        product = stage[pl.ds(at, 16), :]
        high = product.astype(bf16)
        low = (product - high.astype(f32)).astype(bf16)
        weighed[block, 0:16, 0:lanes] = high
        weighed[block, 0:16, lanes : 2 * lanes] = high
        weighed[block, 16:32, 0:lanes] = low
        weighed[block, 16:32, lanes : 2 * lanes] = jnp.zeros_like(low)
        right[block] = stage[pl.ds(at + 16, 32), :].astype(bf16)
        if left is not None:
            left[block] = stage[pl.ds(at + 48, 32), :].astype(bf16)
        return carry

    lax.fori_loop(0, base, shape_block, 0, unroll=8)


def rows_of(ref, start, height):
    return lambda d: ref[start + d * height : start + (d + 1) * height, :]


def own_kernel(sizes, axes, variant, tables, pairs, count, own, right, weighed, left, todo, face_2, stage, table, sem):
    bx, by, bz, _ = sizes
    total = bx * by * bz
    codes = total * code_total
    odd = parities(axes)
    copy = fetch_table(tables, odd, variant, table, sem)
    x_face(sizes, axes, 1, own, face_2)
    shape_blocks(sizes, odd, [(0, lambda d: own[d])], stage, right, weighed, left)
    left[total] = left[0]
    live_count = count[0]
    copy.wait()

    def list_own(step, n):
        ats = [step * 8 + k for k in range(8)]
        codes_here = [pairs[at] for at in ats]
        entries = [table[code] for code in codes_here]
        backs = [table[codes + code] for code in codes_here]
        for at, entry, back in zip(ats, entries, backs):
            alive = (at < live_count).astype(jnp.int32)
            todo[n] = entry
            n = n + jnp.where(entry < 65536, alive, 0)
            todo[n] = back
            n = n + jnp.where(back != total, alive, 0)
        return n

    n = lax.fori_loop(0, (live_count + 7) // 8, list_own, 0)
    todo[list_room] = n
    for k in range(unroll):
        todo[n + k] = total


def fetch_table(tables, odd, variant, table, sem):
    start = pl.multiple_of((odd[0] * 2 + odd[1]) * variant, 1024)
    copy = pltpu.make_async_copy(tables.at[pl.ds(start, variant)], table, sem)
    copy.start()
    return copy


def interact(lookup, first, last, right, weighed, left, acc):
    def step(at, carry):
        results = []
        for k in range(unroll):
            entry = lookup(at * unroll + k)
            row, col = entry & 255, entry >> 8
            square = lax.dot_general(
                right[col], left[row], (((0,), (0,)), ((), ())), preferred_element_type=f32
            )
            root = lax.rsqrt(square)
            weight = root * root * root
            high = weight.astype(bf16)
            low = (weight - high.astype(f32)).astype(bf16)
            both = jnp.dot(
                weighed[col], jnp.concatenate([high, low], 0), preferred_element_type=f32
            )
            results.append((row, both[0:16] + both[16:32]))
        for row, value in results:
            at_row = pl.ds(pl.multiple_of(row * 16, 16), 16)
            acc[at_row, :] += value
        return carry

    lax.fori_loop(first, last, step, 0)


def near_first_kernel(sizes, axes, todo, right, weighed, left, own, x_1, _, acc, face_1, face_2):
    y_face(sizes, axes, 0, own, x_1, face_1)
    y_face(sizes, axes, 1, own, x_1, face_2)
    acc[...] = jnp.zeros_like(acc)
    steps = (todo[list_room] + unroll - 1) // unroll
    interact(lambda at: todo[at], 0, (steps + 1) // 2, right, weighed, left, acc)


def near_second_kernel(todo, right, weighed, left, face_in, x_1, x_2, _, acc, face, x_both):
    face[...] = face_in[...]
    x_both[0 : x_1.shape[0]] = x_1[...]
    x_both[x_1.shape[0] :] = x_2[...]
    acc[...] = jnp.zeros_like(acc)
    steps = (todo[list_room] + unroll - 1) // unroll
    interact(lambda at: todo[at], (steps + 1) // 2, steps, right, weighed, left, acc)


def list_inbound(table, base, size, flags, found, n, total):
    def step(at, n):
        entries = [table[base + at * 8 + k] for k in range(8)]
        ons = [flags[(entry & 65535) >> 4, entry & 15] for entry in entries]
        for entry, on in zip(entries, ons):
            found[n] = entry >> 16
            n = n + (on > 0.5).astype(jnp.int32)
        return n

    n = lax.fori_loop(0, size // 8, step, n)
    for k in range(unroll):
        found[n + k] = total
    return n


def gather_flags(sources, heights, flags_v, flags_s, sem):
    base = 0
    for group, part in sources:
        flags_v[base : base + heights[group], :] = part(9)
        base += heights[group]
    copy = pltpu.make_async_copy(flags_v, flags_s, sem)
    copy.start()
    return copy


def side_sources(sizes, groups, mine, both):
    bx, by, bz, cells = sizes
    heights = group_heights(bx, by, bz)
    mom_rows = 8 * cells // lanes
    sources = []
    for g in groups:
        if g % 5 == 0:
            sources.append((g, lambda d: mine[d]))
        else:
            h = heights[g]
            start = (parts_sent * h + mom_rows) if g % 5 in (2, 4) else 0
            sources.append((g, rows_of(both[g >= 5], start, h)))
    return sources


def beside_kernel(sizes, axes, spans, tables, pairs, count, x_both, p_mine, p_x_both, mom_in, right, weighed, found, mom_out, stage, table, flags_v, flags_s, sems):
    bx, by, bz, _ = sizes
    odd = parities(axes)
    sources = side_sources(sizes, set_groups(1), p_mine, (x_both, p_x_both))
    variant, start, size = spans
    table_copy = fetch_table(tables, odd, variant, table, sems.at[0])
    copy = gather_flags(sources, group_heights(bx, by, bz), flags_v, flags_s, sems.at[1])
    mom_out[...] = mom_in[...]
    shape_blocks(sizes, odd, sources, stage, right, weighed)
    table_copy.wait()
    copy.wait()
    total = bx * by * bz
    live_count = count[0]

    def list_sides(step, n):
        n1, n2 = n
        ats = [step * 8 + k for k in range(8)]
        entries = [table[pairs[at]] for at in ats]
        for at, entry in zip(ats, entries):
            alive = (at < live_count).astype(jnp.int32)
            which = entry >> 16
            entry = entry & 65535
            found[n1] = entry
            found[list_room + n2] = entry
            n1, n2 = n1 + (alive & which), n2 + (alive & (which >> 1))
        return n1, n2

    n1, n2 = lax.fori_loop(0, (live_count + 7) // 8, list_sides, (0, 0))
    found[2 * list_room] = list_inbound(table, start, size, flags_s, found, n1, total)
    found[2 * list_room + 1] = n2


def side_kernel(found, right, weighed, left, acc):
    acc[...] = jnp.zeros_like(acc)
    n = found[2 * list_room]
    interact(lambda at: found[at], 0, (n + unroll - 1) // unroll, right, weighed, left, acc)


def coarse_place(sizes, axes, chunk):
    bx, by, bz, _ = sizes
    coarse = (bx // 2, by // 2, bz // 2)
    number = lax.broadcasted_iota(jnp.int32, (1, lanes), 1) + chunk * lanes
    places = []
    for d in (2, 1, 0):
        places.append(number % coarse[d])
        number = number // coarse[d]
    for k, d in enumerate((2, 1, 0)):
        size = lax.axis_size(axes[d])
        places[k] = places[k] + number % size * coarse[d]
        number = number // size
    return places[::-1]


def close_kernel(sizes, axes, grid, spans, tables, todo, y_both, p_y_both, left, acc_a, acc_b, acc_c, own, mom, out, stage, right, weighed, acc, table, found, flags_v, flags_s, sems):
    bx, by, bz, cells = sizes
    total, face = bx * by * bz, by * bz
    odd = parities(axes)
    sources = side_sources(sizes, set_groups(2), None, (y_both, p_y_both))
    variant, start, size = spans
    table_copy = fetch_table(tables, odd, variant, table, sems.at[0])
    copy = gather_flags(sources, group_heights(bx, by, bz), flags_v, flags_s, sems.at[1])
    shape_blocks(sizes, odd, sources, stage, right, weighed)
    acc[...] = acc_a[...] + acc_b[...] + acc_c[...]
    table_copy.wait()
    copy.wait()
    more = list_inbound(table, start, size, flags_s, found, 0, total)
    n = todo[2 * list_room + 1]
    lookup = lambda at: jnp.where(at < n, todo[list_room + at], found[jnp.maximum(at - n, 0)])
    interact(lookup, 0, (n + more + unroll - 1) // unroll, right, weighed, left, acc)

    cx, cy, cz = bx // 2, by // 2, bz // 2
    deep = lax.broadcasted_iota(jnp.int32, (face, lanes), 0)
    local = (None, deep // (2 * bz), deep % bz // 2)
    far = [[] for _ in range(6)]
    for x in range(cx):
        totals = [jnp.zeros((face, lanes), f32)] * 6
        for chunk in range(cells // lanes):
            lengths = []
            cell_of = coarse_place(sizes, axes, chunk)
            for d, axis in enumerate(axes):
                at = lax.axis_index(axis) * (cx, cy, cz)[d] + (x if d == 0 else local[d])
                delta = at - cell_of[d]
                half = grid[d] // 2
                delta = jnp.where(delta >= grid[d] - half, delta - grid[d], delta)
                delta = jnp.where(delta < -half, delta + grid[d], delta)
                lengths.append(2.0 * delta.astype(f32))
            radius = lengths[0] * lengths[0] + lengths[1] * lengths[1] + lengths[2] * lengths[2]
            root = lax.rsqrt(radius + core_square)
            weight = jnp.where(radius == 0.0, 0.0, root * root * root)
            m = [mom[chunk * 8 + f : chunk * 8 + f + 1, :] for f in range(8)]
            turned = turn_rows([weight * v for v in lengths], m)
            totals = [t + v for t, v in zip(totals, turned)]
        for f in range(6):
            far[f].append(jnp.sum(totals[f], 1, keepdims=True))

    place = position(0, total, bx, by, bz, odd)
    p = [own[d] + place[d] for d in range(3)]
    b = [own[3 + d] for d in range(3)]
    l = [own[6 + d] for d in range(3)]
    moment = [acc[pl.ds(f, total, stride=16), :] for f in range(8)]
    crossed = [acc[pl.ds(8 + f, total, stride=16), :] for f in range(6)]
    turned = turn_rows(p, moment)
    s = []
    for f in range(6):
        column = jnp.concatenate([far[f][x // 2] for x in range(bx)], 0)
        s.append(turned[f] - crossed[f] + column)
    push = [
        s[0] * b[0] + s[3] * b[1] + s[4] * b[2],
        s[3] * b[0] + s[1] * b[1] + s[5] * b[2],
        s[4] * b[0] + s[5] * b[1] + s[2] * b[2],
    ]
    out[0] = kernel_scale * (push[1] * l[2] - push[2] * l[1])
    out[1] = kernel_scale * (push[2] * l[0] - push[0] * l[2])
    out[2] = kernel_scale * (push[0] * l[1] - push[1] * l[0])


def shifted(value, axis, step):
    size = lax.axis_size(axis)
    return lax.ppermute(value, axis, [(i, (i + step) % size) for i in range(size)])


def exchanged(value, axis, turn):
    size = lax.axis_size(axis)
    return lax.ppermute(
        value, axis, [(i, (i + (1 if (i + turn) % 2 == 0 else -1)) % size) for i in range(size)]
    )


def ring_sum(value, axis):
    total = value
    for step in range(1, lax.axis_size(axis)):
        total = total + shifted(value, axis, step)
    return total


def beside_z(value, layers):
    size = lax.axis_size("gz")
    if size == 2:
        return shifted(value, "gz", 1)
    head = value.shape
    split = value.reshape(-1, layers, lanes)
    above = shifted(split[:, :1], "gz", -1)
    below = shifted(split[:, layers - 1 :], "gz", 1)
    middle = split[:, 1 : layers - 1]
    return jnp.concatenate([above, middle, below], 1).reshape(head)


def body(offsets, burgers, line, block_fill, near_pairs, pair_count):
    _, bx, by, bz, slots = offsets.shape
    axes = ("gx", "gy", "gz")
    sizes = [lax.axis_size(axis) for axis in axes]
    heights = group_heights(bx, by, bz)
    own, face, rim = heights[0], heights[1], heights[3]
    set_size = [sum(heights[g] for g in set_groups(which)) for which in range(3)]
    coarse = (bx // 2, by // 2, bz // 2)
    grid = tuple(c * n for c, n in zip(coarse, sizes))
    per_device = coarse[0] * coarse[1] * coarse[2]
    cells = per_device * sizes[0] * sizes[1] * sizes[2]
    mom_rows = 8 * cells // lanes
    kinds = (bx, by, bz, cells)
    riding = sizes[0] == 4 and sizes[1] == 4
    entries = near_pairs.shape[0]
    vmem = pl.BlockSpec(memory_space=pltpu.VMEM)
    smem = pl.BlockSpec(memory_space=pltpu.SMEM)
    hbm = pl.BlockSpec(memory_space=pltpu.HBM)
    anywhere = pl.BlockSpec(memory_space=pl.ANY)
    shape = jax.ShapeDtypeStruct
    flat = lambda v: v.reshape(3, own, slots)
    far = lambda v: pltpu.with_memory_space_constraint(v, pltpu.HBM)

    variants = [work_tables(bx, by, bz, ox, oy) for ox in (0, 1) for oy in (0, 1)]
    span = variants[0][1]
    variant = len(variants[0][0])
    tables = far(jnp.asarray(np.concatenate([v[0] for v in variants])))
    span_1 = (variant, span[0] + span[1], span[2])
    span_2 = (variant, span[0] + span[1] + span[2], span[3])
    assert 2 * entries + unroll + 8 <= list_room

    def call(kernel, out_shape, in_specs, out_specs, scratch, name, cost, limit=12):
        return pl.pallas_call(
            kernel,
            out_shape=out_shape,
            in_specs=in_specs,
            out_specs=out_specs,
            scratch_shapes=scratch,
            compiler_params=pltpu.CompilerParams(vmem_limit_bytes=limit * 2**20),
            cost_estimate=pl.CostEstimate(flops=cost, bytes_accessed=cost, transcendentals=0),
            name=name,
        )

    mine, face_1, mom = call(
        functools.partial(pack_kernel, kinds, axes),
        [
            shape((parts_sent, own, lanes), f32),
            shape((parts_sent * face + mom_rows, lanes), f32),
            shape((mom_rows, lanes), f32),
        ],
        [smem, hbm, hbm, hbm, hbm, hbm],
        [vmem] * 3,
        [
            pltpu.VMEM((bx, bz, by), jnp.int32),
            pltpu.VMEM((3, own, lanes), f32),
            pltpu.VMEM((3, own, lanes), f32),
            pltpu.VMEM((3, own, lanes), f32),
            pltpu.VMEM((1, entries), jnp.int32),
            pltpu.VMEM((own, lanes), jnp.int32),
            pltpu.SemaphoreType.DMA((5,)),
        ],
        "pack",
        10**6,
    )(
        pair_count,
        far(jnp.transpose(block_fill, (0, 2, 1))),
        far(flat(offsets)),
        far(flat(burgers)),
        far(flat(line)),
        far(near_pairs.reshape(1, -1)),
    )

    x_1 = exchanged(face_1, "gx", 0)
    p_mine = beside_z(mine, bz)
    right, weighed, left, todo, face_2 = call(
        functools.partial(own_kernel, kinds, axes, variant),
        [
            shape((own, 32, lanes), bf16),
            shape((own, 32, 2 * lanes), bf16),
            shape((own + 1, 32, lanes), bf16),
            pltpu.SMEM((1024,), jnp.int32),
            shape((parts_sent * face, lanes), f32),
        ],
        [anywhere, smem, smem, vmem],
        [vmem, vmem, vmem, smem, vmem],
        [
            pltpu.VMEM((own * 80, lanes), f32),
            pltpu.SMEM((variant,), jnp.int32),
            pltpu.SemaphoreType.DMA,
        ],
        "own",
        10**7,
    )(tables, near_pairs, pair_count, mine)
    head = parts_sent * face
    mom_x = mom + x_1[head:]
    send = jnp.concatenate([face_2, mom_x], 0)
    x_2 = exchanged(send, "gx", 1)

    near_acc = shape(((own + 1) * 16, lanes), f32)
    near_face = shape((parts_sent, (bx + 1) * bz, lanes), f32)
    acc_a, y_own_1, y_own_2 = call(
        functools.partial(near_first_kernel, kinds, axes),
        [near_acc, near_face, near_face],
        [smem, vmem, vmem, vmem, vmem, vmem, anywhere],
        [vmem, vmem, vmem],
        [],
        "near_first",
        10**7,
    )(todo, right, weighed, left, mine, x_1, send)
    mom_x = mom_x + x_2[head:] if riding else ring_sum(mom, "gx")
    odd_y = lax.rem(lax.axis_index("gy"), 2) == 1

    def y_send(y_own, low, riding_rows):
        split = x_2[:head].reshape(parts_sent, by, bz, lanes)
        last = jnp.where(low, split[:, 0], split[:, by - 1])
        side = jnp.concatenate([y_own, last], 1)
        return jnp.concatenate([side.reshape(parts_sent * rim, lanes), riding_rows], 0)

    send = y_send(y_own_1, odd_y, mom_x)
    y_1 = exchanged(send, "gy", 0)
    acc_b, y_own_2, x_both = call(
        near_second_kernel,
        [near_acc, near_face, shape((2 * x_1.shape[0], lanes), f32)],
        [smem, vmem, vmem, vmem, vmem, vmem, vmem, anywhere],
        [vmem, vmem, vmem],
        [],
        "near_second",
        10**7,
    )(todo, right, weighed, left, y_own_2, x_1, x_2, send)
    p_x_both = beside_z(x_both, bz)
    tail = parts_sent * rim
    mom_y = mom_x + y_1[tail:]
    y_2 = exchanged(y_send(y_own_2, ~odd_y, mom_y), "gy", 1)
    right_1, weighed_1, found, mom_y = call(
        functools.partial(beside_kernel, kinds, axes, span_1),
        [
            shape((set_size[1], 32, lanes), bf16),
            shape((set_size[1], 32, 2 * lanes), bf16),
            pltpu.SMEM((2048,), jnp.int32),
            shape((mom_rows, lanes), f32),
        ],
        [anywhere, smem, smem, vmem, vmem, vmem, vmem],
        [vmem, vmem, smem, vmem],
        [
            pltpu.VMEM((set_size[1] * 80, lanes), f32),
            pltpu.SMEM((variant,), jnp.int32),
            pltpu.VMEM((set_size[1], lanes), f32),
            pltpu.SMEM((set_size[1], lanes), f32),
            pltpu.SemaphoreType.DMA((2,)),
        ],
        "beside",
        10**7,
    )(tables, near_pairs, pair_count, x_both, p_mine, p_x_both, mom_y)
    mom_y = mom_y + y_2[tail:] if riding else ring_sum(mom_x, "gy")
    y_both = jnp.concatenate([y_1, y_2, mom_y], 0)
    p_y_both = beside_z(y_both, bz)
    acc_c = call(
        side_kernel,
        shape(((own + 1) * 16, lanes), f32),
        [smem, vmem, vmem, vmem],
        vmem,
        [],
        "side",
        10**7,
    )(found, right_1, weighed_1, left)
    if sizes[2] == 2:
        mom = mom_y + p_y_both[-mom_rows:]
    else:
        mom = ring_sum(mom_y, "gz")
    forces = call(
        functools.partial(close_kernel, kinds, axes, grid, span_2),
        shape((3, own, lanes), f32),
        [anywhere, smem] + [vmem] * 8,
        vmem,
        [
            pltpu.VMEM((set_size[2] * 80, lanes), f32),
            pltpu.VMEM((set_size[2], 32, lanes), bf16),
            pltpu.VMEM((set_size[2], 32, 2 * lanes), bf16),
            pltpu.VMEM(((own + 1) * 16, lanes), f32),
            pltpu.SMEM((variant,), jnp.int32),
            pltpu.SMEM((1024,), jnp.int32),
            pltpu.VMEM((set_size[2], lanes), f32),
            pltpu.SMEM((set_size[2], lanes), f32),
            pltpu.SemaphoreType.DMA((2,)),
        ],
        "close",
        10**7,
    )(tables, found, y_both, p_y_both, left, acc_a, acc_b, acc_c, mine, mom)
    return forces.reshape(3, bx, by, bz, slots)


def solution(mesh):
    in_specs = (
        P(None, "gx", "gy", "gz", None),
        P(None, "gx", "gy", "gz", None),
        P(None, "gx", "gy", "gz", None),
        P("gx", "gy", "gz"),
        P(("gx", "gy", "gz")),
        P(("gx", "gy", "gz")),
    )
    out_specs = P(None, "gx", "gy", "gz", None)
    return jax.shard_map(body, mesh=mesh, in_specs=in_specs, out_specs=out_specs, check_vma=False)
```

```python
import functools
import math

import jax
import jax.numpy as jnp
import numpy as np
from jax import lax
from jax.experimental import pallas as pl
from jax.experimental.pallas import tpu as pltpu
from jax.sharding import PartitionSpec as P

stencil_table = (
    (0, 0, 0),
    (1, 0, 0),
    (0, 1, 0),
    (0, 0, 1),
    (1, 1, 0),
    (-1, 1, 0),
    (1, 0, 1),
    (1, 0, -1),
    (0, 1, 1),
    (0, -1, 1),
    (1, 1, -1),
    (1, -1, 1),
    (-1, 1, 1),
    (1, 1, 1),
)
code_total = len(stencil_table)
kernel_scale = 1.0 / (8.0 * math.pi)
core_square = 0.09
lanes = 128
mark = 2048.0
parts_sent = 10
unroll = 48
tail_unroll = 16
f32 = jnp.float32
bf16 = jnp.bfloat16


group_set = (0, 1, 1, 2, 2, 1, 1, 1, 2, 2)


def set_groups(which):
    return [g for g in range(10) if group_set[g] == which]


def group_heights(bx, by, bz):
    return [bx * by * bz, by * bz, by * bz, (bx + 2) * bz, (bx + 2) * bz] * 2


def block_layout(bx, by, bz):
    coords = []
    for z_of in ([z + 1 for z in range(bz)], [bz + 1 if z == 0 else 0 for z in range(bz)]):
        coords.append([(x + 1, y + 1, z) for x in range(bx) for y in range(by) for z in z_of])
        for x in (0, bx + 1):
            coords.append([(x, y + 1, z) for y in range(by) for z in z_of])
        for y in (0, by + 1):
            coords.append([(x, y, z) for x in range(bx + 2) for z in z_of])
    return coords


def work_tables(bx, by, bz):
    groups = block_layout(bx, by, bz)
    place = {}
    count = [0, 0, 0]
    for g, group in enumerate(groups):
        for c in group:
            place[c] = (group_set[g], count[group_set[g]])
            count[group_set[g]] += 1
    codes = np.zeros((8, count[0] * code_total), np.float32)
    for a, at in enumerate(groups[0]):
        for code, o in enumerate(stencil_table):
            which, b = place[tuple(at[d] + o[d] for d in range(3))]
            k = a * code_total + code
            codes[:2, k] = a, b
            codes[(2, 4, 5)[which], k] = 1.0
            codes[3, k] = which == 0 and code > 0
    inbound = []
    for which in (1, 2):
        found = []
        for at, (at_set, h) in place.items():
            for code, o in enumerate(stencil_table):
                to, b = place.get(tuple(at[d] + o[d] for d in range(3)), (3, 0))
                if at_set == which and to == 0:
                    found.append((b, h, code))
        size = -(-len(found) // 16) * 16
        rows = np.zeros((size, count[which]), np.float32)
        marks = np.zeros((size, lanes), np.float32)
        ends = np.zeros((8, size), np.float32)
        for k, (b, h, code) in enumerate(found):
            rows[k, h] = marks[k, code] = 1.0
            ends[:2, k] = b, h
        inbound += [rows, marks, ends]
    return [codes, *inbound]


def position(group, rows, bx, by, bz):
    row = lax.broadcasted_iota(jnp.int32, (rows, lanes), 0)
    z = row % bz
    line = row // bz
    kind = group % 5
    if kind == 0:
        x, y = line // by + 1, line % by + 1
    elif kind <= 2:
        x, y = jnp.full_like(row, 0 if kind == 1 else bx + 1), line + 1
    else:
        x, y = line, jnp.full_like(row, 0 if kind == 3 else by + 1)
    if group < 5:
        z = z + 1
    else:
        z = jnp.where(z == 0, bz + 1, 0)
    sides = (bx + 1, by + 1, bz + 1)
    return [v.astype(f32) - 0.5 * side for v, side in zip((x, y, z), sides)]


def moment_rows(b, l):
    zz = b[2] * l[2]
    return [
        b[0] * l[1],
        b[0] * l[2],
        b[1] * l[0],
        b[1] * l[2],
        b[2] * l[0],
        b[2] * l[1],
        b[0] * l[0] - zz,
        b[1] * l[1] - zz,
    ]


def cross_rows(q, b, l):
    c = [q[1] * b[2] - q[2] * b[1], q[2] * b[0] - q[0] * b[2], q[0] * b[1] - q[1] * b[0]]
    return [
        2.0 * c[0] * l[0],
        2.0 * c[1] * l[1],
        2.0 * c[2] * l[2],
        c[0] * l[1] + c[1] * l[0],
        c[0] * l[2] + c[2] * l[0],
        c[1] * l[2] + c[2] * l[1],
    ]


def turn_rows(r, m):
    return [
        2.0 * (r[1] * m[4] - r[2] * m[2]),
        2.0 * (r[2] * m[0] - r[0] * m[5]),
        2.0 * (r[0] * m[3] - r[1] * m[1]),
        r[1] * m[5] - r[0] * m[4] + r[2] * (m[6] - m[7]),
        r[0] * m[2] - r[2] * m[3] - r[1] * m[6],
        r[2] * m[1] + r[0] * m[7] - r[1] * m[0],
    ]


def pieces(value):
    first = value.astype(bf16).astype(f32)
    rest = value - first
    second = rest.astype(bf16).astype(f32)
    return first, second, rest - second


def distance_rows(q):
    near = q[0] * q[0] + q[1] * q[1] + q[2] * q[2]
    one = jnp.ones_like(near)
    left, right = [], []
    for axis in q:
        p1, p2, p3 = pieces(axis)
        left += [p1, p1, p2, p2, p1, p3]
        right += [-2.0 * v for v in (p1, p2, p1, p2, p3, p1)]
    left += [*pieces(near), one, one, one]
    right += [one, one, one, *pieces(near + core_square)]
    return left, right


def pack_kernel(sizes, axes, count, fill_h, offsets_h, burgers_h, line_h, pairs_h, *refs):
    bx, by, bz, cells = sizes
    total, face = bx * by * bz, by * bz
    tables_h, (own, face_lo, face_hi, mom, pairs), tables = refs[:7], refs[7:12], refs[12:19]
    fill, offsets, burgers, line, level, sems = refs[19:]
    table_copies = [
        pltpu.make_async_copy(u, v, sems.at[5 + k]) for k, (u, v) in enumerate(zip(tables_h, tables))
    ]
    moves = ((fill_h, fill), (pairs_h, pairs), (burgers_h, burgers), (line_h, line), (offsets_h, offsets))
    copies = [pltpu.make_async_copy(u, v, sems.at[k]) for k, (u, v) in enumerate(moves)]
    for copy in copies + table_copies:
        copy.start()
    for copy in copies:
        copy.wait()
    for x in range(bx):
        for y in range(by):
            column = jnp.broadcast_to(fill[x][:, y : y + 1], (bz, lanes))
            level[x * face + y * bz : x * face + (y + 1) * bz, :] = column
    live = lax.broadcasted_iota(jnp.int32, (total, lanes), 1) < level[...]
    b, l = [], []
    for d in range(3):
        own[d] = offsets[d]
        b.append(jnp.where(live, burgers[d], 0.0))
        l.append(jnp.where(live, line[d], 0.0))
        own[3 + d] = b[d]
        own[6 + d] = l[d]
    entries = pairs.shape[1]
    code = pairs[...]
    block_no = code // code_total
    code_no = code - block_no * code_total
    alive = lax.broadcasted_iota(jnp.int32, (1, entries), 1) < count[0]
    of_block = lax.broadcasted_iota(jnp.int32, (total, entries), 0) == block_no
    of_code = lax.broadcasted_iota(jnp.int32, (lanes, entries), 0) == code_no
    own[9] = lax.dot_general(
        jnp.where(of_block & alive, 1.0, 0.0).astype(bf16),
        jnp.where(of_code, 1.0, 0.0).astype(bf16),
        (((1,), (1,)), ((), ())),
        preferred_element_type=f32,
    )
    cx, cy, cz = bx // 2, by // 2, bz // 2
    here = lax.axis_index(axes[0])
    for axis in axes[1:]:
        here = here * lax.axis_size(axis) + lax.axis_index(axis)
    first_lane = here * (cx * cy * cz)
    wide = lax.broadcasted_iota(jnp.int32, (face, lanes), 1)
    deep = lax.broadcasted_iota(jnp.int32, (face, lanes), 0)
    local = deep // (2 * bz) * cz + deep % bz // 2
    sums = []
    for feature in moment_rows(b, l):
        column = []
        for x in range(cx):
            both = feature[2 * x * face : (2 * x + 1) * face] + feature[(2 * x + 1) * face : (2 * x + 2) * face]
            column.append(jnp.sum(both, 1, keepdims=True))
        sums.append(column)
    for chunk in range(cells // lanes):
        for f, column in enumerate(sums):
            placed = jnp.zeros((face, lanes), f32)
            for x in range(cx):
                lane_of = first_lane + x * cy * cz + local - chunk * lanes
                placed = placed + jnp.where(wide == lane_of, column[x], 0.0)
            mom[chunk * 8 + f : chunk * 8 + f + 1, :] = jnp.sum(placed, 0, keepdims=True)
    for d in range(parts_sent):
        face_lo[d * face : (d + 1) * face] = own[d, 0:face]
        face_hi[d * face : (d + 1) * face] = own[d, total - face : total]
    face_lo[parts_sent * face :] = mom[...]
    face_hi[parts_sent * face :] = mom[...]
    for copy in table_copies:
        copy.wait()


def rim_kernel(sizes, both_ways, own, mom, x_lo, x_hi, *refs):
    bx, by, bz, _ = sizes
    face = by * bz
    (face_lo, face_hi, x_both, mom_x), more = refs[-4:], refs[1:-4]
    for y, out in ((0, face_lo), (by - 1, face_hi)):
        for d in range(parts_sent):
            to, at = d * (bx + 2) * bz, y * bz
            for x in range(bx + 2):
                if x == 0 or x == bx + 1:
                    start = d * face + at
                    rows = (x_lo if x == 0 else x_hi)[start : start + bz]
                else:
                    start = (x - 1) * face + at
                    rows = own[d, start : start + bz]
                out[to + x * bz : to + (x + 1) * bz] = rows
    x_both[0 : x_lo.shape[0]] = x_lo[...]
    x_both[x_lo.shape[0] :] = x_hi[...]
    head = parts_sent * face
    total = mom[...] + x_lo[head:]
    if both_ways:
        total = total + x_hi[head:]
    for v in more:
        total = total + v[...]
    mom_x[...] = total
    head = parts_sent * (bx + 2) * bz
    face_lo[head:] = total
    face_hi[head:] = total


def shape_blocks(sizes, sources, stage, right, weighed, left=None):
    bx, by, bz, _ = sizes
    heights = group_heights(bx, by, bz)
    base = 0
    for group, part in sources:
        h = heights[group]
        zero = jnp.zeros((h, lanes), f32)
        place = position(group, h, bx, by, bz)
        q = [part(d) + place[d] for d in range(3)]
        b = [part(3 + d) for d in range(3)]
        l = [part(6 + d) for d in range(3)]
        rows = moment_rows(b, l) + cross_rows(q, b, l)
        lhs, rhs = distance_rows(q)
        rows = rows + [zero] * (16 - len(rows)) + rhs + [zero] * (32 - len(rhs))
        if left is not None:
            rows = rows + lhs + [zero] * (32 - len(lhs))
        for f, value in enumerate(rows):
            stage[pl.ds(base * 80 + f, h, stride=80), :] = value
        base += h

    def shape_block(block, carry):
        at = pl.multiple_of(block * 80, 16)
        product = stage[pl.ds(at, 16), :]
        high = product.astype(bf16)
        low = (product - high.astype(f32)).astype(bf16)
        weighed[block, 0:16, 0:lanes] = high
        weighed[block, 0:16, lanes : 2 * lanes] = high
        weighed[block, 16:32, 0:lanes] = low
        weighed[block, 16:32, lanes : 2 * lanes] = jnp.zeros_like(low)
        right[block] = stage[pl.ds(at + 16, 32), :].astype(bf16)
        if left is not None:
            left[block] = stage[pl.ds(at + 48, 32), :].astype(bf16)
        return carry

    lax.fori_loop(0, base, shape_block, 0, unroll=8)


def rows_of(ref, start, height):
    return lambda d: ref[start + d * height : start + (d + 1) * height, :]


def ranked(size):
    down = lax.broadcasted_iota(jnp.int32, (size, size), 0)
    across = lax.broadcasted_iota(jnp.int32, (size, size), 1)
    return jnp.where(down > across, 1.0, jnp.where(down == across, mark, 0.0)).astype(bf16)


def spread(rank, fields, chunks):
    lane = lax.broadcasted_iota(jnp.int32, rank.shape, 1).astype(f32) + mark
    hot = [jnp.where(rank == lane + float(m * lanes), 1.0, 0.0).astype(bf16) for m in range(chunks)]
    return jnp.dot(fields, jnp.concatenate(hot, 1), preferred_element_type=f32)


def put_list(rows, start, low, high, number, spare):
    for m in range(low.shape[1] // lanes):
        lane = lax.broadcasted_iota(jnp.int32, (1, lanes), 1) + m * lanes
        part = slice(m * lanes, (m + 1) * lanes)
        value = (low[:, part] + 256.0 * high[:, part]).astype(jnp.int32)
        rows[start + m : start + m + 1, :] = jnp.where(lane < number, value, spare)


def own_kernel(sizes, codes_of, pairs, count, own, right, weighed, left, todo, stage, rows, sem):
    bx, by, bz, _ = sizes
    total = bx * by * bz
    entries = pairs.shape[1]
    code = lax.broadcasted_iota(jnp.int32, (total * code_total, entries), 0)
    hot = jnp.where(code == pairs[...], 1.0, 0.0).astype(bf16)
    fields = jnp.dot(codes_of[...], hot, preferred_element_type=f32)
    alive = lax.broadcasted_iota(jnp.int32, (1, entries), 1) < count[0]
    marks = [jnp.where(alive, fields[k : k + 1], 0.0) for k in range(2, 6)]
    tall = jnp.concatenate([jnp.broadcast_to(v, (lanes, entries)) for v in marks], 0).astype(bf16)
    ranks = lax.dot_general(
        ranked(entries), tall, (((1,), (1,)), ((), ())), preferred_element_type=f32
    )
    ends = fields.astype(bf16)
    rows[...] = jnp.zeros_like(rows)
    lane = lax.broadcasted_iota(jnp.int32, (1, lanes), 1)
    numbers = jnp.zeros((1, lanes), jnp.int32)
    for k in range(4):
        both = spread(ranks[:, k * lanes : (k + 1) * lanes], ends, 2)
        number = jnp.sum(marks[k], 1, keepdims=True).astype(jnp.int32)
        low, high = (both[1:2], both[0:1]) if k == 1 else (both[0:1], both[1:2])
        put_list(rows, 2 * k, low, high, number, total)
        numbers = jnp.where(lane == k, number, numbers)
    rows[8:9, :] = numbers
    copy = pltpu.make_async_copy(rows, todo, sem)
    copy.start()
    shape_blocks(sizes, [(0, lambda d: own[d])], stage, right, weighed, left)
    left[total] = left[0]
    copy.wait()


def list_inbound(rows_of_set, marks_of, ends_of, sources, flags, rows, spare):
    base = 0
    for _, part in sources:
        height = part(9).shape[0]
        flags[base : base + height, :] = part(9)
        base += height
    picked = jnp.dot(rows_of_set[...], flags[...].astype(bf16), preferred_element_type=f32)
    on = (picked * marks_of[...].astype(f32)).astype(bf16)
    on = jnp.dot(on, jnp.ones((lanes, lanes), bf16), preferred_element_type=f32)
    rank = jnp.dot(ranked(on.shape[0]), on.astype(bf16), preferred_element_type=f32)
    both = spread(rank, ends_of[...], 2)
    number = jnp.sum(on, 0, keepdims=True).astype(jnp.int32)
    rows[...] = jnp.zeros_like(rows)
    put_list(rows, 0, both[0:1], both[1:2], number, spare)
    rows[2:3, :] = number


def interact(lookup, number, right, weighed, left, acc, half=None):
    def step(start, width):
        results = []
        for k in range(width):
            entry = lookup(start + k)
            row, col = entry & 255, entry >> 8
            square = lax.dot_general(
                right[col], left[row], (((0,), (0,)), ((), ())), preferred_element_type=f32
            )
            root = lax.rsqrt(square)
            weight = root * root * root
            high = weight.astype(bf16)
            low = (weight - high.astype(f32)).astype(bf16)
            both = jnp.dot(
                weighed[col], jnp.concatenate([high, low], 0), preferred_element_type=f32
            )
            results.append((row, both[0:16] + both[16:32]))
        for row, value in results:
            at_row = pl.ds(pl.multiple_of(row * 16, 16), 16)
            acc[at_row, :] += value

    def whole(at, carry):
        step(at * unroll, unroll)
        return carry

    def rest(at, carry):
        step(done + at * tail_unroll, tail_unroll)
        return carry

    steps = (number + unroll - 1 - 2 * tail_unroll) // unroll
    done = steps * unroll
    middle = (steps + 1) // 2
    lax.fori_loop(middle if half == 1 else 0, middle if half == 0 else steps, whole, 0)
    if half != 0:
        lax.fori_loop(0, (jnp.maximum(number - done, 0) + tail_unroll - 1) // tail_unroll, rest, 0)


def near_kernel(half, todo, right, weighed, left, *refs):
    acc = refs[-1]
    acc[...] = jnp.zeros_like(acc)
    n = todo[8, 0]
    interact(joined(todo, 0, n, todo, 2), n + todo[8, 1], right, weighed, left, acc, half)


def listed(rows, start):
    return lambda at: rows[start + (at >> 7), at & 127]


def joined(rows, start, number, more, then_start):
    first, then = listed(rows, start), listed(more, then_start)
    return lambda at: jnp.where(at < number, first(at), then(jnp.maximum(at - number, 0)))


def side_sources(sizes, groups, mine, both):
    bx, by, bz, cells = sizes
    heights = group_heights(bx, by, bz)
    mom_rows = 8 * cells // lanes
    sources = []
    for g in groups:
        if g % 5 == 0:
            sources.append((g, lambda d: mine[d]))
        else:
            h = heights[g]
            start = (parts_sent * h + mom_rows) if g % 5 in (2, 4) else 0
            sources.append((g, rows_of(both[g >= 5], start, h)))
    return sources


def beside_kernel(sizes, rows_of_set, marks_of, ends_of, x_both, p_mine, p_x_both, mom_in, _, right, weighed, found, mom_out, stage, flags, rows, sem):
    bx, by, bz, _ = sizes
    sources = side_sources(sizes, set_groups(1), p_mine, (x_both, p_x_both))
    list_inbound(rows_of_set, marks_of, ends_of, sources, flags, rows, bx * by * bz)
    copy = pltpu.make_async_copy(rows, found, sem)
    copy.start()
    mom_out[...] = mom_in[...]
    shape_blocks(sizes, sources, stage, right, weighed)
    copy.wait()


def side_kernel(todo, found, right, weighed, left, _, acc):
    acc[...] = jnp.zeros_like(acc)
    n = todo[8, 2]
    interact(joined(todo, 4, n, found, 0), n + found[2, 0], right, weighed, left, acc)


def coarse_place(sizes, axes, chunk):
    bx, by, bz, _ = sizes
    coarse = (bx // 2, by // 2, bz // 2)
    number = lax.broadcasted_iota(jnp.int32, (1, lanes), 1) + chunk * lanes
    places = []
    for d in (2, 1, 0):
        places.append(number % coarse[d])
        number = number // coarse[d]
    for k, d in enumerate((2, 1, 0)):
        size = lax.axis_size(axes[d])
        places[k] = places[k] + number % size * coarse[d]
        number = number // size
    return places[::-1]


def close_kernel(sizes, axes, grid, moments, todo, rows_of_set, marks_of, ends_of, y_both, p_y_both, left, acc_a, acc_b, acc_c, own, *refs):
    bx, by, bz, cells = sizes
    total, face = bx * by * bz, by * bz
    mom_parts = refs[:-9]
    out, right, weighed, stage, acc, flags, rows, found, sem = refs[-9:]
    sources = side_sources(sizes, set_groups(2), None, (y_both, p_y_both))
    list_inbound(rows_of_set, marks_of, ends_of, sources, flags, rows, total)
    copy = pltpu.make_async_copy(rows, found, sem)
    copy.start()
    shape_blocks(sizes, sources, stage, right, weighed)
    acc[...] = acc_a[...] + acc_b[...] + acc_c[...]
    copy.wait()
    n = todo[8, 3]
    interact(joined(todo, 6, n, found, 0), n + found[2, 0], right, weighed, left, acc)
    mom = moments(y_both, p_y_both, mom_parts)

    cx, cy, cz = bx // 2, by // 2, bz // 2
    deep = lax.broadcasted_iota(jnp.int32, (face, lanes), 0)
    local = (None, deep // (2 * bz), deep % bz // 2)
    far = [[] for _ in range(6)]
    for x in range(cx):
        totals = [jnp.zeros((face, lanes), f32)] * 6
        for chunk in range(cells // lanes):
            lengths = []
            cell_of = coarse_place(sizes, axes, chunk)
            for d, axis in enumerate(axes):
                at = lax.axis_index(axis) * (cx, cy, cz)[d] + (x if d == 0 else local[d])
                delta = at - cell_of[d]
                half = grid[d] // 2
                delta = jnp.where(delta >= grid[d] - half, delta - grid[d], delta)
                delta = jnp.where(delta < -half, delta + grid[d], delta)
                lengths.append(2.0 * delta.astype(f32))
            radius = lengths[0] * lengths[0] + lengths[1] * lengths[1] + lengths[2] * lengths[2]
            root = lax.rsqrt(radius + core_square)
            weight = jnp.where(radius == 0.0, 0.0, root * root * root)
            m = [mom[chunk * 8 + f : chunk * 8 + f + 1] for f in range(8)]
            turned = turn_rows([weight * v for v in lengths], m)
            totals = [t + v for t, v in zip(totals, turned)]
        for f in range(6):
            far[f].append(jnp.sum(totals[f], 1, keepdims=True))

    place = position(0, total, bx, by, bz)
    p = [own[d] + place[d] for d in range(3)]
    b = [own[3 + d] for d in range(3)]
    l = [own[6 + d] for d in range(3)]
    moment = [acc[pl.ds(f, total, stride=16), :] for f in range(8)]
    crossed = [acc[pl.ds(8 + f, total, stride=16), :] for f in range(6)]
    turned = turn_rows(p, moment)
    s = []
    for f in range(6):
        column = jnp.concatenate([far[f][x // 2] for x in range(bx)], 0)
        s.append(turned[f] - crossed[f] + column)
    push = [
        s[0] * b[0] + s[3] * b[1] + s[4] * b[2],
        s[3] * b[0] + s[1] * b[1] + s[5] * b[2],
        s[4] * b[0] + s[5] * b[1] + s[2] * b[2],
    ]
    out[0] = kernel_scale * (push[1] * l[2] - push[2] * l[1])
    out[1] = kernel_scale * (push[2] * l[0] - push[0] * l[2])
    out[2] = kernel_scale * (push[0] * l[1] - push[1] * l[0])


def shifted(value, axis, step):
    size = lax.axis_size(axis)
    return lax.ppermute(value, axis, [(i, (i + step) % size) for i in range(size)])


def ring_sum(value, axis):
    total = value
    for step in range(1, lax.axis_size(axis)):
        total = total + shifted(value, axis, step)
    return total


def beside_z(value, layers):
    size = lax.axis_size("gz")
    if size == 2:
        return shifted(value, "gz", 1)
    head = value.shape
    split = value.reshape(-1, layers, lanes)
    above = shifted(split[:, :1], "gz", -1)
    below = shifted(split[:, layers - 1 :], "gz", 1)
    middle = split[:, 1 : layers - 1]
    return jnp.concatenate([above, middle, below], 1).reshape(head)


def body(offsets, burgers, line, block_fill, near_pairs, pair_count):
    _, bx, by, bz, slots = offsets.shape
    axes = ("gx", "gy", "gz")
    sizes = [lax.axis_size(axis) for axis in axes]
    heights = group_heights(bx, by, bz)
    own, face, rim = heights[0], heights[1], heights[3]
    set_size = [sum(heights[g] for g in set_groups(which)) for which in range(3)]
    coarse = (bx // 2, by // 2, bz // 2)
    grid = tuple(c * n for c, n in zip(coarse, sizes))
    per_device = coarse[0] * coarse[1] * coarse[2]
    cells = per_device * sizes[0] * sizes[1] * sizes[2]
    mom_rows = 8 * cells // lanes
    kinds = (bx, by, bz, cells)
    entries = near_pairs.shape[0]
    vmem = pl.BlockSpec(memory_space=pltpu.VMEM)
    smem = pl.BlockSpec(memory_space=pltpu.SMEM)
    hbm = pl.BlockSpec(memory_space=pltpu.HBM)
    anywhere = pl.BlockSpec(memory_space=pl.ANY)
    shape = jax.ShapeDtypeStruct
    flat = lambda v: v.reshape(3, own, slots)
    far = lambda v: pltpu.with_memory_space_constraint(v, pltpu.HBM)

    tables = [jnp.asarray(v.astype(bf16)) for v in work_tables(bx, by, bz)]
    assert max(entries, tables[1].shape[0], tables[4].shape[0]) + unroll <= 2 * lanes

    def call(kernel, out_shape, in_specs, out_specs, scratch, name, cost, limit=12):
        return pl.pallas_call(
            kernel,
            out_shape=out_shape,
            in_specs=in_specs,
            out_specs=out_specs,
            scratch_shapes=scratch,
            compiler_params=pltpu.CompilerParams(vmem_limit_bytes=limit * 2**20),
            cost_estimate=pl.CostEstimate(flops=cost, bytes_accessed=cost, transcendentals=0),
            name=name,
        )

    face_shape = shape((parts_sent * face + mom_rows, lanes), f32)
    rim_shape = shape((parts_sent * rim + mom_rows, lanes), f32)
    mom_shape = shape((mom_rows, lanes), f32)
    acc_shape = shape(((own + 1) * 16, lanes), f32)
    mine, face_lo, face_hi, mom, pairs, codes_of, *inbound = call(
        functools.partial(pack_kernel, kinds, axes),
        [
            shape((parts_sent, own, lanes), f32),
            face_shape,
            face_shape,
            mom_shape,
            shape((1, entries), jnp.int32),
            *[shape(v.shape, v.dtype) for v in tables],
        ],
        [smem] + [hbm] * 12,
        [vmem] * 12,
        [
            pltpu.VMEM((bx, bz, by), jnp.int32),
            pltpu.VMEM((3, own, lanes), f32),
            pltpu.VMEM((3, own, lanes), f32),
            pltpu.VMEM((3, own, lanes), f32),
            pltpu.VMEM((own, lanes), jnp.int32),
            pltpu.SemaphoreType.DMA((12,)),
        ],
        "pack",
        10**6,
    )(
        pair_count,
        far(jnp.transpose(block_fill, (0, 2, 1))),
        far(flat(offsets)),
        far(flat(burgers)),
        far(flat(line)),
        far(near_pairs.reshape(1, -1)),
        *[far(v) for v in tables],
    )

    x_far = [shifted(mom, "gx", step) for step in range(2, sizes[0] - 1)]
    x_lo = shifted(face_hi, "gx", 1)
    x_hi = shifted(face_lo, "gx", -1)
    right, weighed, left, todo = call(
        functools.partial(own_kernel, kinds),
        [
            shape((own, 32, lanes), bf16),
            shape((own, 32, 2 * lanes), bf16),
            shape((own + 1, 32, lanes), bf16),
            pltpu.SMEM((16, lanes), jnp.int32),
        ],
        [vmem, vmem, smem, vmem],
        [vmem, vmem, vmem, smem],
        [
            pltpu.VMEM((own * 80, lanes), f32),
            pltpu.VMEM((16, lanes), jnp.int32),
            pltpu.SemaphoreType.DMA,
        ],
        "own",
        10**7,
    )(codes_of, pairs, pair_count, mine)
    p_mine = beside_z(mine, bz)

    def near(half, *follows):
        return call(
            functools.partial(near_kernel, half),
            acc_shape,
            [smem, vmem, vmem, vmem] + [anywhere] * len(follows),
            vmem,
            [],
            "near_first" if half == 0 else "near_second",
            10**7,
        )(todo, right, weighed, left, *follows)

    acc_a = near(0)
    side_lo, side_hi, x_both, mom_x = call(
        functools.partial(rim_kernel, kinds, sizes[0] > 2),
        [rim_shape, rim_shape, shape((2 * (parts_sent * face + mom_rows), lanes), f32), mom_shape],
        [vmem] * 4 + [anywhere] + [vmem] * len(x_far),
        [vmem] * 4,
        [],
        "rim",
        10**6,
    )(mine, mom, x_lo, x_hi, acc_a, *x_far)
    y_lo = shifted(side_hi, "gy", 1)
    y_hi = shifted(side_lo, "gy", -1)
    y_far = [shifted(mom_x, "gy", step) for step in range(2, sizes[1] - 1)]
    p_x_both = beside_z(x_both, bz)
    acc_b = near(1, side_lo, side_hi)
    right_1, weighed_1, found, mom_kept = call(
        functools.partial(beside_kernel, kinds),
        [
            shape((set_size[1], 32, lanes), bf16),
            shape((set_size[1], 32, 2 * lanes), bf16),
            pltpu.SMEM((8, lanes), jnp.int32),
            mom_shape,
        ],
        [vmem] * 7 + [anywhere],
        [vmem, vmem, smem, vmem],
        [
            pltpu.VMEM((set_size[1] * 80, lanes), f32),
            pltpu.VMEM((set_size[1], lanes), f32),
            pltpu.VMEM((8, lanes), jnp.int32),
            pltpu.SemaphoreType.DMA,
        ],
        "beside",
        10**7,
    )(*inbound[:3], x_both, p_mine, p_x_both, mom_x, acc_b)
    for v in y_far:
        mom_kept = mom_kept + v
    y_both = jnp.concatenate([y_lo, y_hi, mom_kept], 0)
    p_y_both = beside_z(y_both, bz)

    acc_c = call(
        side_kernel,
        acc_shape,
        [smem, smem, vmem, vmem, vmem, anywhere],
        vmem,
        [],
        "side",
        10**7,
    )(todo, found, right_1, weighed_1, left, y_both)
    tail = parts_sent * rim
    if sizes[2] == 2:
        mom_parts = []

        def moments(y_both, p_y_both, parts):
            spans = [slice(tail, tail + mom_rows)]
            if sizes[1] > 2:
                spans.append(slice(2 * tail + mom_rows, 2 * (tail + mom_rows)))
            spans.append(slice(2 * (tail + mom_rows), 2 * tail + 3 * mom_rows))
            return sum(y_both[span] + p_y_both[span] for span in spans)

    else:
        mom_parts = [ring_sum(mom_kept + y_lo[tail:] + y_hi[tail:], "gz")]
        moments = lambda y_both, p_y_both, parts: parts[0][...]

    forces = call(
        functools.partial(close_kernel, kinds, axes, grid, moments),
        shape((3, own, lanes), f32),
        [smem] + [vmem] * (10 + len(mom_parts)),
        vmem,
        [
            pltpu.VMEM((set_size[2], 32, lanes), bf16),
            pltpu.VMEM((set_size[2], 32, 2 * lanes), bf16),
            pltpu.VMEM((set_size[2] * 80, lanes), f32),
            pltpu.VMEM(((own + 1) * 16, lanes), f32),
            pltpu.VMEM((set_size[2], lanes), f32),
            pltpu.VMEM((8, lanes), jnp.int32),
            pltpu.SMEM((8, lanes), jnp.int32),
            pltpu.SemaphoreType.DMA,
        ],
        "close",
        10**7,
    )(todo, *inbound[3:], y_both, p_y_both, left, acc_a, acc_b, acc_c, mine, *mom_parts)
    return forces.reshape(3, bx, by, bz, slots)


def solution(mesh):
    in_specs = (
        P(None, "gx", "gy", "gz", None),
        P(None, "gx", "gy", "gz", None),
        P(None, "gx", "gy", "gz", None),
        P("gx", "gy", "gz"),
        P(("gx", "gy", "gz")),
        P(("gx", "gy", "gz")),
    )
    out_specs = P(None, "gx", "gy", "gz", None)
    return jax.shard_map(body, mesh=mesh, in_specs=in_specs, out_specs=out_specs, check_vma=False)
```

```python
import functools
import math

import jax
import jax.numpy as jnp
import numpy as np
from jax import lax
from jax.experimental import pallas as pl
from jax.experimental.pallas import tpu as pltpu
from jax.sharding import PartitionSpec as P

stencil_table = (
    (0, 0, 0),
    (1, 0, 0),
    (0, 1, 0),
    (0, 0, 1),
    (1, 1, 0),
    (-1, 1, 0),
    (1, 0, 1),
    (1, 0, -1),
    (0, 1, 1),
    (0, -1, 1),
    (1, 1, -1),
    (1, -1, 1),
    (-1, 1, 1),
    (1, 1, 1),
)
code_total = len(stencil_table)
kernel_scale = 1.0 / (8.0 * math.pi)
core_square = 0.09
lanes = 128
mark = 2048.0
parts_sent = 10
unroll = 64
short_steps = (16, 32, 48)
first_share = 96
f32 = jnp.float32
bf16 = jnp.bfloat16


group_set = (0, 1, 1, 2, 2, 1, 1, 1, 2, 2)


def set_groups(which):
    return [g for g in range(10) if group_set[g] == which]


def group_heights(bx, by, bz):
    return [bx * by * bz, by * bz, by * bz, (bx + 2) * bz, (bx + 2) * bz] * 2


def block_layout(bx, by, bz):
    coords = []
    for z_of in ([z + 1 for z in range(bz)], [bz + 1 if z == 0 else 0 for z in range(bz)]):
        coords.append([(x + 1, y + 1, z) for x in range(bx) for y in range(by) for z in z_of])
        for x in (0, bx + 1):
            coords.append([(x, y + 1, z) for y in range(by) for z in z_of])
        for y in (0, by + 1):
            coords.append([(x, y, z) for x in range(bx + 2) for z in z_of])
    return coords


def work_tables(bx, by, bz):
    groups = block_layout(bx, by, bz)
    place = {}
    count = [0, 0, 0]
    for g, group in enumerate(groups):
        for c in group:
            place[c] = (group_set[g], count[group_set[g]])
            count[group_set[g]] += 1
    codes = np.zeros((8, count[0] * code_total), np.float32)
    for a, at in enumerate(groups[0]):
        for code, o in enumerate(stencil_table):
            which, b = place[tuple(at[d] + o[d] for d in range(3))]
            k = a * code_total + code
            codes[:2, k] = a, b
            codes[(2, 4, 5)[which], k] = 1.0
            codes[3, k] = which == 0 and code > 0
    inbound = []
    for which in (1, 2):
        found = []
        for at, (at_set, h) in place.items():
            for code, o in enumerate(stencil_table):
                to, b = place.get(tuple(at[d] + o[d] for d in range(3)), (3, 0))
                if at_set == which and to == 0 and code:
                    found.append((b, h, code))
        size = -(-(len(found) + 1) // 16) * 16
        ranks = np.zeros((size, (code_total - 1) * count[which]), np.float32)
        ends = np.zeros((8, size), np.float32)
        for k, (b, h, code) in enumerate(found):
            at = (code - 1) * count[which] + h
            ranks[k + 1 : len(found), at] = ranks[size - 1, at] = 1.0
            ranks[k, at] = mark
            ends[:2, k] = b, h
        inbound += [ranks, ends]
    return [codes, *inbound]


def position(group, rows, bx, by, bz):
    row = lax.broadcasted_iota(jnp.int32, (rows, lanes), 0)
    z = row % bz
    line = row // bz
    kind = group % 5
    if kind == 0:
        x, y = line // by + 1, line % by + 1
    elif kind <= 2:
        x, y = jnp.full_like(row, 0 if kind == 1 else bx + 1), line + 1
    else:
        x, y = line, jnp.full_like(row, 0 if kind == 3 else by + 1)
    if group < 5:
        z = z + 1
    else:
        z = jnp.where(z == 0, bz + 1, 0)
    sides = (bx + 1, by + 1, bz + 1)
    return [v.astype(f32) - 0.5 * side for v, side in zip((x, y, z), sides)]


def moment_rows(b, l):
    zz = b[2] * l[2]
    return [
        b[0] * l[1],
        b[0] * l[2],
        b[1] * l[0],
        b[1] * l[2],
        b[2] * l[0],
        b[2] * l[1],
        b[0] * l[0] - zz,
        b[1] * l[1] - zz,
    ]


def cross_rows(q, b, l):
    c = [q[1] * b[2] - q[2] * b[1], q[2] * b[0] - q[0] * b[2], q[0] * b[1] - q[1] * b[0]]
    return [
        2.0 * c[0] * l[0],
        2.0 * c[1] * l[1],
        2.0 * c[2] * l[2],
        c[0] * l[1] + c[1] * l[0],
        c[0] * l[2] + c[2] * l[0],
        c[1] * l[2] + c[2] * l[1],
    ]


def turn_rows(r, m):
    return [
        2.0 * (r[1] * m[4] - r[2] * m[2]),
        2.0 * (r[2] * m[0] - r[0] * m[5]),
        2.0 * (r[0] * m[3] - r[1] * m[1]),
        r[1] * m[5] - r[0] * m[4] + r[2] * (m[6] - m[7]),
        r[0] * m[2] - r[2] * m[3] - r[1] * m[6],
        r[2] * m[1] + r[0] * m[7] - r[1] * m[0],
    ]


def pieces(value):
    first = value.astype(bf16).astype(f32)
    rest = value - first
    second = rest.astype(bf16).astype(f32)
    return first, second, rest - second


def distance_rows(q):
    near = q[0] * q[0] + q[1] * q[1] + q[2] * q[2]
    one = jnp.ones_like(near)
    left, right = [], []
    for axis in q:
        p1, p2, p3 = pieces(axis)
        left += [p1, p1, p2, p2, p1, p3]
        right += [-2.0 * v for v in (p1, p2, p1, p2, p3, p1)]
    left += [*pieces(near), one, one, one]
    right += [one, one, one, *pieces(near + core_square)]
    return left, right


def pack_kernel(sizes, axes, count, fill_h, offsets_h, burgers_h, line_h, pairs_h, *refs):
    bx, by, bz, cells = sizes
    total, face = bx * by * bz, by * bz
    tables_h, (own, face_lo, face_hi, mom, pairs), tables = refs[:5], refs[5:10], refs[10:15]
    fill, offsets, burgers, line, level, sems = refs[15:]
    table_copies = [
        pltpu.make_async_copy(u, v, sems.at[5 + k]) for k, (u, v) in enumerate(zip(tables_h, tables))
    ]
    moves = ((fill_h, fill), (pairs_h, pairs), (burgers_h, burgers), (line_h, line), (offsets_h, offsets))
    copies = [pltpu.make_async_copy(u, v, sems.at[k]) for k, (u, v) in enumerate(moves)]
    for copy in copies + table_copies:
        copy.start()
    for copy in copies:
        copy.wait()
    for x in range(bx):
        for y in range(by):
            column = jnp.broadcast_to(fill[x][:, y : y + 1], (bz, lanes))
            level[x * face + y * bz : x * face + (y + 1) * bz, :] = column
    live = lax.broadcasted_iota(jnp.int32, (total, lanes), 1) < level[...]
    b, l = [], []
    for d in range(3):
        own[d] = offsets[d]
        b.append(jnp.where(live, burgers[d], 0.0))
        l.append(jnp.where(live, line[d], 0.0))
        own[3 + d] = b[d]
        own[6 + d] = l[d]
    entries = pairs.shape[1]
    code = pairs[...]
    block_no = code // code_total
    code_no = code - block_no * code_total
    alive = lax.broadcasted_iota(jnp.int32, (1, entries), 1) < count[0]
    of_block = lax.broadcasted_iota(jnp.int32, (total, entries), 0) == block_no
    of_code = lax.broadcasted_iota(jnp.int32, (lanes, entries), 0) == code_no
    own[9] = lax.dot_general(
        jnp.where(of_block & alive, 1.0, 0.0).astype(bf16),
        jnp.where(of_code, 1.0, 0.0).astype(bf16),
        (((1,), (1,)), ((), ())),
        preferred_element_type=f32,
    )
    cx, cy, cz = bx // 2, by // 2, bz // 2
    here = lax.axis_index(axes[0])
    for axis in axes[1:]:
        here = here * lax.axis_size(axis) + lax.axis_index(axis)
    first_lane = here * (cx * cy * cz)
    wide = lax.broadcasted_iota(jnp.int32, (face, lanes), 1)
    deep = lax.broadcasted_iota(jnp.int32, (face, lanes), 0)
    local = deep // (2 * bz) * cz + deep % bz // 2
    sums = []
    for feature in moment_rows(b, l):
        column = []
        for x in range(cx):
            both = feature[2 * x * face : (2 * x + 1) * face] + feature[(2 * x + 1) * face : (2 * x + 2) * face]
            column.append(jnp.sum(both, 1, keepdims=True))
        sums.append(column)
    for chunk in range(cells // lanes):
        for f, column in enumerate(sums):
            placed = jnp.zeros((face, lanes), f32)
            for x in range(cx):
                lane_of = first_lane + x * cy * cz + local - chunk * lanes
                placed = placed + jnp.where(wide == lane_of, column[x], 0.0)
            mom[chunk * 8 + f : chunk * 8 + f + 1, :] = jnp.sum(placed, 0, keepdims=True)
    for d in range(parts_sent):
        face_lo[d * face : (d + 1) * face] = own[d, 0:face]
        face_hi[d * face : (d + 1) * face] = own[d, total - face : total]
    face_lo[parts_sent * face :] = mom[...]
    face_hi[parts_sent * face :] = mom[...]
    for copy in table_copies:
        copy.wait()


def rim_kernel(sizes, both_ways, own, mom, x_lo, x_hi, *refs):
    bx, by, bz, _ = sizes
    face = by * bz
    (face_lo, face_hi, x_all, mom_x), more = refs[-4:], refs[1:-4]
    for y, out in ((0, face_lo), (by - 1, face_hi)):
        for d in range(parts_sent):
            to, at = d * (bx + 2) * bz, y * bz
            for x in range(bx + 2):
                if x == 0 or x == bx + 1:
                    start = d * face + at
                    rows = (x_lo if x == 0 else x_hi)[start : start + bz]
                else:
                    start = (x - 1) * face + at
                    rows = own[d, start : start + bz]
                out[to + x * bz : to + (x + 1) * bz] = rows
    total = bx * by * bz
    for d in range(parts_sent):
        x_all[d * total : (d + 1) * total] = own[d]
    start = parts_sent * total
    for v in (x_lo, x_hi):
        x_all[start : start + v.shape[0]] = v[...]
        start += v.shape[0]
    head = parts_sent * face
    total = mom[...] + x_lo[head:]
    if both_ways:
        total = total + x_hi[head:]
    for v in more:
        total = total + v[...]
    mom_x[...] = total
    head = parts_sent * (bx + 2) * bz
    face_lo[head:] = total
    face_hi[head:] = total


def shape_blocks(sizes, sources, stage, right, weighed, left=None):
    bx, by, bz, _ = sizes
    heights = group_heights(bx, by, bz)
    base = 0
    for group, part in sources:
        h = heights[group]
        zero = jnp.zeros((h, lanes), f32)
        place = position(group, h, bx, by, bz)
        q = [part(d) + place[d] for d in range(3)]
        b = [part(3 + d) for d in range(3)]
        l = [part(6 + d) for d in range(3)]
        rows = moment_rows(b, l) + cross_rows(q, b, l)
        lhs, rhs = distance_rows(q)
        rows = rows + [zero] * (16 - len(rows)) + rhs + [zero] * (32 - len(rhs))
        if left is not None:
            rows = rows + lhs + [zero] * (32 - len(lhs))
        for f, value in enumerate(rows):
            stage[pl.ds(base * 80 + f, h, stride=80), :] = value
        base += h

    def shape_block(block, carry):
        at = pl.multiple_of(block * 80, 16)
        product = stage[pl.ds(at, 16), :]
        high = product.astype(bf16)
        low = (product - high.astype(f32)).astype(bf16)
        weighed[block, 0:16, 0:lanes] = high
        weighed[block, 0:16, lanes : 2 * lanes] = high
        weighed[block, 16:32, 0:lanes] = low
        weighed[block, 16:32, lanes : 2 * lanes] = jnp.zeros_like(low)
        right[block] = stage[pl.ds(at + 16, 32), :].astype(bf16)
        if left is not None:
            left[block] = stage[pl.ds(at + 48, 32), :].astype(bf16)
        return carry

    lax.fori_loop(0, base, shape_block, 0, unroll=8)


def rows_of(ref, start, height):
    return lambda d: ref[start + d * height : start + (d + 1) * height, :]


def ranked(size):
    down = lax.broadcasted_iota(jnp.int32, (size, size), 0)
    across = lax.broadcasted_iota(jnp.int32, (size, size), 1)
    return jnp.where(down > across, 1.0, jnp.where(down == across, mark, 0.0)).astype(bf16)


def spread(rank, fields, chunks):
    lane = lax.broadcasted_iota(jnp.int32, rank.shape, 1).astype(f32) + mark
    hot = [jnp.where(rank == lane + float(m * lanes), 1.0, 0.0).astype(bf16) for m in range(chunks)]
    return jnp.dot(fields, jnp.concatenate(hot, 1), preferred_element_type=f32)


def put_list(rows, start, low, high, number, spare):
    for m in range(low.shape[1] // lanes):
        lane = lax.broadcasted_iota(jnp.int32, (1, lanes), 1) + m * lanes
        part = slice(m * lanes, (m + 1) * lanes)
        value = (low[:, part] + 256.0 * high[:, part]).astype(jnp.int32)
        rows[start + m : start + m + 1, :] = jnp.where(lane < number, value, spare)


def own_kernel(sizes, codes_of, pairs, count, own, right, weighed, left, todo, stage, rows, sem):
    bx, by, bz, _ = sizes
    total = bx * by * bz
    entries = pairs.shape[1]
    code = lax.broadcasted_iota(jnp.int32, (total * code_total, entries), 0)
    hot = jnp.where(code == pairs[...], 1.0, 0.0).astype(bf16)
    fields = jnp.dot(codes_of[...], hot, preferred_element_type=f32)
    alive = lax.broadcasted_iota(jnp.int32, (1, entries), 1) < count[0]
    marks = [jnp.where(alive, fields[k : k + 1], 0.0) for k in range(2, 6)]
    tall = jnp.concatenate([jnp.broadcast_to(v, (lanes, entries)) for v in marks], 0).astype(bf16)
    ranks = lax.dot_general(
        ranked(entries), tall, (((1,), (1,)), ((), ())), preferred_element_type=f32
    )
    ends = fields.astype(bf16)
    rows[...] = jnp.zeros_like(rows)
    lane = lax.broadcasted_iota(jnp.int32, (1, lanes), 1)
    numbers = jnp.zeros((1, lanes), jnp.int32)
    for k in range(4):
        both = spread(ranks[:, k * lanes : (k + 1) * lanes], ends, 2)
        number = jnp.sum(marks[k], 1, keepdims=True).astype(jnp.int32)
        low, high = (both[1:2], both[0:1]) if k == 1 else (both[0:1], both[1:2])
        put_list(rows, 2 * k, low, high, number, total)
        numbers = jnp.where(lane == k, number, numbers)
    rows[8:9, :] = numbers
    copy = pltpu.make_async_copy(rows, todo, sem)
    copy.start()
    shape_blocks(sizes, [(0, lambda d: own[d])], stage, right, weighed, left)
    left[total] = left[0]
    copy.wait()


def list_inbound(ranks_of, ends_of, sources, flags, rows, spare):
    base = 0
    for _, part in sources:
        height = part(9).shape[0]
        flags[base : base + height, :] = part(9)
        base += height
    by_code = [jnp.broadcast_to(flags[:, c : c + 1], (base, lanes)) for c in range(1, code_total)]
    tall = jnp.concatenate(by_code, 0).astype(bf16)
    rank = jnp.dot(ranks_of[...], tall, preferred_element_type=f32)
    both = spread(rank, ends_of[...], 2)
    number = rank[rank.shape[0] - 1 :, :].astype(jnp.int32)
    rows[...] = jnp.zeros_like(rows)
    put_list(rows, 0, both[0:1], both[1:2], number, spare)
    rows[2:3, :] = number


def add_step(lookup, start, width, right, weighed, left, acc):
    results = []
    for k in range(width):
        entry = lookup(start + k)
        row, col = entry & 255, entry >> 8
        square = lax.dot_general(
            right[col], left[row], (((0,), (0,)), ((), ())), preferred_element_type=f32
        )
        root = lax.rsqrt(square)
        weight = root * root * root
        high = weight.astype(bf16)
        low = (weight - high.astype(f32)).astype(bf16)
        both = jnp.dot(weighed[col], jnp.concatenate([high, low], 0), preferred_element_type=f32)
        results.append((row, both[0:16] + both[16:32]))
    for row, value in results:
        at_row = pl.ds(pl.multiple_of(row * 16, 16), 16)
        acc[at_row, :] += value


def interact(lookup, start, end, *refs):
    number = end - start
    steps = (number + unroll - 1 - short_steps[-1]) // unroll
    done = start + steps * unroll

    def whole(at, carry):
        add_step(lookup, start + at * unroll, unroll, *refs)
        return carry

    lax.fori_loop(0, steps, whole, 0)
    left_over = end - done
    least = 0
    for width in short_steps:

        @pl.when((left_over > least) & (left_over <= width))
        def _():
            add_step(lookup, done, width, *refs)

        least = width


def near_list(todo):
    n = todo[8, 0]
    number = n + todo[8, 1]
    return joined(todo, 0, n, todo, 2), jnp.minimum(number, first_share), number


def near_kernel(todo, right, weighed, left, acc):
    acc[...] = jnp.zeros_like(acc)
    lookup, middle, _ = near_list(todo)
    interact(lookup, 0, middle, right, weighed, left, acc)


def listed(rows, start):
    return lambda at: rows[start + (at >> 7), at & 127]


def joined(rows, start, number, more, then_start):
    first, then = listed(rows, start), listed(more, then_start)
    return lambda at: jnp.where(at < number, first(at), then(jnp.maximum(at - number, 0)))


def side_sources(sizes, groups, here, beside):
    bx, by, bz, cells = sizes
    heights = group_heights(bx, by, bz)
    mom_rows = 8 * cells // lanes
    x_start = parts_sent * heights[0]
    starts = {0: 0, 1: x_start, 2: x_start + parts_sent * heights[1] + mom_rows, 3: 0, 4: parts_sent * heights[3] + mom_rows}
    return [(g, rows_of((here, beside)[g >= 5], starts[g % 5], heights[g])) for g in groups]


def mid_kernel(sizes, ranks_of, ends_of, x_all, p_x_all, mom_in, todo, right, weighed, left, *refs):
    bx, by, bz, _ = sizes
    right_1, weighed_1, found, mom_out, acc, stage, flags, rows, sem = refs[-9:]
    sources = side_sources(sizes, set_groups(1), x_all, p_x_all)
    list_inbound(ranks_of, ends_of, sources, flags, rows, bx * by * bz)
    copy = pltpu.make_async_copy(rows, found, sem)
    copy.start()
    mom_out[...] = mom_in[...]
    shape_blocks(sizes, sources, stage, right_1, weighed_1)
    acc[...] = jnp.zeros_like(acc)
    lookup, middle, number = near_list(todo)
    interact(lookup, middle, number, right, weighed, left, acc)
    copy.wait()


def side_kernel(todo, found, right, weighed, left, _, acc):
    acc[...] = jnp.zeros_like(acc)
    n = todo[8, 2]
    interact(joined(todo, 4, n, found, 0), 0, n + found[2, 0], right, weighed, left, acc)


def coarse_place(sizes, axes, chunk):
    bx, by, bz, _ = sizes
    coarse = (bx // 2, by // 2, bz // 2)
    number = lax.broadcasted_iota(jnp.int32, (1, lanes), 1) + chunk * lanes
    places = []
    for d in (2, 1, 0):
        places.append(number % coarse[d])
        number = number // coarse[d]
    for k, d in enumerate((2, 1, 0)):
        size = lax.axis_size(axes[d])
        places[k] = places[k] + number % size * coarse[d]
        number = number // size
    return places[::-1]


def close_kernel(sizes, axes, grid, moments, todo, ranks_of, ends_of, y_both, p_y_both, left, acc_a, acc_b, acc_c, own, *refs):
    bx, by, bz, cells = sizes
    total, face = bx * by * bz, by * bz
    mom_parts = refs[:-9]
    out, right, weighed, stage, acc, flags, rows, found, sem = refs[-9:]
    sources = side_sources(sizes, set_groups(2), y_both, p_y_both)
    list_inbound(ranks_of, ends_of, sources, flags, rows, total)
    copy = pltpu.make_async_copy(rows, found, sem)
    copy.start()
    shape_blocks(sizes, sources, stage, right, weighed)
    acc[...] = acc_a[...] + acc_b[...] + acc_c[...]
    copy.wait()
    n = todo[8, 3]
    interact(joined(todo, 6, n, found, 0), 0, n + found[2, 0], right, weighed, left, acc)
    mom = moments(y_both, p_y_both, mom_parts)

    cx, cy, cz = bx // 2, by // 2, bz // 2
    deep = lax.broadcasted_iota(jnp.int32, (face, lanes), 0)
    local = (None, deep // (2 * bz), deep % bz // 2)
    far = [[] for _ in range(6)]
    for x in range(cx):
        totals = [jnp.zeros((face, lanes), f32)] * 6
        for chunk in range(cells // lanes):
            lengths = []
            cell_of = coarse_place(sizes, axes, chunk)
            for d, axis in enumerate(axes):
                at = lax.axis_index(axis) * (cx, cy, cz)[d] + (x if d == 0 else local[d])
                delta = at - cell_of[d]
                half = grid[d] // 2
                delta = jnp.where(delta >= grid[d] - half, delta - grid[d], delta)
                delta = jnp.where(delta < -half, delta + grid[d], delta)
                lengths.append(2.0 * delta.astype(f32))
            radius = lengths[0] * lengths[0] + lengths[1] * lengths[1] + lengths[2] * lengths[2]
            root = lax.rsqrt(radius + core_square)
            weight = jnp.where(radius == 0.0, 0.0, root * root * root)
            m = [mom[chunk * 8 + f : chunk * 8 + f + 1] for f in range(8)]
            turned = turn_rows([weight * v for v in lengths], m)
            totals = [t + v for t, v in zip(totals, turned)]
        for f in range(6):
            far[f].append(jnp.sum(totals[f], 1, keepdims=True))

    place = position(0, total, bx, by, bz)
    p = [own[d] + place[d] for d in range(3)]
    b = [own[3 + d] for d in range(3)]
    l = [own[6 + d] for d in range(3)]
    moment = [acc[pl.ds(f, total, stride=16), :] for f in range(8)]
    crossed = [acc[pl.ds(8 + f, total, stride=16), :] for f in range(6)]
    turned = turn_rows(p, moment)
    s = []
    for f in range(6):
        column = jnp.concatenate([far[f][x // 2] for x in range(bx)], 0)
        s.append(turned[f] - crossed[f] + column)
    push = [
        s[0] * b[0] + s[3] * b[1] + s[4] * b[2],
        s[3] * b[0] + s[1] * b[1] + s[5] * b[2],
        s[4] * b[0] + s[5] * b[1] + s[2] * b[2],
    ]
    out[0] = kernel_scale * (push[1] * l[2] - push[2] * l[1])
    out[1] = kernel_scale * (push[2] * l[0] - push[0] * l[2])
    out[2] = kernel_scale * (push[0] * l[1] - push[1] * l[0])


def shifted(value, axis, step):
    size = lax.axis_size(axis)
    return lax.ppermute(value, axis, [(i, (i + step) % size) for i in range(size)])


def ring_sum(value, axis):
    total = value
    for step in range(1, lax.axis_size(axis)):
        total = total + shifted(value, axis, step)
    return total


def beside_z(value, layers):
    size = lax.axis_size("gz")
    if size == 2:
        return shifted(value, "gz", 1)
    head = value.shape
    split = value.reshape(-1, layers, lanes)
    above = shifted(split[:, :1], "gz", -1)
    below = shifted(split[:, layers - 1 :], "gz", 1)
    middle = split[:, 1 : layers - 1]
    return jnp.concatenate([above, middle, below], 1).reshape(head)


def body(offsets, burgers, line, block_fill, near_pairs, pair_count):
    _, bx, by, bz, slots = offsets.shape
    axes = ("gx", "gy", "gz")
    sizes = [lax.axis_size(axis) for axis in axes]
    heights = group_heights(bx, by, bz)
    own, face, rim = heights[0], heights[1], heights[3]
    set_size = [sum(heights[g] for g in set_groups(which)) for which in range(3)]
    coarse = (bx // 2, by // 2, bz // 2)
    grid = tuple(c * n for c, n in zip(coarse, sizes))
    per_device = coarse[0] * coarse[1] * coarse[2]
    cells = per_device * sizes[0] * sizes[1] * sizes[2]
    mom_rows = 8 * cells // lanes
    kinds = (bx, by, bz, cells)
    entries = near_pairs.shape[0]
    vmem = pl.BlockSpec(memory_space=pltpu.VMEM)
    smem = pl.BlockSpec(memory_space=pltpu.SMEM)
    hbm = pl.BlockSpec(memory_space=pltpu.HBM)
    anywhere = pl.BlockSpec(memory_space=pl.ANY)
    shape = jax.ShapeDtypeStruct
    flat = lambda v: v.reshape(3, own, slots)
    far = lambda v: pltpu.with_memory_space_constraint(v, pltpu.HBM)

    tables = [jnp.asarray(v.astype(bf16)) for v in work_tables(bx, by, bz)]
    assert max(entries, tables[1].shape[0], tables[3].shape[0]) + unroll <= 2 * lanes

    def call(kernel, out_shape, in_specs, out_specs, scratch, name, cost, limit=12):
        return pl.pallas_call(
            kernel,
            out_shape=out_shape,
            in_specs=in_specs,
            out_specs=out_specs,
            scratch_shapes=scratch,
            compiler_params=pltpu.CompilerParams(vmem_limit_bytes=limit * 2**20),
            cost_estimate=pl.CostEstimate(flops=cost, bytes_accessed=cost, transcendentals=0),
            name=name,
        )

    face_shape = shape((parts_sent * face + mom_rows, lanes), f32)
    rim_shape = shape((parts_sent * rim + mom_rows, lanes), f32)
    mom_shape = shape((mom_rows, lanes), f32)
    acc_shape = shape(((own + 1) * 16, lanes), f32)
    mine, face_lo, face_hi, mom, pairs, codes_of, *inbound = call(
        functools.partial(pack_kernel, kinds, axes),
        [
            shape((parts_sent, own, lanes), f32),
            face_shape,
            face_shape,
            mom_shape,
            shape((1, entries), jnp.int32),
            *[shape(v.shape, v.dtype) for v in tables],
        ],
        [smem] + [hbm] * 10,
        [vmem] * 10,
        [
            pltpu.VMEM((bx, bz, by), jnp.int32),
            pltpu.VMEM((3, own, lanes), f32),
            pltpu.VMEM((3, own, lanes), f32),
            pltpu.VMEM((3, own, lanes), f32),
            pltpu.VMEM((own, lanes), jnp.int32),
            pltpu.SemaphoreType.DMA((10,)),
        ],
        "pack",
        10**6,
    )(
        pair_count,
        far(jnp.transpose(block_fill, (0, 2, 1))),
        far(flat(offsets)),
        far(flat(burgers)),
        far(flat(line)),
        far(near_pairs.reshape(1, -1)),
        *[far(v) for v in tables],
    )

    x_far = [shifted(mom, "gx", step) for step in range(2, sizes[0] - 1)]
    x_lo = shifted(face_hi, "gx", 1)
    x_hi = shifted(face_lo, "gx", -1)
    right, weighed, left, todo = call(
        functools.partial(own_kernel, kinds),
        [
            shape((own, 32, lanes), bf16),
            shape((own, 32, 2 * lanes), bf16),
            shape((own + 1, 32, lanes), bf16),
            pltpu.SMEM((16, lanes), jnp.int32),
        ],
        [vmem, vmem, smem, vmem],
        [vmem, vmem, vmem, smem],
        [
            pltpu.VMEM((own * 80, lanes), f32),
            pltpu.VMEM((16, lanes), jnp.int32),
            pltpu.SemaphoreType.DMA,
        ],
        "own",
        10**7,
    )(codes_of, pairs, pair_count, mine)
    acc_a = call(
        near_kernel,
        acc_shape,
        [smem, vmem, vmem, vmem],
        vmem,
        [],
        "near",
        10**7,
    )(todo, right, weighed, left)
    side_lo, side_hi, x_all, mom_x = call(
        functools.partial(rim_kernel, kinds, sizes[0] > 2),
        [
            rim_shape,
            rim_shape,
            shape((parts_sent * (own + 2 * face) + 2 * mom_rows, lanes), f32),
            mom_shape,
        ],
        [vmem] * 4 + [anywhere] + [vmem] * len(x_far),
        [vmem] * 4,
        [],
        "rim",
        10**6,
    )(mine, mom, x_lo, x_hi, acc_a, *x_far)
    y_lo = shifted(side_hi, "gy", 1)
    y_hi = shifted(side_lo, "gy", -1)
    y_far = [shifted(mom_x, "gy", step) for step in range(2, sizes[1] - 1)]
    p_x_all = beside_z(x_all, bz)
    right_1, weighed_1, found, mom_kept, acc_b = call(
        functools.partial(mid_kernel, kinds),
        [
            shape((set_size[1], 32, lanes), bf16),
            shape((set_size[1], 32, 2 * lanes), bf16),
            pltpu.SMEM((8, lanes), jnp.int32),
            mom_shape,
            acc_shape,
        ],
        [vmem] * 5 + [smem, vmem, vmem, vmem, anywhere, anywhere],
        [vmem, vmem, smem, vmem, vmem],
        [
            pltpu.VMEM((set_size[1] * 80, lanes), f32),
            pltpu.VMEM((set_size[1], lanes), f32),
            pltpu.VMEM((8, lanes), jnp.int32),
            pltpu.SemaphoreType.DMA,
        ],
        "mid",
        10**7,
    )(*inbound[:2], x_all, p_x_all, mom_x, todo, right, weighed, left, side_lo, side_hi)
    for v in y_far:
        mom_kept = mom_kept + v
    y_both = jnp.concatenate([y_lo, y_hi, mom_kept], 0)
    p_y_both = beside_z(y_both, bz)

    acc_c = call(
        side_kernel,
        acc_shape,
        [smem, smem, vmem, vmem, vmem, anywhere],
        vmem,
        [],
        "side",
        10**7,
    )(todo, found, right_1, weighed_1, left, y_both)
    tail = parts_sent * rim
    if sizes[2] == 2:
        mom_parts = []

        def moments(y_both, p_y_both, parts):
            spans = [slice(tail, tail + mom_rows)]
            if sizes[1] > 2:
                spans.append(slice(2 * tail + mom_rows, 2 * (tail + mom_rows)))
            spans.append(slice(2 * (tail + mom_rows), 2 * tail + 3 * mom_rows))
            return sum(y_both[span] + p_y_both[span] for span in spans)

    else:
        mom_parts = [ring_sum(mom_kept + y_lo[tail:] + y_hi[tail:], "gz")]
        moments = lambda y_both, p_y_both, parts: parts[0][...]

    forces = call(
        functools.partial(close_kernel, kinds, axes, grid, moments),
        shape((3, own, lanes), f32),
        [smem] + [vmem] * (9 + len(mom_parts)),
        vmem,
        [
            pltpu.VMEM((set_size[2], 32, lanes), bf16),
            pltpu.VMEM((set_size[2], 32, 2 * lanes), bf16),
            pltpu.VMEM((set_size[2] * 80, lanes), f32),
            pltpu.VMEM(((own + 1) * 16, lanes), f32),
            pltpu.VMEM((set_size[2], lanes), f32),
            pltpu.VMEM((8, lanes), jnp.int32),
            pltpu.SMEM((8, lanes), jnp.int32),
            pltpu.SemaphoreType.DMA,
        ],
        "close",
        10**7,
    )(todo, *inbound[2:], y_both, p_y_both, left, acc_a, acc_b, acc_c, mine, *mom_parts)
    return forces.reshape(3, bx, by, bz, slots)


def solution(mesh):
    in_specs = (
        P(None, "gx", "gy", "gz", None),
        P(None, "gx", "gy", "gz", None),
        P(None, "gx", "gy", "gz", None),
        P("gx", "gy", "gz"),
        P(("gx", "gy", "gz")),
        P(("gx", "gy", "gz")),
    )
    out_specs = P(None, "gx", "gy", "gz", None)
    return jax.shard_map(body, mesh=mesh, in_specs=in_specs, out_specs=out_specs, check_vma=False)
```

```python
import functools
import math

import jax
import jax.numpy as jnp
import numpy as np
from jax import lax
from jax.experimental import pallas as pl
from jax.experimental.pallas import tpu as pltpu
from jax.sharding import PartitionSpec as P

stencil_table = (
    (0, 0, 0),
    (1, 0, 0),
    (0, 1, 0),
    (0, 0, 1),
    (1, 1, 0),
    (-1, 1, 0),
    (1, 0, 1),
    (1, 0, -1),
    (0, 1, 1),
    (0, -1, 1),
    (1, 1, -1),
    (1, -1, 1),
    (-1, 1, 1),
    (1, 1, 1),
)
code_total = len(stencil_table)
kernel_scale = 1.0 / (8.0 * math.pi)
core_square = 0.09
lanes = 128
mark = 2048.0
parts_sent = 10
unroll = 64
short_steps = (16, 32, 48)
first_share = 96
f32 = jnp.float32
bf16 = jnp.bfloat16


group_set = (0, 1, 1, 2, 2, 1, 1, 1, 2, 2)


def set_groups(which):
    return [g for g in range(10) if group_set[g] == which]


def group_heights(bx, by, bz):
    return [bx * by * bz, by * bz, by * bz, (bx + 2) * bz, (bx + 2) * bz] * 2


def block_layout(bx, by, bz):
    coords = []
    for z_of in ([z + 1 for z in range(bz)], [bz + 1 if z == 0 else 0 for z in range(bz)]):
        coords.append([(x + 1, y + 1, z) for x in range(bx) for y in range(by) for z in z_of])
        for x in (0, bx + 1):
            coords.append([(x, y + 1, z) for y in range(by) for z in z_of])
        for y in (0, by + 1):
            coords.append([(x, y, z) for x in range(bx + 2) for z in z_of])
    return coords


def work_tables(bx, by, bz):
    groups = block_layout(bx, by, bz)
    place = {}
    count = [0, 0, 0]
    for g, group in enumerate(groups):
        for c in group:
            place[c] = (group_set[g], count[group_set[g]])
            count[group_set[g]] += 1
    codes = np.zeros((8, count[0] * code_total), np.float32)
    for a, at in enumerate(groups[0]):
        for code, o in enumerate(stencil_table):
            which, b = place[tuple(at[d] + o[d] for d in range(3))]
            k = a * code_total + code
            codes[:2, k] = a, b
            codes[(2, 4, 5)[which], k] = 1.0
            codes[3, k] = which == 0 and code > 0
    inbound = []
    for which in (1, 2):
        found = []
        for at, (at_set, h) in place.items():
            for code, o in enumerate(stencil_table):
                to, b = place.get(tuple(at[d] + o[d] for d in range(3)), (3, 0))
                if at_set == which and to == 0 and code:
                    found.append((b, h, code))
        size = -(-(len(found) + 1) // 16) * 16
        ranks = np.zeros((size, (code_total - 1) * count[which]), np.float32)
        ends = np.zeros((8, size), np.float32)
        for k, (b, h, code) in enumerate(found):
            at = (code - 1) * count[which] + h
            ranks[k + 1 : len(found), at] = ranks[size - 1, at] = 1.0
            ranks[k, at] = mark
            ends[:2, k] = b, h
        inbound += [ranks, ends]
    return [codes, *inbound]


def position(group, rows, bx, by, bz):
    row = lax.broadcasted_iota(jnp.int32, (rows, lanes), 0)
    z = row % bz
    line = row // bz
    kind = group % 5
    if kind == 0:
        x, y = line // by + 1, line % by + 1
    elif kind <= 2:
        x, y = jnp.full_like(row, 0 if kind == 1 else bx + 1), line + 1
    else:
        x, y = line, jnp.full_like(row, 0 if kind == 3 else by + 1)
    if group < 5:
        z = z + 1
    else:
        z = jnp.where(z == 0, bz + 1, 0)
    sides = (bx + 1, by + 1, bz + 1)
    return [v.astype(f32) - 0.5 * side for v, side in zip((x, y, z), sides)]


def moment_rows(b, l):
    zz = b[2] * l[2]
    return [
        b[0] * l[1],
        b[0] * l[2],
        b[1] * l[0],
        b[1] * l[2],
        b[2] * l[0],
        b[2] * l[1],
        b[0] * l[0] - zz,
        b[1] * l[1] - zz,
    ]


def cross_rows(q, b, l):
    c = [q[1] * b[2] - q[2] * b[1], q[2] * b[0] - q[0] * b[2], q[0] * b[1] - q[1] * b[0]]
    return [
        2.0 * c[0] * l[0],
        2.0 * c[1] * l[1],
        2.0 * c[2] * l[2],
        c[0] * l[1] + c[1] * l[0],
        c[0] * l[2] + c[2] * l[0],
        c[1] * l[2] + c[2] * l[1],
    ]


def turn_rows(r, m):
    return [
        2.0 * (r[1] * m[4] - r[2] * m[2]),
        2.0 * (r[2] * m[0] - r[0] * m[5]),
        2.0 * (r[0] * m[3] - r[1] * m[1]),
        r[1] * m[5] - r[0] * m[4] + r[2] * (m[6] - m[7]),
        r[0] * m[2] - r[2] * m[3] - r[1] * m[6],
        r[2] * m[1] + r[0] * m[7] - r[1] * m[0],
    ]


def pieces(value):
    first = value.astype(bf16).astype(f32)
    rest = value - first
    second = rest.astype(bf16).astype(f32)
    return first, second, rest - second


def distance_rows(q):
    near = q[0] * q[0] + q[1] * q[1] + q[2] * q[2]
    one = jnp.ones_like(near)
    left, right = [], []
    for axis in q:
        p1, p2, p3 = pieces(axis)
        left += [p1, p1, p2, p2, p1, p3]
        right += [-2.0 * v for v in (p1, p2, p1, p2, p3, p1)]
    left += [*pieces(near), one, one, one]
    right += [one, one, one, *pieces(near + core_square)]
    return left, right


def pack_kernel(sizes, axes, count, fill_h, offsets_h, burgers_h, line_h, pairs_h, *refs):
    bx, by, bz, cells = sizes
    total, face = bx * by * bz, by * bz
    tables_h, (own, face_lo, face_hi, mom, pairs), tables = refs[:5], refs[5:10], refs[10:15]
    fill, offsets, burgers, line, level, sems = refs[15:]
    table_copies = [
        pltpu.make_async_copy(u, v, sems.at[5 + k]) for k, (u, v) in enumerate(zip(tables_h, tables))
    ]
    moves = ((fill_h, fill), (pairs_h, pairs), (burgers_h, burgers), (line_h, line), (offsets_h, offsets))
    copies = [pltpu.make_async_copy(u, v, sems.at[k]) for k, (u, v) in enumerate(moves)]
    for copy in copies + table_copies:
        copy.start()
    for copy in copies:
        copy.wait()
    for x in range(bx):
        for y in range(by):
            column = jnp.broadcast_to(fill[x][:, y : y + 1], (bz, lanes))
            level[x * face + y * bz : x * face + (y + 1) * bz, :] = column
    live = lax.broadcasted_iota(jnp.int32, (total, lanes), 1) < level[...]
    b, l = [], []
    for d in range(3):
        own[d] = offsets[d]
        b.append(jnp.where(live, burgers[d], 0.0))
        l.append(jnp.where(live, line[d], 0.0))
        own[3 + d] = b[d]
        own[6 + d] = l[d]
    entries = pairs.shape[1]
    code = pairs[...]
    block_no = code // code_total
    code_no = code - block_no * code_total
    alive = lax.broadcasted_iota(jnp.int32, (1, entries), 1) < count[0]
    of_block = lax.broadcasted_iota(jnp.int32, (total, entries), 0) == block_no
    of_code = lax.broadcasted_iota(jnp.int32, (lanes, entries), 0) == code_no
    own[9] = lax.dot_general(
        jnp.where(of_block & alive, 1.0, 0.0).astype(bf16),
        jnp.where(of_code, 1.0, 0.0).astype(bf16),
        (((1,), (1,)), ((), ())),
        preferred_element_type=f32,
    )
    cx, cy, cz = bx // 2, by // 2, bz // 2
    here = lax.axis_index(axes[0])
    for axis in axes[1:]:
        here = here * lax.axis_size(axis) + lax.axis_index(axis)
    first_lane = here * (cx * cy * cz)
    wide = lax.broadcasted_iota(jnp.int32, (face, lanes), 1)
    deep = lax.broadcasted_iota(jnp.int32, (face, lanes), 0)
    local = deep // (2 * bz) * cz + deep % bz // 2
    sums = []
    for feature in moment_rows(b, l):
        column = []
        for x in range(cx):
            both = feature[2 * x * face : (2 * x + 1) * face] + feature[(2 * x + 1) * face : (2 * x + 2) * face]
            column.append(jnp.sum(both, 1, keepdims=True))
        sums.append(column)
    for chunk in range(cells // lanes):
        for f, column in enumerate(sums):
            placed = jnp.zeros((face, lanes), f32)
            for x in range(cx):
                lane_of = first_lane + x * cy * cz + local - chunk * lanes
                placed = placed + jnp.where(wide == lane_of, column[x], 0.0)
            mom[chunk * 8 + f : chunk * 8 + f + 1, :] = jnp.sum(placed, 0, keepdims=True)
    for d in range(parts_sent):
        face_lo[d * face : (d + 1) * face] = own[d, 0:face]
        face_hi[d * face : (d + 1) * face] = own[d, total - face : total]
    face_lo[parts_sent * face :] = mom[...]
    face_hi[parts_sent * face :] = mom[...]
    for copy in table_copies:
        copy.wait()


def rim_kernel(sizes, both_ways, own, mom, x_lo, x_hi, *refs):
    bx, by, bz, _ = sizes
    face = by * bz
    (face_lo, face_hi, x_all, mom_x), more = refs[-4:], refs[1:-4]
    for y, out in ((0, face_lo), (by - 1, face_hi)):
        for d in range(parts_sent):
            to, at = d * (bx + 2) * bz, y * bz
            for x in range(bx + 2):
                if x == 0 or x == bx + 1:
                    start = d * face + at
                    rows = (x_lo if x == 0 else x_hi)[start : start + bz]
                else:
                    start = (x - 1) * face + at
                    rows = own[d, start : start + bz]
                out[to + x * bz : to + (x + 1) * bz] = rows
    total = bx * by * bz
    for d in range(parts_sent):
        x_all[d * total : (d + 1) * total] = own[d]
    start = parts_sent * total
    for v in (x_lo, x_hi):
        x_all[start : start + v.shape[0]] = v[...]
        start += v.shape[0]
    head = parts_sent * face
    total = mom[...] + x_lo[head:]
    if both_ways:
        total = total + x_hi[head:]
    for v in more:
        total = total + v[...]
    mom_x[...] = total
    head = parts_sent * (bx + 2) * bz
    face_lo[head:] = total
    face_hi[head:] = total


def shape_blocks(sizes, sources, stage, right, weighed, left=None):
    bx, by, bz, _ = sizes
    heights = group_heights(bx, by, bz)
    base = 0
    for group, part in sources:
        h = heights[group]
        zero = jnp.zeros((h, lanes), f32)
        place = position(group, h, bx, by, bz)
        q = [part(d) + place[d] for d in range(3)]
        b = [part(3 + d) for d in range(3)]
        l = [part(6 + d) for d in range(3)]
        rows = moment_rows(b, l) + cross_rows(q, b, l)
        lhs, rhs = distance_rows(q)
        rows = rows + [zero] * (16 - len(rows)) + rhs + [zero] * (32 - len(rhs))
        if left is not None:
            rows = rows + lhs + [zero] * (32 - len(lhs))
        for f, value in enumerate(rows):
            stage[pl.ds(base * 80 + f, h, stride=80), :] = value
        base += h

    def shape_block(block, carry):
        at = pl.multiple_of(block * 80, 16)
        product = stage[pl.ds(at, 16), :]
        high = product.astype(bf16)
        low = (product - high.astype(f32)).astype(bf16)
        weighed[block, 0:16, 0:lanes] = high
        weighed[block, 0:16, lanes : 2 * lanes] = high
        weighed[block, 16:32, 0:lanes] = low
        weighed[block, 16:32, lanes : 2 * lanes] = jnp.zeros_like(low)
        right[block] = stage[pl.ds(at + 16, 32), :].astype(bf16)
        if left is not None:
            left[block] = stage[pl.ds(at + 48, 32), :].astype(bf16)
        return carry

    lax.fori_loop(0, base, shape_block, 0, unroll=8)


def rows_of(ref, start, height):
    return lambda d: ref[start + d * height : start + (d + 1) * height, :]


def ranked(size):
    down = lax.broadcasted_iota(jnp.int32, (size, size), 0)
    across = lax.broadcasted_iota(jnp.int32, (size, size), 1)
    return jnp.where(down > across, 1.0, jnp.where(down == across, mark, 0.0)).astype(bf16)


def spread(rank, fields, chunks):
    lane = lax.broadcasted_iota(jnp.int32, rank.shape, 1).astype(f32) + mark
    hot = [jnp.where(rank == lane + float(m * lanes), 1.0, 0.0).astype(bf16) for m in range(chunks)]
    return jnp.dot(fields, jnp.concatenate(hot, 1), preferred_element_type=f32)


def put_list(rows, start, low, high, number, spare):
    for m in range(low.shape[1] // lanes):
        lane = lax.broadcasted_iota(jnp.int32, (1, lanes), 1) + m * lanes
        part = slice(m * lanes, (m + 1) * lanes)
        value = (low[:, part] + 256.0 * high[:, part]).astype(jnp.int32)
        rows[start + m : start + m + 1, :] = jnp.where(lane < number, value, spare)


def own_kernel(sizes, codes_of, pairs, count, own, right, weighed, left, todo, stage, rows, sem):
    bx, by, bz, _ = sizes
    total = bx * by * bz
    entries = pairs.shape[1]
    code = lax.broadcasted_iota(jnp.int32, (total * code_total, entries), 0)
    hot = jnp.where(code == pairs[...], 1.0, 0.0).astype(bf16)
    fields = jnp.dot(codes_of[...], hot, preferred_element_type=f32)
    alive = lax.broadcasted_iota(jnp.int32, (1, entries), 1) < count[0]
    marks = [jnp.where(alive, fields[k : k + 1], 0.0) for k in range(2, 6)]
    tall = jnp.concatenate([jnp.broadcast_to(v, (lanes, entries)) for v in marks], 0).astype(bf16)
    ranks = lax.dot_general(
        ranked(entries), tall, (((1,), (1,)), ((), ())), preferred_element_type=f32
    )
    ends = fields.astype(bf16)
    rows[...] = jnp.zeros_like(rows)
    lane = lax.broadcasted_iota(jnp.int32, (1, lanes), 1)
    numbers = jnp.zeros((1, lanes), jnp.int32)
    for k in range(4):
        both = spread(ranks[:, k * lanes : (k + 1) * lanes], ends, 2)
        number = jnp.sum(marks[k], 1, keepdims=True).astype(jnp.int32)
        low, high = (both[1:2], both[0:1]) if k == 1 else (both[0:1], both[1:2])
        put_list(rows, 2 * k, low, high, number, total)
        numbers = jnp.where(lane == k, number, numbers)
    rows[8:9, :] = numbers
    copy = pltpu.make_async_copy(rows, todo, sem)
    copy.start()
    shape_blocks(sizes, [(0, lambda d: own[d])], stage, right, weighed, left)
    left[total] = left[0]
    copy.wait()


def list_inbound(ranks_of, ends_of, sources, flags, rows, spare):
    base = 0
    for _, part in sources:
        height = part(9).shape[0]
        flags[base : base + height, :] = part(9)
        base += height
    by_code = [jnp.broadcast_to(flags[:, c : c + 1], (base, lanes)) for c in range(1, code_total)]
    tall = jnp.concatenate(by_code, 0).astype(bf16)
    rank = jnp.dot(ranks_of[...], tall, preferred_element_type=f32)
    both = spread(rank, ends_of[...], 2)
    number = rank[rank.shape[0] - 1 :, :].astype(jnp.int32)
    rows[...] = jnp.zeros_like(rows)
    put_list(rows, 0, both[0:1], both[1:2], number, spare)
    rows[2:3, :] = number


def add_step(lookup, start, width, right, weighed, left, acc):
    results = []
    for k in range(width):
        entry = lookup(start + k)
        row, col = entry & 255, entry >> 8
        square = lax.dot_general(
            right[col], left[row], (((0,), (0,)), ((), ())), preferred_element_type=f32
        )
        root = lax.rsqrt(square)
        weight = root * root * root
        high = weight.astype(bf16)
        low = (weight - high.astype(f32)).astype(bf16)
        both = jnp.dot(weighed[col], jnp.concatenate([high, low], 0), preferred_element_type=f32)
        results.append((row, both[0:16] + both[16:32]))
    for row, value in results:
        at_row = pl.ds(pl.multiple_of(row * 16, 16), 16)
        acc[at_row, :] += value


def interact(lookup, start, end, *refs):
    number = end - start
    steps = (number + unroll - 1 - short_steps[-1]) // unroll
    done = start + steps * unroll

    def whole(at, carry):
        add_step(lookup, start + at * unroll, unroll, *refs)
        return carry

    lax.fori_loop(0, steps, whole, 0)
    left_over = end - done
    least = 0
    for width in short_steps:

        @pl.when((left_over > least) & (left_over <= width))
        def _():
            add_step(lookup, done, width, *refs)

        least = width


def near_list(todo):
    n = todo[8, 0]
    number = n + todo[8, 1]
    return joined(todo, 0, n, todo, 2), jnp.minimum(number, first_share), number


def near_kernel(todo, right, weighed, left, acc):
    acc[...] = jnp.zeros_like(acc)
    lookup, middle, _ = near_list(todo)
    interact(lookup, 0, middle, right, weighed, left, acc)


def listed(rows, start):
    return lambda at: rows[start + (at >> 7), at & 127]


def joined(rows, start, number, more, then_start):
    first, then = listed(rows, start), listed(more, then_start)
    return lambda at: jnp.where(at < number, first(at), then(jnp.maximum(at - number, 0)))


def side_sources(sizes, groups, here, beside):
    bx, by, bz, cells = sizes
    heights = group_heights(bx, by, bz)
    mom_rows = 8 * cells // lanes
    x_start = parts_sent * heights[0]
    starts = {0: 0, 1: x_start, 2: x_start + parts_sent * heights[1] + mom_rows, 4: 0, 3: parts_sent * heights[3] + mom_rows}
    return [(g, rows_of((here, beside)[g >= 5], starts[g % 5], heights[g])) for g in groups]


def mid_kernel(sizes, ranks_of, ends_of, x_all, p_x_all, mom_in, todo, right, weighed, left, *refs):
    bx, by, bz, _ = sizes
    right_1, weighed_1, found, mom_out, acc, stage, flags, rows, sem = refs[-9:]
    sources = side_sources(sizes, set_groups(1), x_all, p_x_all)
    list_inbound(ranks_of, ends_of, sources, flags, rows, bx * by * bz)
    copy = pltpu.make_async_copy(rows, found, sem)
    copy.start()
    mom_out[...] = mom_in[...]
    shape_blocks(sizes, sources, stage, right_1, weighed_1)
    acc[...] = jnp.zeros_like(acc)
    lookup, middle, number = near_list(todo)
    interact(lookup, middle, number, right, weighed, left, acc)
    copy.wait()


def side_kernel(todo, found, right, weighed, left, _, acc):
    acc[...] = jnp.zeros_like(acc)
    n = todo[8, 2]
    interact(joined(todo, 4, n, found, 0), 0, n + found[2, 0], right, weighed, left, acc)


def coarse_place(sizes, axes, chunk):
    bx, by, bz, _ = sizes
    coarse = (bx // 2, by // 2, bz // 2)
    number = lax.broadcasted_iota(jnp.int32, (1, lanes), 1) + chunk * lanes
    places = []
    for d in (2, 1, 0):
        places.append(number % coarse[d])
        number = number // coarse[d]
    for k, d in enumerate((2, 1, 0)):
        size = lax.axis_size(axes[d])
        places[k] = places[k] + number % size * coarse[d]
        number = number // size
    return places[::-1]


def close_kernel(sizes, axes, grid, moments, todo, ranks_of, ends_of, y_both, p_y_both, left, acc_a, acc_b, acc_c, own, *refs):
    bx, by, bz, cells = sizes
    total, face = bx * by * bz, by * bz
    mom_parts = refs[:-9]
    out, right, weighed, stage, acc, flags, rows, found, sem = refs[-9:]
    sources = side_sources(sizes, set_groups(2), y_both, p_y_both)
    list_inbound(ranks_of, ends_of, sources, flags, rows, total)
    copy = pltpu.make_async_copy(rows, found, sem)
    copy.start()
    shape_blocks(sizes, sources, stage, right, weighed)
    acc[...] = acc_a[...] + acc_b[...] + acc_c[...]
    copy.wait()
    n = todo[8, 3]
    interact(joined(todo, 6, n, found, 0), 0, n + found[2, 0], right, weighed, left, acc)
    mom = moments(y_both, p_y_both, mom_parts)

    cx, cy, cz = bx // 2, by // 2, bz // 2
    deep = lax.broadcasted_iota(jnp.int32, (face, lanes), 0)
    local = (None, deep // (2 * bz), deep % bz // 2)
    far = [[] for _ in range(6)]
    for x in range(cx):
        totals = [jnp.zeros((face, lanes), f32)] * 6
        for chunk in range(cells // lanes):
            lengths = []
            cell_of = coarse_place(sizes, axes, chunk)
            for d, axis in enumerate(axes):
                at = lax.axis_index(axis) * (cx, cy, cz)[d] + (x if d == 0 else local[d])
                delta = at - cell_of[d]
                half = grid[d] // 2
                delta = jnp.where(delta >= grid[d] - half, delta - grid[d], delta)
                delta = jnp.where(delta < -half, delta + grid[d], delta)
                lengths.append(2.0 * delta.astype(f32))
            radius = lengths[0] * lengths[0] + lengths[1] * lengths[1] + lengths[2] * lengths[2]
            root = lax.rsqrt(radius + core_square)
            weight = jnp.where(radius == 0.0, 0.0, root * root * root)
            m = [mom[chunk * 8 + f : chunk * 8 + f + 1] for f in range(8)]
            turned = turn_rows([weight * v for v in lengths], m)
            totals = [t + v for t, v in zip(totals, turned)]
        for f in range(6):
            far[f].append(jnp.sum(totals[f], 1, keepdims=True))

    place = position(0, total, bx, by, bz)
    p = [own[d] + place[d] for d in range(3)]
    b = [own[3 + d] for d in range(3)]
    l = [own[6 + d] for d in range(3)]
    moment = [acc[pl.ds(f, total, stride=16), :] for f in range(8)]
    crossed = [acc[pl.ds(8 + f, total, stride=16), :] for f in range(6)]
    turned = turn_rows(p, moment)
    s = []
    for f in range(6):
        column = jnp.concatenate([far[f][x // 2] for x in range(bx)], 0)
        s.append(turned[f] - crossed[f] + column)
    push = [
        s[0] * b[0] + s[3] * b[1] + s[4] * b[2],
        s[3] * b[0] + s[1] * b[1] + s[5] * b[2],
        s[4] * b[0] + s[5] * b[1] + s[2] * b[2],
    ]
    out[0] = kernel_scale * (push[1] * l[2] - push[2] * l[1])
    out[1] = kernel_scale * (push[2] * l[0] - push[0] * l[2])
    out[2] = kernel_scale * (push[0] * l[1] - push[1] * l[0])


def shifted(value, axis, step):
    size = lax.axis_size(axis)
    return lax.ppermute(value, axis, [(i, (i + step) % size) for i in range(size)])


def ring_sum(value, axis):
    total = value
    for step in range(1, lax.axis_size(axis)):
        total = total + shifted(value, axis, step)
    return total


def beside_z(value, layers):
    size = lax.axis_size("gz")
    if size == 2:
        return shifted(value, "gz", 1)
    head = value.shape
    split = value.reshape(-1, layers, lanes)
    above = shifted(split[:, :1], "gz", -1)
    below = shifted(split[:, layers - 1 :], "gz", 1)
    middle = split[:, 1 : layers - 1]
    return jnp.concatenate([above, middle, below], 1).reshape(head)


def body(offsets, burgers, line, block_fill, near_pairs, pair_count):
    _, bx, by, bz, slots = offsets.shape
    axes = ("gx", "gy", "gz")
    sizes = [lax.axis_size(axis) for axis in axes]
    heights = group_heights(bx, by, bz)
    own, face, rim = heights[0], heights[1], heights[3]
    set_size = [sum(heights[g] for g in set_groups(which)) for which in range(3)]
    coarse = (bx // 2, by // 2, bz // 2)
    grid = tuple(c * n for c, n in zip(coarse, sizes))
    per_device = coarse[0] * coarse[1] * coarse[2]
    cells = per_device * sizes[0] * sizes[1] * sizes[2]
    mom_rows = 8 * cells // lanes
    kinds = (bx, by, bz, cells)
    entries = near_pairs.shape[0]
    vmem = pl.BlockSpec(memory_space=pltpu.VMEM)
    smem = pl.BlockSpec(memory_space=pltpu.SMEM)
    hbm = pl.BlockSpec(memory_space=pltpu.HBM)
    anywhere = pl.BlockSpec(memory_space=pl.ANY)
    shape = jax.ShapeDtypeStruct
    flat = lambda v: v.reshape(3, own, slots)
    far = lambda v: pltpu.with_memory_space_constraint(v, pltpu.HBM)

    tables = [jnp.asarray(v.astype(bf16)) for v in work_tables(bx, by, bz)]
    assert max(entries, tables[1].shape[0], tables[3].shape[0]) + unroll <= 2 * lanes

    def call(kernel, out_shape, in_specs, out_specs, scratch, name, cost, limit=12):
        return pl.pallas_call(
            kernel,
            out_shape=out_shape,
            in_specs=in_specs,
            out_specs=out_specs,
            scratch_shapes=scratch,
            compiler_params=pltpu.CompilerParams(vmem_limit_bytes=limit * 2**20),
            cost_estimate=pl.CostEstimate(flops=cost, bytes_accessed=cost, transcendentals=0),
            name=name,
        )

    face_shape = shape((parts_sent * face + mom_rows, lanes), f32)
    rim_shape = shape((parts_sent * rim + mom_rows, lanes), f32)
    mom_shape = shape((mom_rows, lanes), f32)
    acc_shape = shape(((own + 1) * 16, lanes), f32)
    mine, face_lo, face_hi, mom, pairs, codes_of, *inbound = call(
        functools.partial(pack_kernel, kinds, axes),
        [
            shape((parts_sent, own, lanes), f32),
            face_shape,
            face_shape,
            mom_shape,
            shape((1, entries), jnp.int32),
            *[shape(v.shape, v.dtype) for v in tables],
        ],
        [smem] + [hbm] * 10,
        [vmem] * 10,
        [
            pltpu.VMEM((bx, bz, by), jnp.int32),
            pltpu.VMEM((3, own, lanes), f32),
            pltpu.VMEM((3, own, lanes), f32),
            pltpu.VMEM((3, own, lanes), f32),
            pltpu.VMEM((own, lanes), jnp.int32),
            pltpu.SemaphoreType.DMA((10,)),
        ],
        "pack",
        10**6,
    )(
        pair_count,
        far(jnp.transpose(block_fill, (0, 2, 1))),
        far(flat(offsets)),
        far(flat(burgers)),
        far(flat(line)),
        far(near_pairs.reshape(1, -1)),
        *[far(v) for v in tables],
    )

    x_far = [shifted(mom, "gx", step) for step in range(2, sizes[0] - 1)]
    x_lo = shifted(face_hi, "gx", 1)
    x_hi = shifted(face_lo, "gx", -1)
    right, weighed, left, todo = call(
        functools.partial(own_kernel, kinds),
        [
            shape((own, 32, lanes), bf16),
            shape((own, 32, 2 * lanes), bf16),
            shape((own + 1, 32, lanes), bf16),
            pltpu.SMEM((16, lanes), jnp.int32),
        ],
        [vmem, vmem, smem, vmem],
        [vmem, vmem, vmem, smem],
        [
            pltpu.VMEM((own * 80, lanes), f32),
            pltpu.VMEM((16, lanes), jnp.int32),
            pltpu.SemaphoreType.DMA,
        ],
        "own",
        10**7,
    )(codes_of, pairs, pair_count, mine)
    acc_a = call(
        near_kernel,
        acc_shape,
        [smem, vmem, vmem, vmem],
        vmem,
        [],
        "near",
        10**7,
    )(todo, right, weighed, left)
    side_lo, side_hi, x_all, mom_x = call(
        functools.partial(rim_kernel, kinds, sizes[0] > 2),
        [
            rim_shape,
            rim_shape,
            shape((parts_sent * (own + 2 * face) + 2 * mom_rows, lanes), f32),
            mom_shape,
        ],
        [vmem] * 4 + [anywhere] + [vmem] * len(x_far),
        [vmem] * 4,
        [],
        "rim",
        10**6,
    )(mine, mom, x_lo, x_hi, acc_a, *x_far)
    y_lo = shifted(side_hi, "gy", 1)
    y_hi = shifted(side_lo, "gy", -1)
    y_far = [shifted(mom_x, "gy", step) for step in range(2, sizes[1] - 1)]
    p_x_all = beside_z(x_all, bz)
    right_1, weighed_1, found, mom_kept, acc_b = call(
        functools.partial(mid_kernel, kinds),
        [
            shape((set_size[1], 32, lanes), bf16),
            shape((set_size[1], 32, 2 * lanes), bf16),
            pltpu.SMEM((8, lanes), jnp.int32),
            mom_shape,
            acc_shape,
        ],
        [vmem] * 5 + [smem, vmem, vmem, vmem, anywhere, anywhere],
        [vmem, vmem, smem, vmem, vmem],
        [
            pltpu.VMEM((set_size[1] * 80, lanes), f32),
            pltpu.VMEM((set_size[1], lanes), f32),
            pltpu.VMEM((8, lanes), jnp.int32),
            pltpu.SemaphoreType.DMA,
        ],
        "mid",
        10**7,
    )(*inbound[:2], x_all, p_x_all, mom_x, todo, right, weighed, left, side_lo, side_hi)
    for v in y_far:
        mom_kept = mom_kept + v
    y_both = jnp.concatenate([y_hi, y_lo, mom_kept], 0)
    p_y_both = beside_z(y_both, bz)

    acc_c = call(
        side_kernel,
        acc_shape,
        [smem, smem, vmem, vmem, vmem, anywhere],
        vmem,
        [],
        "side",
        10**7,
    )(todo, found, right_1, weighed_1, left, y_both)
    tail = parts_sent * rim
    if sizes[2] == 2:
        mom_parts = []

        def moments(y_both, p_y_both, parts):
            spans = [slice(tail, tail + mom_rows)]
            if sizes[1] > 2:
                spans.append(slice(2 * tail + mom_rows, 2 * (tail + mom_rows)))
            spans.append(slice(2 * (tail + mom_rows), 2 * tail + 3 * mom_rows))
            return sum(y_both[span] + p_y_both[span] for span in spans)

    else:
        mom_parts = [ring_sum(mom_kept + y_lo[tail:] + y_hi[tail:], "gz")]
        moments = lambda y_both, p_y_both, parts: parts[0][...]

    forces = call(
        functools.partial(close_kernel, kinds, axes, grid, moments),
        shape((3, own, lanes), f32),
        [smem] + [vmem] * (9 + len(mom_parts)),
        vmem,
        [
            pltpu.VMEM((set_size[2], 32, lanes), bf16),
            pltpu.VMEM((set_size[2], 32, 2 * lanes), bf16),
            pltpu.VMEM((set_size[2] * 80, lanes), f32),
            pltpu.VMEM(((own + 1) * 16, lanes), f32),
            pltpu.VMEM((set_size[2], lanes), f32),
            pltpu.VMEM((8, lanes), jnp.int32),
            pltpu.SMEM((8, lanes), jnp.int32),
            pltpu.SemaphoreType.DMA,
        ],
        "close",
        10**7,
    )(todo, *inbound[2:], y_both, p_y_both, left, acc_a, acc_b, acc_c, mine, *mom_parts)
    return forces.reshape(3, bx, by, bz, slots)


def solution(mesh):
    in_specs = (
        P(None, "gx", "gy", "gz", None),
        P(None, "gx", "gy", "gz", None),
        P(None, "gx", "gy", "gz", None),
        P("gx", "gy", "gz"),
        P(("gx", "gy", "gz")),
        P(("gx", "gy", "gz")),
    )
    out_specs = P(None, "gx", "gy", "gz", None)
    return jax.shard_map(body, mesh=mesh, in_specs=in_specs, out_specs=out_specs, check_vma=False)
```

```python
import functools
import math

import jax
import jax.numpy as jnp
import numpy as np
from jax import lax
from jax.experimental import pallas as pl
from jax.experimental.pallas import tpu as pltpu
from jax.sharding import PartitionSpec as P

stencil_table = (
    (0, 0, 0),
    (1, 0, 0),
    (0, 1, 0),
    (0, 0, 1),
    (1, 1, 0),
    (-1, 1, 0),
    (1, 0, 1),
    (1, 0, -1),
    (0, 1, 1),
    (0, -1, 1),
    (1, 1, -1),
    (1, -1, 1),
    (-1, 1, 1),
    (1, 1, 1),
)
code_total = len(stencil_table)
kernel_scale = 1.0 / (8.0 * math.pi)
core_square = 0.09
lanes = 128
mark = 2048.0
parts_sent = 10
unroll = 64
short_steps = (16, 32, 48)
first_share = 96
f32 = jnp.float32
bf16 = jnp.bfloat16


group_set = (0, 1, 1, 2, 2, 1, 1, 1, 2, 2)


def set_groups(which):
    return [g for g in range(10) if group_set[g] == which]


def group_heights(bx, by, bz):
    return [bx * by * bz, by * bz, by * bz, (bx + 2) * bz, (bx + 2) * bz] * 2


def block_layout(bx, by, bz):
    coords = []
    for z_of in ([z + 1 for z in range(bz)], [bz + 1 if z == 0 else 0 for z in range(bz)]):
        coords.append([(x + 1, y + 1, z) for x in range(bx) for y in range(by) for z in z_of])
        for x in (0, bx + 1):
            coords.append([(x, y + 1, z) for y in range(by) for z in z_of])
        for y in (0, by + 1):
            coords.append([(x, y, z) for x in range(bx + 2) for z in z_of])
    return coords


def work_tables(bx, by, bz):
    groups = block_layout(bx, by, bz)
    place = {}
    count = [0, 0, 0]
    for g, group in enumerate(groups):
        for c in group:
            place[c] = (group_set[g], count[group_set[g]])
            count[group_set[g]] += 1
    codes = np.zeros((8, count[0] * code_total), np.float32)
    for a, at in enumerate(groups[0]):
        for code, o in enumerate(stencil_table):
            which, b = place[tuple(at[d] + o[d] for d in range(3))]
            k = a * code_total + code
            codes[:2, k] = a, b
            codes[(2, 4, 5)[which], k] = 1.0
            codes[3, k] = which == 0 and code > 0
    inbound = []
    for which in (1, 2):
        found = []
        for at, (at_set, h) in place.items():
            for code, o in enumerate(stencil_table):
                to, b = place.get(tuple(at[d] + o[d] for d in range(3)), (3, 0))
                if at_set == which and to == 0 and code:
                    found.append((b, h, code))
        size = -(-(len(found) + 1) // 16) * 16
        ranks = np.zeros((size, (code_total - 1) * count[which]), np.float32)
        ends = np.zeros((8, size), np.float32)
        for k, (b, h, code) in enumerate(found):
            at = (code - 1) * count[which] + h
            ranks[k + 1 : len(found), at] = ranks[size - 1, at] = 1.0
            ranks[k, at] = mark
            ends[:2, k] = b, h
        inbound += [ranks, ends]
    return [codes, *inbound]


def position(group, rows, bx, by, bz):
    row = lax.broadcasted_iota(jnp.int32, (rows, lanes), 0)
    z = row % bz
    line = row // bz
    kind = group % 5
    if kind == 0:
        x, y = line // by + 1, line % by + 1
    elif kind <= 2:
        x, y = jnp.full_like(row, 0 if kind == 1 else bx + 1), line + 1
    else:
        x, y = line, jnp.full_like(row, 0 if kind == 3 else by + 1)
    if group < 5:
        z = z + 1
    else:
        z = jnp.where(z == 0, bz + 1, 0)
    sides = (bx + 1, by + 1, bz + 1)
    return [v.astype(f32) - 0.5 * side for v, side in zip((x, y, z), sides)]


def moment_rows(b, l):
    zz = b[2] * l[2]
    return [
        b[0] * l[1],
        b[0] * l[2],
        b[1] * l[0],
        b[1] * l[2],
        b[2] * l[0],
        b[2] * l[1],
        b[0] * l[0] - zz,
        b[1] * l[1] - zz,
    ]


def cross_rows(q, b, l):
    c = [q[1] * b[2] - q[2] * b[1], q[2] * b[0] - q[0] * b[2], q[0] * b[1] - q[1] * b[0]]
    return [
        2.0 * c[0] * l[0],
        2.0 * c[1] * l[1],
        2.0 * c[2] * l[2],
        c[0] * l[1] + c[1] * l[0],
        c[0] * l[2] + c[2] * l[0],
        c[1] * l[2] + c[2] * l[1],
    ]


def turn_rows(r, m):
    return [
        2.0 * (r[1] * m[4] - r[2] * m[2]),
        2.0 * (r[2] * m[0] - r[0] * m[5]),
        2.0 * (r[0] * m[3] - r[1] * m[1]),
        r[1] * m[5] - r[0] * m[4] + r[2] * (m[6] - m[7]),
        r[0] * m[2] - r[2] * m[3] - r[1] * m[6],
        r[2] * m[1] + r[0] * m[7] - r[1] * m[0],
    ]


def pieces(value):
    first = value.astype(bf16).astype(f32)
    rest = value - first
    second = rest.astype(bf16).astype(f32)
    return first, second, rest - second


def distance_rows(q):
    near = q[0] * q[0] + q[1] * q[1] + q[2] * q[2]
    one = jnp.ones_like(near)
    left, right = [], []
    for axis in q:
        p1, p2, p3 = pieces(axis)
        left += [p1, p1, p2, p2, p1, p3]
        right += [-2.0 * v for v in (p1, p2, p1, p2, p3, p1)]
    left += [*pieces(near), one, one, one]
    right += [one, one, one, *pieces(near + core_square)]
    return left, right


def pack_kernel(sizes, axes, count, fill_h, offsets_h, burgers_h, line_h, pairs_h, *refs):
    bx, by, bz, cells = sizes
    total, face = bx * by * bz, by * bz
    tables_h, (own, face_lo, face_hi, mom, pairs), tables = refs[:5], refs[5:10], refs[10:15]
    fill, offsets, burgers, line, level, sems = refs[15:]
    table_copies = [
        pltpu.make_async_copy(u, v, sems.at[5 + k]) for k, (u, v) in enumerate(zip(tables_h, tables))
    ]
    moves = ((fill_h, fill), (pairs_h, pairs), (burgers_h, burgers), (line_h, line), (offsets_h, offsets))
    copies = [pltpu.make_async_copy(u, v, sems.at[k]) for k, (u, v) in enumerate(moves)]
    for copy in copies + table_copies:
        copy.start()
    for copy in copies:
        copy.wait()
    for x in range(bx):
        for y in range(by):
            column = jnp.broadcast_to(fill[x][:, y : y + 1], (bz, lanes))
            level[x * face + y * bz : x * face + (y + 1) * bz, :] = column
    live = lax.broadcasted_iota(jnp.int32, (total, lanes), 1) < level[...]
    b, l = [], []
    for d in range(3):
        own[d] = offsets[d]
        b.append(jnp.where(live, burgers[d], 0.0))
        l.append(jnp.where(live, line[d], 0.0))
        own[3 + d] = b[d]
        own[6 + d] = l[d]
    entries = pairs.shape[1]
    code = pairs[...]
    block_no = code // code_total
    code_no = code - block_no * code_total
    alive = lax.broadcasted_iota(jnp.int32, (1, entries), 1) < count[0]
    of_block = lax.broadcasted_iota(jnp.int32, (total, entries), 0) == block_no
    of_code = lax.broadcasted_iota(jnp.int32, (lanes, entries), 0) == code_no
    own[9] = lax.dot_general(
        jnp.where(of_block & alive, 1.0, 0.0).astype(bf16),
        jnp.where(of_code, 1.0, 0.0).astype(bf16),
        (((1,), (1,)), ((), ())),
        preferred_element_type=f32,
    )
    cx, cy, cz = bx // 2, by // 2, bz // 2
    here = lax.axis_index(axes[0])
    for axis in axes[1:]:
        here = here * lax.axis_size(axis) + lax.axis_index(axis)
    first_lane = here * (cx * cy * cz)
    wide = lax.broadcasted_iota(jnp.int32, (face, lanes), 1)
    deep = lax.broadcasted_iota(jnp.int32, (face, lanes), 0)
    local = deep // (2 * bz) * cz + deep % bz // 2
    sums = []
    for feature in moment_rows(b, l):
        column = []
        for x in range(cx):
            both = feature[2 * x * face : (2 * x + 1) * face] + feature[(2 * x + 1) * face : (2 * x + 2) * face]
            column.append(jnp.sum(both, 1, keepdims=True))
        sums.append(column)
    for chunk in range(cells // lanes):
        for f, column in enumerate(sums):
            placed = jnp.zeros((face, lanes), f32)
            for x in range(cx):
                lane_of = first_lane + x * cy * cz + local - chunk * lanes
                placed = placed + jnp.where(wide == lane_of, column[x], 0.0)
            mom[chunk * 8 + f : chunk * 8 + f + 1, :] = jnp.sum(placed, 0, keepdims=True)
    for d in range(parts_sent):
        face_lo[d * face : (d + 1) * face] = own[d, 0:face]
        face_hi[d * face : (d + 1) * face] = own[d, total - face : total]
    face_lo[parts_sent * face :] = mom[...]
    face_hi[parts_sent * face :] = mom[...]
    for copy in table_copies:
        copy.wait()


def rim_kernel(sizes, both_ways, own, mom, x_lo, x_hi, *refs):
    bx, by, bz, _ = sizes
    face = by * bz
    (face_lo, face_hi, x_all, mom_x), more = refs[-4:], refs[1:-4]
    for y, out in ((0, face_lo), (by - 1, face_hi)):
        for d in range(parts_sent):
            to, at = d * (bx + 2) * bz, y * bz
            for x in range(bx + 2):
                if x == 0 or x == bx + 1:
                    start = d * face + at
                    rows = (x_lo if x == 0 else x_hi)[start : start + bz]
                else:
                    start = (x - 1) * face + at
                    rows = own[d, start : start + bz]
                out[to + x * bz : to + (x + 1) * bz] = rows
    total = bx * by * bz
    for d in range(parts_sent):
        x_all[d * total : (d + 1) * total] = own[d]
    start = parts_sent * total
    for v in (x_lo, x_hi):
        x_all[start : start + v.shape[0]] = v[...]
        start += v.shape[0]
    head = parts_sent * face
    total = mom[...] + x_lo[head:]
    if both_ways:
        total = total + x_hi[head:]
    for v in more:
        total = total + v[...]
    mom_x[...] = total
    head = parts_sent * (bx + 2) * bz
    face_lo[head:] = total
    face_hi[head:] = total


def shape_blocks(sizes, sources, stage, right, weighed, left=None):
    bx, by, bz, _ = sizes
    heights = group_heights(bx, by, bz)
    base = 0
    for group, part in sources:
        h = heights[group]
        zero = jnp.zeros((h, lanes), f32)
        place = position(group, h, bx, by, bz)
        q = [part(d) + place[d] for d in range(3)]
        b = [part(3 + d) for d in range(3)]
        l = [part(6 + d) for d in range(3)]
        rows = moment_rows(b, l) + cross_rows(q, b, l)
        lhs, rhs = distance_rows(q)
        rows = rows + [zero] * (16 - len(rows)) + rhs + [zero] * (32 - len(rhs))
        if left is not None:
            rows = rows + lhs + [zero] * (32 - len(lhs))
        for f, value in enumerate(rows):
            stage[pl.ds(base * 80 + f, h, stride=80), :] = value
        base += h

    def shape_block(block, carry):
        at = pl.multiple_of(block * 80, 16)
        product = stage[pl.ds(at, 16), :]
        high = product.astype(bf16)
        low = (product - high.astype(f32)).astype(bf16)
        weighed[block, 0:16, 0:lanes] = high
        weighed[block, 0:16, lanes : 2 * lanes] = high
        weighed[block, 16:32, 0:lanes] = low
        weighed[block, 16:32, lanes : 2 * lanes] = jnp.zeros_like(low)
        right[block] = stage[pl.ds(at + 16, 32), :].astype(bf16)
        if left is not None:
            left[block] = stage[pl.ds(at + 48, 32), :].astype(bf16)
        return carry

    lax.fori_loop(0, base, shape_block, 0, unroll=8)


def rows_of(ref, start, height):
    return lambda d: ref[start + d * height : start + (d + 1) * height, :]


def ranked(size):
    down = lax.broadcasted_iota(jnp.int32, (size, size), 0)
    across = lax.broadcasted_iota(jnp.int32, (size, size), 1)
    return jnp.where(down > across, 1.0, jnp.where(down == across, mark, 0.0)).astype(bf16)


def spread(rank, fields, chunks):
    lane = lax.broadcasted_iota(jnp.int32, rank.shape, 1).astype(f32) + mark
    hot = [jnp.where(rank == lane + float(m * lanes), 1.0, 0.0).astype(bf16) for m in range(chunks)]
    return jnp.dot(fields, jnp.concatenate(hot, 1), preferred_element_type=f32)


def put_list(rows, start, low, high, number, spare):
    for m in range(low.shape[1] // lanes):
        lane = lax.broadcasted_iota(jnp.int32, (1, lanes), 1) + m * lanes
        part = slice(m * lanes, (m + 1) * lanes)
        value = (low[:, part] + 256.0 * high[:, part]).astype(jnp.int32)
        rows[start + m : start + m + 1, :] = jnp.where(lane < number, value, spare)


def own_kernel(sizes, codes_of, pairs, count, own, right, weighed, left, todo, stage, rows, sem):
    bx, by, bz, _ = sizes
    total = bx * by * bz
    entries = pairs.shape[1]
    code = lax.broadcasted_iota(jnp.int32, (total * code_total, entries), 0)
    hot = jnp.where(code == pairs[...], 1.0, 0.0).astype(bf16)
    fields = jnp.dot(codes_of[...], hot, preferred_element_type=f32)
    alive = lax.broadcasted_iota(jnp.int32, (1, entries), 1) < count[0]
    marks = [jnp.where(alive, fields[k : k + 1], 0.0) for k in range(2, 6)]
    tall = jnp.concatenate([jnp.broadcast_to(v, (lanes, entries)) for v in marks], 0).astype(bf16)
    ranks = lax.dot_general(
        ranked(entries), tall, (((1,), (1,)), ((), ())), preferred_element_type=f32
    )
    ends = fields.astype(bf16)
    rows[...] = jnp.zeros_like(rows)
    lane = lax.broadcasted_iota(jnp.int32, (1, lanes), 1)
    numbers = jnp.zeros((1, lanes), jnp.int32)
    for k in range(4):
        both = spread(ranks[:, k * lanes : (k + 1) * lanes], ends, 2)
        number = jnp.sum(marks[k], 1, keepdims=True).astype(jnp.int32)
        low, high = (both[1:2], both[0:1]) if k == 1 else (both[0:1], both[1:2])
        put_list(rows, 2 * k, low, high, number, total)
        numbers = jnp.where(lane == k, number, numbers)
    rows[8:9, :] = numbers
    copy = pltpu.make_async_copy(rows, todo, sem)
    copy.start()
    shape_blocks(sizes, [(0, lambda d: own[d])], stage, right, weighed, left)
    left[total] = left[0]
    copy.wait()


def list_inbound(ranks_of, ends_of, sources, flags, rows, spare):
    base = 0
    for _, part in sources:
        height = part(9).shape[0]
        flags[base : base + height, :] = part(9)
        base += height
    by_code = [jnp.broadcast_to(flags[:, c : c + 1], (base, lanes)) for c in range(1, code_total)]
    tall = jnp.concatenate(by_code, 0).astype(bf16)
    rank = jnp.dot(ranks_of[...], tall, preferred_element_type=f32)
    both = spread(rank, ends_of[...], 2)
    number = rank[rank.shape[0] - 1 :, :].astype(jnp.int32)
    rows[...] = jnp.zeros_like(rows)
    put_list(rows, 0, both[0:1], both[1:2], number, spare)
    rows[2:3, :] = number


def add_step(lookup, start, width, right, weighed, left, acc):
    results = []
    for k in range(width):
        entry = lookup(start + k)
        row, col = entry & 255, entry >> 8
        square = lax.dot_general(
            right[col], left[row], (((0,), (0,)), ((), ())), preferred_element_type=f32
        )
        root = lax.rsqrt(square)
        weight = root * root * root
        high = weight.astype(bf16)
        low = (weight - high.astype(f32)).astype(bf16)
        both = jnp.dot(weighed[col], jnp.concatenate([high, low], 0), preferred_element_type=f32)
        results.append((row, both[0:16] + both[16:32]))
    for row, value in results:
        at_row = pl.ds(pl.multiple_of(row * 16, 16), 16)
        acc[at_row, :] += value


def interact(lookup, start, end, *refs):
    number = end - start
    steps = (number + unroll - 1 - short_steps[-1]) // unroll
    done = start + steps * unroll

    def whole(at, carry):
        add_step(lookup, start + at * unroll, unroll, *refs)
        return carry

    lax.fori_loop(0, steps, whole, 0)
    left_over = end - done
    least = 0
    for width in short_steps:

        @pl.when((left_over > least) & (left_over <= width))
        def _():
            add_step(lookup, done, width, *refs)

        least = width


def near_list(todo):
    n = todo[8, 0]
    number = n + todo[8, 1]
    return joined(todo, 0, n, todo, 2), jnp.minimum(number, first_share), number


def near_kernel(todo, right, weighed, left, acc):
    acc[...] = jnp.zeros_like(acc)
    lookup, middle, _ = near_list(todo)
    interact(lookup, 0, middle, right, weighed, left, acc)


def listed(rows, start):
    return lambda at: rows[start + (at >> 7), at & 127]


def joined(rows, start, number, more, then_start):
    first, then = listed(rows, start), listed(more, then_start)
    return lambda at: jnp.where(at < number, first(at), then(jnp.maximum(at - number, 0)))


def side_sources(sizes, groups, here, beside):
    bx, by, bz, cells = sizes
    heights = group_heights(bx, by, bz)
    mom_rows = 8 * cells // lanes
    x_start = parts_sent * heights[0]
    starts = {0: 0, 1: x_start, 2: x_start + parts_sent * heights[1] + mom_rows, 4: 0, 3: parts_sent * heights[3] + mom_rows}
    return [(g, rows_of((here, beside)[g >= 5], starts[g % 5], heights[g])) for g in groups]


def mid_kernel(sizes, ranks_of, ends_of, x_all, p_x_all, mom_in, todo, right, weighed, left, *refs):
    bx, by, bz, _ = sizes
    right_1, weighed_1, found, mom_out, acc, stage, flags, rows, sem = refs[-9:]
    sources = side_sources(sizes, set_groups(1), x_all, p_x_all)
    list_inbound(ranks_of, ends_of, sources, flags, rows, bx * by * bz)
    copy = pltpu.make_async_copy(rows, found, sem)
    copy.start()
    mom_out[...] = mom_in[...]
    shape_blocks(sizes, sources, stage, right_1, weighed_1)
    acc[...] = jnp.zeros_like(acc)
    lookup, middle, number = near_list(todo)
    interact(lookup, middle, number, right, weighed, left, acc)
    copy.wait()


def side_kernel(todo, found, right, weighed, left, _, acc):
    acc[...] = jnp.zeros_like(acc)
    n = todo[8, 2]
    interact(joined(todo, 4, n, found, 0), 0, n + found[2, 0], right, weighed, left, acc)


def coarse_place(sizes, axes, chunk):
    bx, by, bz, _ = sizes
    coarse = (bx // 2, by // 2, bz // 2)
    number = lax.broadcasted_iota(jnp.int32, (1, lanes), 1) + chunk * lanes
    places = []
    for d in (2, 1, 0):
        places.append(number % coarse[d])
        number = number // coarse[d]
    for k, d in enumerate((2, 1, 0)):
        size = lax.axis_size(axes[d])
        places[k] = places[k] + number % size * coarse[d]
        number = number // size
    return places[::-1]


def close_kernel(sizes, axes, grid, moments, todo, ranks_of, ends_of, y_both, p_y_both, left, acc_a, acc_b, acc_c, own, *refs):
    bx, by, bz, cells = sizes
    total, face = bx * by * bz, by * bz
    mom_parts = refs[:-9]
    out, right, weighed, stage, acc, flags, rows, found, sem = refs[-9:]
    sources = side_sources(sizes, set_groups(2), y_both, p_y_both)
    list_inbound(ranks_of, ends_of, sources, flags, rows, total)
    copy = pltpu.make_async_copy(rows, found, sem)
    copy.start()
    shape_blocks(sizes, sources, stage, right, weighed)
    acc[...] = acc_a[...] + acc_b[...] + acc_c[...]
    copy.wait()
    n = todo[8, 3]
    interact(joined(todo, 6, n, found, 0), 0, n + found[2, 0], right, weighed, left, acc)
    mom = moments(y_both, p_y_both, mom_parts)

    cx, cy, cz = bx // 2, by // 2, bz // 2
    deep = lax.broadcasted_iota(jnp.int32, (face, lanes), 0)
    local = (None, deep // (2 * bz), deep % bz // 2)
    far = [[] for _ in range(6)]
    for x in range(cx):
        totals = [jnp.zeros((face, lanes), f32)] * 6
        for chunk in range(cells // lanes):
            lengths = []
            cell_of = coarse_place(sizes, axes, chunk)
            for d, axis in enumerate(axes):
                at = lax.axis_index(axis) * (cx, cy, cz)[d] + (x if d == 0 else local[d])
                delta = at - cell_of[d]
                half = grid[d] // 2
                delta = jnp.where(delta >= grid[d] - half, delta - grid[d], delta)
                delta = jnp.where(delta < -half, delta + grid[d], delta)
                lengths.append(2.0 * delta.astype(f32))
            radius = lengths[0] * lengths[0] + lengths[1] * lengths[1] + lengths[2] * lengths[2]
            root = lax.rsqrt(radius + core_square)
            weight = jnp.where(radius == 0.0, 0.0, root * root * root)
            m = [mom[chunk * 8 + f : chunk * 8 + f + 1] for f in range(8)]
            turned = turn_rows([weight * v for v in lengths], m)
            totals = [t + v for t, v in zip(totals, turned)]
        for f in range(6):
            far[f].append(jnp.sum(totals[f], 1, keepdims=True))

    place = position(0, total, bx, by, bz)
    p = [own[d] + place[d] for d in range(3)]
    b = [own[3 + d] for d in range(3)]
    l = [own[6 + d] for d in range(3)]
    moment = [acc[pl.ds(f, total, stride=16), :] for f in range(8)]
    crossed = [acc[pl.ds(8 + f, total, stride=16), :] for f in range(6)]
    turned = turn_rows(p, moment)
    s = []
    for f in range(6):
        column = jnp.concatenate([far[f][x // 2] for x in range(bx)], 0)
        s.append(turned[f] - crossed[f] + column)
    push = [
        s[0] * b[0] + s[3] * b[1] + s[4] * b[2],
        s[3] * b[0] + s[1] * b[1] + s[5] * b[2],
        s[4] * b[0] + s[5] * b[1] + s[2] * b[2],
    ]
    out[0] = kernel_scale * (push[1] * l[2] - push[2] * l[1])
    out[1] = kernel_scale * (push[2] * l[0] - push[0] * l[2])
    out[2] = kernel_scale * (push[0] * l[1] - push[1] * l[0])


def shifted(value, axis, step):
    size = lax.axis_size(axis)
    return lax.ppermute(value, axis, [(i, (i + step) % size) for i in range(size)])


def ring_sum(value, axis):
    total = value
    for step in range(1, lax.axis_size(axis)):
        total = total + shifted(value, axis, step)
    return total


def beside_z(value, layers):
    size = lax.axis_size("gz")
    if size == 2:
        return shifted(value, "gz", 1)
    head = value.shape
    split = value.reshape(-1, layers, lanes)
    above = shifted(split[:, :1], "gz", -1)
    below = shifted(split[:, layers - 1 :], "gz", 1)
    middle = split[:, 1 : layers - 1]
    return jnp.concatenate([above, middle, below], 1).reshape(head)


def body(offsets, burgers, line, block_fill, near_pairs, pair_count):
    _, bx, by, bz, slots = offsets.shape
    axes = ("gx", "gy", "gz")
    sizes = [lax.axis_size(axis) for axis in axes]
    heights = group_heights(bx, by, bz)
    own, face, rim = heights[0], heights[1], heights[3]
    set_size = [sum(heights[g] for g in set_groups(which)) for which in range(3)]
    coarse = (bx // 2, by // 2, bz // 2)
    grid = tuple(c * n for c, n in zip(coarse, sizes))
    per_device = coarse[0] * coarse[1] * coarse[2]
    cells = per_device * sizes[0] * sizes[1] * sizes[2]
    mom_rows = 8 * cells // lanes
    kinds = (bx, by, bz, cells)
    entries = near_pairs.shape[0]
    vmem = pl.BlockSpec(memory_space=pltpu.VMEM)
    smem = pl.BlockSpec(memory_space=pltpu.SMEM)
    hbm = pl.BlockSpec(memory_space=pltpu.HBM)
    anywhere = pl.BlockSpec(memory_space=pl.ANY)
    shape = jax.ShapeDtypeStruct
    flat = lambda v: v.reshape(3, own, slots)
    far = lambda v: pltpu.with_memory_space_constraint(v, pltpu.HBM)

    tables = [jnp.asarray(v.astype(bf16)) for v in work_tables(bx, by, bz)]
    assert max(entries, tables[1].shape[0], tables[3].shape[0]) + unroll <= 2 * lanes

    def call(kernel, out_shape, in_specs, out_specs, scratch, name, cost, limit=12):
        return pl.pallas_call(
            kernel,
            out_shape=out_shape,
            in_specs=in_specs,
            out_specs=out_specs,
            scratch_shapes=scratch,
            compiler_params=pltpu.CompilerParams(vmem_limit_bytes=limit * 2**20),
            cost_estimate=pl.CostEstimate(flops=cost, bytes_accessed=cost, transcendentals=0),
            name=name,
        )

    face_shape = shape((parts_sent * face + mom_rows, lanes), f32)
    rim_shape = shape((parts_sent * rim + mom_rows, lanes), f32)
    mom_shape = shape((mom_rows, lanes), f32)
    acc_shape = shape(((own + 1) * 16, lanes), f32)
    mine, face_lo, face_hi, mom, pairs, codes_of, *inbound = call(
        functools.partial(pack_kernel, kinds, axes),
        [
            shape((parts_sent, own, lanes), f32),
            face_shape,
            face_shape,
            mom_shape,
            shape((1, entries), jnp.int32),
            *[shape(v.shape, v.dtype) for v in tables],
        ],
        [smem] + [hbm] * 10,
        [vmem] * 10,
        [
            pltpu.VMEM((bx, bz, by), jnp.int32),
            pltpu.VMEM((3, own, lanes), f32),
            pltpu.VMEM((3, own, lanes), f32),
            pltpu.VMEM((3, own, lanes), f32),
            pltpu.VMEM((own, lanes), jnp.int32),
            pltpu.SemaphoreType.DMA((10,)),
        ],
        "pack",
        10**6,
    )(
        pair_count,
        far(jnp.transpose(block_fill, (0, 2, 1))),
        far(flat(offsets)),
        far(flat(burgers)),
        far(flat(line)),
        far(near_pairs.reshape(1, -1)),
        *[far(v) for v in tables],
    )

    x_far = [shifted(mom, "gx", step) for step in range(2, sizes[0] - 1)]
    x_lo = shifted(face_hi, "gx", 1)
    x_hi = shifted(face_lo, "gx", -1)
    right, weighed, left, todo = call(
        functools.partial(own_kernel, kinds),
        [
            shape((own, 32, lanes), bf16),
            shape((own, 32, 2 * lanes), bf16),
            shape((own + 1, 32, lanes), bf16),
            pltpu.SMEM((16, lanes), jnp.int32),
        ],
        [vmem, vmem, smem, vmem],
        [vmem, vmem, vmem, smem],
        [
            pltpu.VMEM((own * 80, lanes), f32),
            pltpu.VMEM((16, lanes), jnp.int32),
            pltpu.SemaphoreType.DMA,
        ],
        "own",
        10**7,
    )(codes_of, pairs, pair_count, mine)
    acc_a = call(
        near_kernel,
        acc_shape,
        [smem, vmem, vmem, vmem],
        vmem,
        [],
        "near",
        10**7,
    )(todo, right, weighed, left)
    side_lo, side_hi, x_all, mom_x = call(
        functools.partial(rim_kernel, kinds, sizes[0] > 2),
        [
            rim_shape,
            rim_shape,
            shape((parts_sent * (own + 2 * face) + 2 * mom_rows, lanes), f32),
            mom_shape,
        ],
        [vmem] * 4 + [anywhere] + [vmem] * len(x_far),
        [vmem] * 4,
        [],
        "rim",
        10**6,
    )(mine, mom, x_lo, x_hi, acc_a, *x_far)
    y_lo = shifted(side_hi, "gy", 1)
    y_hi = shifted(side_lo, "gy", -1)
    y_far = [shifted(mom_x, "gy", step) for step in range(2, sizes[1] - 1)]
    p_x_all = beside_z(x_all, bz)
    right_1, weighed_1, found, mom_kept, acc_b = call(
        functools.partial(mid_kernel, kinds),
        [
            shape((set_size[1], 32, lanes), bf16),
            shape((set_size[1], 32, 2 * lanes), bf16),
            pltpu.SMEM((8, lanes), jnp.int32),
            mom_shape,
            acc_shape,
        ],
        [vmem] * 5 + [smem, vmem, vmem, vmem, anywhere, anywhere],
        [vmem, vmem, smem, vmem, vmem],
        [
            pltpu.VMEM((set_size[1] * 80, lanes), f32),
            pltpu.VMEM((set_size[1], lanes), f32),
            pltpu.VMEM((8, lanes), jnp.int32),
            pltpu.SemaphoreType.DMA,
        ],
        "mid",
        10**7,
    )(*inbound[:2], x_all, p_x_all, mom_x, todo, right, weighed, left, side_lo, side_hi)
    for v in y_far:
        mom_kept = mom_kept + v
    y_both = jnp.concatenate([y_hi, y_lo, mom_kept], 0)
    p_y_both = beside_z(y_both, bz)

    acc_c = call(
        side_kernel,
        acc_shape,
        [smem, smem, vmem, vmem, vmem, anywhere],
        vmem,
        [],
        "side",
        10**7,
    )(todo, found, right_1, weighed_1, left, y_both)
    tail = parts_sent * rim
    if sizes[2] == 2:
        mom_parts = []

        def moments(y_both, p_y_both, parts):
            spans = [slice(tail, tail + mom_rows)]
            if sizes[1] > 2:
                spans.append(slice(2 * tail + mom_rows, 2 * (tail + mom_rows)))
            spans.append(slice(2 * (tail + mom_rows), 2 * tail + 3 * mom_rows))
            return sum(y_both[span] + p_y_both[span] for span in spans)

    else:
        mom_parts = [ring_sum(mom_kept + y_lo[tail:] + y_hi[tail:], "gz")]
        moments = lambda y_both, p_y_both, parts: parts[0][...]

    forces = call(
        functools.partial(close_kernel, kinds, axes, grid, moments),
        shape((3, own, lanes), f32),
        [smem] + [vmem] * (9 + len(mom_parts)),
        vmem,
        [
            pltpu.VMEM((set_size[2], 32, lanes), bf16),
            pltpu.VMEM((set_size[2], 32, 2 * lanes), bf16),
            pltpu.VMEM(((set_size[2] + 8) * 80, lanes), f32),
            pltpu.VMEM(((own + 1) * 16, lanes), f32),
            pltpu.VMEM((set_size[2], lanes), f32),
            pltpu.VMEM((8, lanes), jnp.int32),
            pltpu.SMEM((8, lanes), jnp.int32),
            pltpu.SemaphoreType.DMA,
        ],
        "close",
        10**7,
    )(todo, *inbound[2:], y_both, p_y_both, left, acc_a, acc_b, acc_c, mine, *mom_parts)
    return forces.reshape(3, bx, by, bz, slots)


def solution(mesh):
    in_specs = (
        P(None, "gx", "gy", "gz", None),
        P(None, "gx", "gy", "gz", None),
        P(None, "gx", "gy", "gz", None),
        P("gx", "gy", "gz"),
        P(("gx", "gy", "gz")),
        P(("gx", "gy", "gz")),
    )
    out_specs = P(None, "gx", "gy", "gz", None)
    return jax.shard_map(body, mesh=mesh, in_specs=in_specs, out_specs=out_specs, check_vma=False)
```

```python
import functools
import math

import jax
import jax.numpy as jnp
import numpy as np
from jax import lax
from jax.experimental import pallas as pl
from jax.experimental.pallas import tpu as pltpu
from jax.sharding import PartitionSpec as P

stencil_table = (
    (0, 0, 0),
    (1, 0, 0),
    (0, 1, 0),
    (0, 0, 1),
    (1, 1, 0),
    (-1, 1, 0),
    (1, 0, 1),
    (1, 0, -1),
    (0, 1, 1),
    (0, -1, 1),
    (1, 1, -1),
    (1, -1, 1),
    (-1, 1, 1),
    (1, 1, 1),
)
code_total = len(stencil_table)
kernel_scale = 1.0 / (8.0 * math.pi)
core_square = 0.09
lanes = 128
mark = 2048.0
parts_sent = 10
unroll = 64
short_steps = (16, 32, 48)
first_share = 96
f32 = jnp.float32
bf16 = jnp.bfloat16


group_set = (0, 1, 1, 2, 2, 1, 1, 1, 2, 2)


def set_groups(which):
    return [g for g in range(10) if group_set[g] == which]


def group_heights(bx, by, bz):
    return [bx * by * bz, by * bz, by * bz, (bx + 2) * bz, (bx + 2) * bz] * 2


def block_layout(bx, by, bz):
    coords = []
    for z_of in ([z + 1 for z in range(bz)], [bz + 1 if z == 0 else 0 for z in range(bz)]):
        coords.append([(x + 1, y + 1, z) for x in range(bx) for y in range(by) for z in z_of])
        for x in (0, bx + 1):
            coords.append([(x, y + 1, z) for y in range(by) for z in z_of])
        for y in (0, by + 1):
            coords.append([(x, y, z) for x in range(bx + 2) for z in z_of])
    return coords


def work_tables(bx, by, bz):
    groups = block_layout(bx, by, bz)
    place = {}
    count = [0, 0, 0]
    for g, group in enumerate(groups):
        for c in group:
            place[c] = (group_set[g], count[group_set[g]])
            count[group_set[g]] += 1
    codes = np.zeros((8, count[0] * code_total), np.float32)
    for a, at in enumerate(groups[0]):
        for code, o in enumerate(stencil_table):
            which, b = place[tuple(at[d] + o[d] for d in range(3))]
            k = a * code_total + code
            codes[:2, k] = a, b
            codes[(2, 4, 5)[which], k] = 1.0
            codes[3, k] = which == 0 and code > 0
    inbound = []
    for which in (1, 2):
        found = []
        for at, (at_set, h) in place.items():
            for code, o in enumerate(stencil_table):
                to, b = place.get(tuple(at[d] + o[d] for d in range(3)), (3, 0))
                if at_set == which and to == 0 and code:
                    found.append((b, h, code))
        size = -(-(len(found) + 1) // 16) * 16
        ranks = np.zeros((size, (code_total - 1) * count[which]), np.float32)
        ends = np.zeros((8, size), np.float32)
        for k, (b, h, code) in enumerate(found):
            at = (code - 1) * count[which] + h
            ranks[k + 1 : len(found), at] = ranks[size - 1, at] = 1.0
            ranks[k, at] = mark
            ends[:2, k] = b, h
        inbound += [ranks, ends]
    return [codes, *inbound]


def position(group, rows, bx, by, bz):
    row = lax.broadcasted_iota(jnp.int32, (rows, lanes), 0)
    z = row % bz
    line = row // bz
    kind = group % 5
    if kind == 0:
        x, y = line // by + 1, line % by + 1
    elif kind <= 2:
        x, y = jnp.full_like(row, 0 if kind == 1 else bx + 1), line + 1
    else:
        x, y = line, jnp.full_like(row, 0 if kind == 3 else by + 1)
    if group < 5:
        z = z + 1
    else:
        z = jnp.where(z == 0, bz + 1, 0)
    sides = (bx + 1, by + 1, bz + 1)
    return [v.astype(f32) - 0.5 * side for v, side in zip((x, y, z), sides)]


def moment_rows(b, l):
    zz = b[2] * l[2]
    return [
        b[0] * l[1],
        b[0] * l[2],
        b[1] * l[0],
        b[1] * l[2],
        b[2] * l[0],
        b[2] * l[1],
        b[0] * l[0] - zz,
        b[1] * l[1] - zz,
    ]


def cross_rows(q, b, l):
    c = [q[1] * b[2] - q[2] * b[1], q[2] * b[0] - q[0] * b[2], q[0] * b[1] - q[1] * b[0]]
    return [
        2.0 * c[0] * l[0],
        2.0 * c[1] * l[1],
        2.0 * c[2] * l[2],
        c[0] * l[1] + c[1] * l[0],
        c[0] * l[2] + c[2] * l[0],
        c[1] * l[2] + c[2] * l[1],
    ]


def turn_rows(r, m):
    return [
        2.0 * (r[1] * m[4] - r[2] * m[2]),
        2.0 * (r[2] * m[0] - r[0] * m[5]),
        2.0 * (r[0] * m[3] - r[1] * m[1]),
        r[1] * m[5] - r[0] * m[4] + r[2] * (m[6] - m[7]),
        r[0] * m[2] - r[2] * m[3] - r[1] * m[6],
        r[2] * m[1] + r[0] * m[7] - r[1] * m[0],
    ]


def pieces(value):
    first = value.astype(bf16).astype(f32)
    rest = value - first
    second = rest.astype(bf16).astype(f32)
    return first, second, rest - second


def distance_rows(q):
    near = q[0] * q[0] + q[1] * q[1] + q[2] * q[2]
    one = jnp.ones_like(near)
    left, right = [], []
    for axis in q:
        p1, p2, p3 = pieces(axis)
        left += [p1, p1, p2, p2, p1, p3]
        right += [-2.0 * v for v in (p1, p2, p1, p2, p3, p1)]
    left += [*pieces(near), one, one, one]
    right += [one, one, one, *pieces(near + core_square)]
    return left, right


def pack_kernel(sizes, axes, count, fill_h, offsets_h, burgers_h, line_h, pairs_h, *refs):
    bx, by, bz, cells = sizes
    total, face = bx * by * bz, by * bz
    tables_h, (own, face_lo, face_hi, mom, pairs), tables = refs[:5], refs[5:10], refs[10:15]
    fill, offsets, burgers, line, level, sems = refs[15:]
    table_copies = [
        pltpu.make_async_copy(u, v, sems.at[5 + k]) for k, (u, v) in enumerate(zip(tables_h, tables))
    ]
    moves = ((fill_h, fill), (pairs_h, pairs), (burgers_h, burgers), (line_h, line), (offsets_h, offsets))
    copies = [pltpu.make_async_copy(u, v, sems.at[k]) for k, (u, v) in enumerate(moves)]
    for copy in copies + table_copies:
        copy.start()
    for copy in copies:
        copy.wait()
    for x in range(bx):
        for y in range(by):
            column = jnp.broadcast_to(fill[x][:, y : y + 1], (bz, lanes))
            level[x * face + y * bz : x * face + (y + 1) * bz, :] = column
    live = lax.broadcasted_iota(jnp.int32, (total, lanes), 1) < level[...]
    b, l = [], []
    for d in range(3):
        own[d] = offsets[d]
        b.append(jnp.where(live, burgers[d], 0.0))
        l.append(jnp.where(live, line[d], 0.0))
        own[3 + d] = b[d]
        own[6 + d] = l[d]
    entries = pairs.shape[1]
    code = pairs[...]
    block_no = code // code_total
    code_no = code - block_no * code_total
    alive = lax.broadcasted_iota(jnp.int32, (1, entries), 1) < count[0]
    of_block = lax.broadcasted_iota(jnp.int32, (total, entries), 0) == block_no
    of_code = lax.broadcasted_iota(jnp.int32, (lanes, entries), 0) == code_no
    own[9] = lax.dot_general(
        jnp.where(of_block & alive, 1.0, 0.0).astype(bf16),
        jnp.where(of_code, 1.0, 0.0).astype(bf16),
        (((1,), (1,)), ((), ())),
        preferred_element_type=f32,
    )
    cx, cy, cz = bx // 2, by // 2, bz // 2
    here = lax.axis_index(axes[0])
    for axis in axes[1:]:
        here = here * lax.axis_size(axis) + lax.axis_index(axis)
    first_lane = here * (cx * cy * cz)
    wide = lax.broadcasted_iota(jnp.int32, (face, lanes), 1)
    deep = lax.broadcasted_iota(jnp.int32, (face, lanes), 0)
    local = deep // (2 * bz) * cz + deep % bz // 2
    sums = []
    for feature in moment_rows(b, l):
        column = []
        for x in range(cx):
            both = feature[2 * x * face : (2 * x + 1) * face] + feature[(2 * x + 1) * face : (2 * x + 2) * face]
            column.append(jnp.sum(both, 1, keepdims=True))
        sums.append(column)
    for chunk in range(cells // lanes):
        for f, column in enumerate(sums):
            placed = jnp.zeros((face, lanes), f32)
            for x in range(cx):
                lane_of = first_lane + x * cy * cz + local - chunk * lanes
                placed = placed + jnp.where(wide == lane_of, column[x], 0.0)
            mom[chunk * 8 + f : chunk * 8 + f + 1, :] = jnp.sum(placed, 0, keepdims=True)
    for d in range(parts_sent):
        face_lo[d * face : (d + 1) * face] = own[d, 0:face]
        face_hi[d * face : (d + 1) * face] = own[d, total - face : total]
    face_lo[parts_sent * face :] = mom[...]
    face_hi[parts_sent * face :] = mom[...]
    for copy in table_copies:
        copy.wait()


def rim_kernel(sizes, axes, both_ways, own, mom, x_lo_in, x_hi_in, *refs):
    bx, by, bz, _ = sizes
    face = by * bz
    (side_1, side_2, x_all, mom_x), more = refs[-4:], refs[1:-4]
    odd_y = lax.rem(lax.axis_index(axes[1]), 2) == 1
    total = bx * by * bz
    for d in range(parts_sent):
        x_all[d * total : (d + 1) * total] = own[d]
    start, tall = parts_sent * total, x_lo_in.shape[0]
    x_lo, x_hi = x_lo_in[...], x_hi_in[...]
    x_all[start : start + tall] = x_lo
    x_all[start + tall : start + 2 * tall] = x_hi

    def side(d, y):
        rows = [x_lo[d * face + y * bz : d * face + (y + 1) * bz]]
        for x in range(bx):
            rows.append(own[d, x * face + y * bz : x * face + (y + 1) * bz])
        return rows + [x_hi[d * face + y * bz : d * face + (y + 1) * bz]]

    for d in range(parts_sent):
        for x, (lo, hi) in enumerate(zip(side(d, 0), side(d, by - 1))):
            at = (d * (bx + 2) + x) * bz
            side_1[at : at + bz] = jnp.where(odd_y, lo, hi)
            side_2[at : at + bz] = jnp.where(odd_y, hi, lo)
    head = parts_sent * face
    sums = mom[...] + x_lo[head:]
    if both_ways:
        sums = sums + x_hi[head:]
    for v in more:
        sums = sums + v[...]
    mom_x[...] = sums
    head = parts_sent * (bx + 2) * bz
    side_1[head:] = sums
    side_2[head:] = sums


def join_kernel(axes, y_2, y_1, *refs):
    odd = lax.rem(lax.axis_index(axes[1]), 2) == 1
    out, tall = refs[-1], y_1.shape[0]
    out[0:tall] = jnp.where(odd, y_1[...], y_2[...])
    out[tall : 2 * tall] = jnp.where(odd, y_2[...], y_1[...])
    sums = refs[0][...]
    for v in refs[1:-1]:
        sums = sums + v[...]
    out[2 * tall :] = sums


def shape_blocks(sizes, sources, stage, right, weighed, left=None):
    bx, by, bz, _ = sizes
    heights = group_heights(bx, by, bz)
    base = 0
    for group, part in sources:
        h = heights[group]
        zero = jnp.zeros((h, lanes), f32)
        place = position(group, h, bx, by, bz)
        q = [part(d) + place[d] for d in range(3)]
        b = [part(3 + d) for d in range(3)]
        l = [part(6 + d) for d in range(3)]
        rows = moment_rows(b, l) + cross_rows(q, b, l)
        lhs, rhs = distance_rows(q)
        rows = rows + [zero] * (16 - len(rows)) + rhs + [zero] * (32 - len(rhs))
        if left is not None:
            rows = rows + lhs + [zero] * (32 - len(lhs))
        for f, value in enumerate(rows):
            stage[pl.ds(base * 80 + f, h, stride=80), :] = value
        base += h

    def shape_block(block, carry):
        at = pl.multiple_of(block * 80, 16)
        product = stage[pl.ds(at, 16), :]
        high = product.astype(bf16)
        low = (product - high.astype(f32)).astype(bf16)
        weighed[block, 0:16, 0:lanes] = high
        weighed[block, 0:16, lanes : 2 * lanes] = high
        weighed[block, 16:32, 0:lanes] = low
        weighed[block, 16:32, lanes : 2 * lanes] = jnp.zeros_like(low)
        right[block] = stage[pl.ds(at + 16, 32), :].astype(bf16)
        if left is not None:
            left[block] = stage[pl.ds(at + 48, 32), :].astype(bf16)
        return carry

    lax.fori_loop(0, base, shape_block, 0, unroll=8)


def rows_of(ref, start, height):
    return lambda d: ref[start + d * height : start + (d + 1) * height, :]


def ranked(size):
    down = lax.broadcasted_iota(jnp.int32, (size, size), 0)
    across = lax.broadcasted_iota(jnp.int32, (size, size), 1)
    return jnp.where(down > across, 1.0, jnp.where(down == across, mark, 0.0)).astype(bf16)


def spread(rank, fields, chunks):
    lane = lax.broadcasted_iota(jnp.int32, rank.shape, 1).astype(f32) + mark
    hot = [jnp.where(rank == lane + float(m * lanes), 1.0, 0.0).astype(bf16) for m in range(chunks)]
    return jnp.dot(fields, jnp.concatenate(hot, 1), preferred_element_type=f32)


def put_list(rows, start, low, high, number, spare):
    for m in range(low.shape[1] // lanes):
        lane = lax.broadcasted_iota(jnp.int32, (1, lanes), 1) + m * lanes
        part = slice(m * lanes, (m + 1) * lanes)
        value = (low[:, part] + 256.0 * high[:, part]).astype(jnp.int32)
        rows[start + m : start + m + 1, :] = jnp.where(lane < number, value, spare)


def own_kernel(sizes, codes_of, pairs, count, own, right, weighed, left, todo, stage, rows, sem):
    bx, by, bz, _ = sizes
    total = bx * by * bz
    entries = pairs.shape[1]
    code = lax.broadcasted_iota(jnp.int32, (total * code_total, entries), 0)
    hot = jnp.where(code == pairs[...], 1.0, 0.0).astype(bf16)
    fields = jnp.dot(codes_of[...], hot, preferred_element_type=f32)
    alive = lax.broadcasted_iota(jnp.int32, (1, entries), 1) < count[0]
    marks = [jnp.where(alive, fields[k : k + 1], 0.0) for k in range(2, 6)]
    tall = jnp.concatenate([jnp.broadcast_to(v, (lanes, entries)) for v in marks], 0).astype(bf16)
    ranks = lax.dot_general(
        ranked(entries), tall, (((1,), (1,)), ((), ())), preferred_element_type=f32
    )
    ends = fields.astype(bf16)
    rows[...] = jnp.zeros_like(rows)
    lane = lax.broadcasted_iota(jnp.int32, (1, lanes), 1)
    numbers = jnp.zeros((1, lanes), jnp.int32)
    for k in range(4):
        both = spread(ranks[:, k * lanes : (k + 1) * lanes], ends, 2)
        number = jnp.sum(marks[k], 1, keepdims=True).astype(jnp.int32)
        low, high = (both[1:2], both[0:1]) if k == 1 else (both[0:1], both[1:2])
        put_list(rows, 2 * k, low, high, number, total)
        numbers = jnp.where(lane == k, number, numbers)
    rows[8:9, :] = numbers
    copy = pltpu.make_async_copy(rows, todo, sem)
    copy.start()
    shape_blocks(sizes, [(0, lambda d: own[d])], stage, right, weighed, left)
    left[total] = left[0]
    copy.wait()


def list_inbound(ranks_of, ends_of, sources, flags, rows, spare):
    base = 0
    for _, part in sources:
        height = part(9).shape[0]
        flags[base : base + height, :] = part(9)
        base += height
    by_code = [jnp.broadcast_to(flags[:, c : c + 1], (base, lanes)) for c in range(1, code_total)]
    tall = jnp.concatenate(by_code, 0).astype(bf16)
    rank = jnp.dot(ranks_of[...], tall, preferred_element_type=f32)
    both = spread(rank, ends_of[...], 2)
    number = rank[rank.shape[0] - 1 :, :].astype(jnp.int32)
    rows[...] = jnp.zeros_like(rows)
    put_list(rows, 0, both[0:1], both[1:2], number, spare)
    rows[2:3, :] = number


def add_step(lookup, start, width, right, weighed, left, acc):
    results = []
    for k in range(width):
        entry = lookup(start + k)
        row, col = entry & 255, entry >> 8
        square = lax.dot_general(
            right[col], left[row], (((0,), (0,)), ((), ())), preferred_element_type=f32
        )
        root = lax.rsqrt(square)
        weight = root * root * root
        high = weight.astype(bf16)
        low = (weight - high.astype(f32)).astype(bf16)
        both = jnp.dot(weighed[col], jnp.concatenate([high, low], 0), preferred_element_type=f32)
        results.append((row, both[0:16] + both[16:32]))
    for row, value in results:
        at_row = pl.ds(pl.multiple_of(row * 16, 16), 16)
        acc[at_row, :] += value


def interact(lookup, start, end, *refs):
    number = end - start
    steps = (number + unroll - 1 - short_steps[-1]) // unroll
    done = start + steps * unroll

    def whole(at, carry):
        add_step(lookup, start + at * unroll, unroll, *refs)
        return carry

    lax.fori_loop(0, steps, whole, 0)
    left_over = end - done
    least = 0
    for width in short_steps:

        @pl.when((left_over > least) & (left_over <= width))
        def _():
            add_step(lookup, done, width, *refs)

        least = width


def near_list(todo):
    n = todo[8, 0]
    number = n + todo[8, 1]
    return joined(todo, 0, n, todo, 2), jnp.minimum(number, first_share), number


def near_kernel(todo, right, weighed, left, acc):
    acc[...] = jnp.zeros_like(acc)
    lookup, middle, _ = near_list(todo)
    interact(lookup, 0, middle, right, weighed, left, acc)


def listed(rows, start):
    return lambda at: rows[start + (at >> 7), at & 127]


def joined(rows, start, number, more, then_start):
    first, then = listed(rows, start), listed(more, then_start)
    return lambda at: jnp.where(at < number, first(at), then(jnp.maximum(at - number, 0)))


def side_sources(sizes, groups, here, beside):
    bx, by, bz, cells = sizes
    heights = group_heights(bx, by, bz)
    mom_rows = 8 * cells // lanes
    x_start = parts_sent * heights[0]
    starts = {0: 0, 1: x_start, 2: x_start + parts_sent * heights[1] + mom_rows, 3: 0, 4: parts_sent * heights[3] + mom_rows}
    return [(g, rows_of((here, beside)[g >= 5], starts[g % 5], heights[g])) for g in groups]


def mid_kernel(sizes, ranks_of, ends_of, x_all, p_x_all, mom_in, todo, right, weighed, left, *refs):
    bx, by, bz, _ = sizes
    right_1, weighed_1, found, mom_out, acc, stage, flags, rows, sem = refs[-9:]
    sources = side_sources(sizes, set_groups(1), x_all, p_x_all)
    list_inbound(ranks_of, ends_of, sources, flags, rows, bx * by * bz)
    copy = pltpu.make_async_copy(rows, found, sem)
    copy.start()
    mom_out[...] = mom_in[...]
    shape_blocks(sizes, sources, stage, right_1, weighed_1)
    acc[...] = jnp.zeros_like(acc)
    lookup, middle, number = near_list(todo)
    interact(lookup, middle, number, right, weighed, left, acc)
    copy.wait()


def side_kernel(todo, found, right, weighed, left, _, acc):
    acc[...] = jnp.zeros_like(acc)
    n = todo[8, 2]
    interact(joined(todo, 4, n, found, 0), 0, n + found[2, 0], right, weighed, left, acc)


def coarse_place(sizes, axes, chunk):
    bx, by, bz, _ = sizes
    coarse = (bx // 2, by // 2, bz // 2)
    number = lax.broadcasted_iota(jnp.int32, (1, lanes), 1) + chunk * lanes
    places = []
    for d in (2, 1, 0):
        places.append(number % coarse[d])
        number = number // coarse[d]
    for k, d in enumerate((2, 1, 0)):
        size = lax.axis_size(axes[d])
        places[k] = places[k] + number % size * coarse[d]
        number = number // size
    return places[::-1]


def close_kernel(sizes, axes, grid, moments, todo, ranks_of, ends_of, y_both, p_y_both, left, acc_a, acc_b, acc_c, own, *refs):
    bx, by, bz, cells = sizes
    total, face = bx * by * bz, by * bz
    mom_parts = refs[:-9]
    out, right, weighed, stage, acc, flags, rows, found, sem = refs[-9:]
    sources = side_sources(sizes, set_groups(2), y_both, p_y_both)
    list_inbound(ranks_of, ends_of, sources, flags, rows, total)
    copy = pltpu.make_async_copy(rows, found, sem)
    copy.start()
    shape_blocks(sizes, sources, stage, right, weighed)
    acc[...] = acc_a[...] + acc_b[...] + acc_c[...]
    copy.wait()
    n = todo[8, 3]
    interact(joined(todo, 6, n, found, 0), 0, n + found[2, 0], right, weighed, left, acc)
    mom = moments(y_both, p_y_both, mom_parts)

    cx, cy, cz = bx // 2, by // 2, bz // 2
    deep = lax.broadcasted_iota(jnp.int32, (face, lanes), 0)
    local = (None, deep // (2 * bz), deep % bz // 2)
    far = [[] for _ in range(6)]
    for x in range(cx):
        totals = [jnp.zeros((face, lanes), f32)] * 6
        for chunk in range(cells // lanes):
            lengths = []
            cell_of = coarse_place(sizes, axes, chunk)
            for d, axis in enumerate(axes):
                at = lax.axis_index(axis) * (cx, cy, cz)[d] + (x if d == 0 else local[d])
                delta = at - cell_of[d]
                half = grid[d] // 2
                delta = jnp.where(delta >= grid[d] - half, delta - grid[d], delta)
                delta = jnp.where(delta < -half, delta + grid[d], delta)
                lengths.append(2.0 * delta.astype(f32))
            radius = lengths[0] * lengths[0] + lengths[1] * lengths[1] + lengths[2] * lengths[2]
            root = lax.rsqrt(radius + core_square)
            weight = jnp.where(radius == 0.0, 0.0, root * root * root)
            m = [mom[chunk * 8 + f : chunk * 8 + f + 1] for f in range(8)]
            turned = turn_rows([weight * v for v in lengths], m)
            totals = [t + v for t, v in zip(totals, turned)]
        for f in range(6):
            far[f].append(jnp.sum(totals[f], 1, keepdims=True))

    place = position(0, total, bx, by, bz)
    p = [own[d] + place[d] for d in range(3)]
    b = [own[3 + d] for d in range(3)]
    l = [own[6 + d] for d in range(3)]
    moment = [acc[pl.ds(f, total, stride=16), :] for f in range(8)]
    crossed = [acc[pl.ds(8 + f, total, stride=16), :] for f in range(6)]
    turned = turn_rows(p, moment)
    s = []
    for f in range(6):
        column = jnp.concatenate([far[f][x // 2] for x in range(bx)], 0)
        s.append(turned[f] - crossed[f] + column)
    push = [
        s[0] * b[0] + s[3] * b[1] + s[4] * b[2],
        s[3] * b[0] + s[1] * b[1] + s[5] * b[2],
        s[4] * b[0] + s[5] * b[1] + s[2] * b[2],
    ]
    out[0] = kernel_scale * (push[1] * l[2] - push[2] * l[1])
    out[1] = kernel_scale * (push[2] * l[0] - push[0] * l[2])
    out[2] = kernel_scale * (push[0] * l[1] - push[1] * l[0])


def shifted(value, axis, step):
    size = lax.axis_size(axis)
    return lax.ppermute(value, axis, [(i, (i + step) % size) for i in range(size)])


def exchanged(value, axis, turn):
    size = lax.axis_size(axis)
    return lax.ppermute(
        value, axis, [(i, (i + (1 if (i + turn) % 2 == 0 else -1)) % size) for i in range(size)]
    )


def ring_sum(value, axis):
    total = value
    for step in range(1, lax.axis_size(axis)):
        total = total + shifted(value, axis, step)
    return total


def beside_z(value, layers):
    size = lax.axis_size("gz")
    if size == 2:
        return shifted(value, "gz", 1)
    head = value.shape
    split = value.reshape(-1, layers, lanes)
    above = shifted(split[:, :1], "gz", -1)
    below = shifted(split[:, layers - 1 :], "gz", 1)
    middle = split[:, 1 : layers - 1]
    return jnp.concatenate([above, middle, below], 1).reshape(head)


def body(offsets, burgers, line, block_fill, near_pairs, pair_count):
    _, bx, by, bz, slots = offsets.shape
    axes = ("gx", "gy", "gz")
    sizes = [lax.axis_size(axis) for axis in axes]
    heights = group_heights(bx, by, bz)
    own, face, rim = heights[0], heights[1], heights[3]
    set_size = [sum(heights[g] for g in set_groups(which)) for which in range(3)]
    coarse = (bx // 2, by // 2, bz // 2)
    grid = tuple(c * n for c, n in zip(coarse, sizes))
    per_device = coarse[0] * coarse[1] * coarse[2]
    cells = per_device * sizes[0] * sizes[1] * sizes[2]
    mom_rows = 8 * cells // lanes
    kinds = (bx, by, bz, cells)
    entries = near_pairs.shape[0]
    vmem = pl.BlockSpec(memory_space=pltpu.VMEM)
    smem = pl.BlockSpec(memory_space=pltpu.SMEM)
    hbm = pl.BlockSpec(memory_space=pltpu.HBM)
    anywhere = pl.BlockSpec(memory_space=pl.ANY)
    shape = jax.ShapeDtypeStruct
    flat = lambda v: v.reshape(3, own, slots)
    far = lambda v: pltpu.with_memory_space_constraint(v, pltpu.HBM)

    tables = [jnp.asarray(v.astype(bf16)) for v in work_tables(bx, by, bz)]
    assert max(entries, tables[1].shape[0], tables[3].shape[0]) + unroll <= 2 * lanes

    def call(kernel, out_shape, in_specs, out_specs, scratch, name, cost, limit=12):
        return pl.pallas_call(
            kernel,
            out_shape=out_shape,
            in_specs=in_specs,
            out_specs=out_specs,
            scratch_shapes=scratch,
            compiler_params=pltpu.CompilerParams(vmem_limit_bytes=limit * 2**20),
            cost_estimate=pl.CostEstimate(flops=cost, bytes_accessed=cost, transcendentals=0),
            name=name,
        )

    face_shape = shape((parts_sent * face + mom_rows, lanes), f32)
    rim_shape = shape((parts_sent * rim + mom_rows, lanes), f32)
    mom_shape = shape((mom_rows, lanes), f32)
    acc_shape = shape(((own + 1) * 16, lanes), f32)
    mine, face_lo, face_hi, mom, pairs, codes_of, *inbound = call(
        functools.partial(pack_kernel, kinds, axes),
        [
            shape((parts_sent, own, lanes), f32),
            face_shape,
            face_shape,
            mom_shape,
            shape((1, entries), jnp.int32),
            *[shape(v.shape, v.dtype) for v in tables],
        ],
        [smem] + [hbm] * 10,
        [vmem] * 10,
        [
            pltpu.VMEM((bx, bz, by), jnp.int32),
            pltpu.VMEM((3, own, lanes), f32),
            pltpu.VMEM((3, own, lanes), f32),
            pltpu.VMEM((3, own, lanes), f32),
            pltpu.VMEM((own, lanes), jnp.int32),
            pltpu.SemaphoreType.DMA((10,)),
        ],
        "pack",
        10**6,
    )(
        pair_count,
        far(jnp.transpose(block_fill, (0, 2, 1))),
        far(flat(offsets)),
        far(flat(burgers)),
        far(flat(line)),
        far(near_pairs.reshape(1, -1)),
        *[far(v) for v in tables],
    )

    x_far = [shifted(mom, "gx", step) for step in range(2, sizes[0] - 1)]
    x_lo = shifted(face_hi, "gx", 1)
    x_hi = shifted(face_lo, "gx", -1)
    right, weighed, left, todo = call(
        functools.partial(own_kernel, kinds),
        [
            shape((own, 32, lanes), bf16),
            shape((own, 32, 2 * lanes), bf16),
            shape((own + 1, 32, lanes), bf16),
            pltpu.SMEM((16, lanes), jnp.int32),
        ],
        [vmem, vmem, smem, vmem],
        [vmem, vmem, vmem, smem],
        [
            pltpu.VMEM((own * 80, lanes), f32),
            pltpu.VMEM((16, lanes), jnp.int32),
            pltpu.SemaphoreType.DMA,
        ],
        "own",
        10**7,
    )(codes_of, pairs, pair_count, mine)
    acc_a = call(
        near_kernel,
        acc_shape,
        [smem, vmem, vmem, vmem],
        vmem,
        [],
        "near",
        10**7,
    )(todo, right, weighed, left)
    side_1, side_2, x_all, mom_x = call(
        functools.partial(rim_kernel, kinds, axes, sizes[0] > 2),
        [
            rim_shape,
            rim_shape,
            shape((parts_sent * (own + 2 * face) + 2 * mom_rows, lanes), f32),
            mom_shape,
        ],
        [vmem] * 4 + [anywhere] + [vmem] * len(x_far),
        [vmem] * 4,
        [],
        "rim",
        10**6,
    )(mine, mom, x_lo, x_hi, acc_a, *x_far)
    y_1 = exchanged(side_1, "gy", 0)
    y_2 = exchanged(side_2, "gy", 1)
    y_far = [shifted(mom_x, "gy", step) for step in range(2, sizes[1] - 1)]
    p_x_all = beside_z(x_all, bz)
    right_1, weighed_1, found, mom_kept, acc_b = call(
        functools.partial(mid_kernel, kinds),
        [
            shape((set_size[1], 32, lanes), bf16),
            shape((set_size[1], 32, 2 * lanes), bf16),
            pltpu.SMEM((8, lanes), jnp.int32),
            mom_shape,
            acc_shape,
        ],
        [vmem] * 5 + [smem, vmem, vmem, vmem, anywhere, anywhere],
        [vmem, vmem, smem, vmem, vmem],
        [
            pltpu.VMEM((set_size[1] * 80, lanes), f32),
            pltpu.VMEM((set_size[1], lanes), f32),
            pltpu.VMEM((8, lanes), jnp.int32),
            pltpu.SemaphoreType.DMA,
        ],
        "mid",
        10**7,
    )(*inbound[:2], x_all, p_x_all, mom_x, todo, right, weighed, left, side_1, side_2)
    y_both = call(
        functools.partial(join_kernel, axes),
        shape((2 * parts_sent * rim + 3 * mom_rows, lanes), f32),
        [vmem] * (3 + len(y_far)),
        vmem,
        [],
        "join",
        10**5,
    )(y_2, y_1, mom_kept, *y_far)
    p_y_both = beside_z(y_both, bz)

    acc_c = call(
        side_kernel,
        acc_shape,
        [smem, smem, vmem, vmem, vmem, anywhere],
        vmem,
        [],
        "side",
        10**7,
    )(todo, found, right_1, weighed_1, left, y_both)
    tail = parts_sent * rim
    if sizes[2] == 2:
        mom_parts = []

        def moments(y_both, p_y_both, parts):
            spans = [slice(tail, tail + mom_rows)]
            if sizes[1] > 2:
                spans.append(slice(2 * tail + mom_rows, 2 * (tail + mom_rows)))
            spans.append(slice(2 * (tail + mom_rows), 2 * tail + 3 * mom_rows))
            return sum(y_both[span] + p_y_both[span] for span in spans)

    else:
        mom_parts = [ring_sum(y_both[tail : tail + mom_rows] + y_both[-2 * mom_rows - tail : -mom_rows - tail] if False else sum(y_both[k] for k in (slice(tail, tail + mom_rows), slice(2 * tail + mom_rows, 2 * tail + 2 * mom_rows), slice(2 * tail + 2 * mom_rows, None))), "gz")]
        moments = lambda y_both, p_y_both, parts: parts[0][...]

    forces = call(
        functools.partial(close_kernel, kinds, axes, grid, moments),
        shape((3, own, lanes), f32),
        [smem] + [vmem] * (9 + len(mom_parts)),
        vmem,
        [
            pltpu.VMEM((set_size[2], 32, lanes), bf16),
            pltpu.VMEM((set_size[2], 32, 2 * lanes), bf16),
            pltpu.VMEM(((set_size[2] + 8) * 80, lanes), f32),
            pltpu.VMEM(((own + 1) * 16, lanes), f32),
            pltpu.VMEM((set_size[2], lanes), f32),
            pltpu.VMEM((8, lanes), jnp.int32),
            pltpu.SMEM((8, lanes), jnp.int32),
            pltpu.SemaphoreType.DMA,
        ],
        "close",
        10**7,
    )(todo, *inbound[2:], y_both, p_y_both, left, acc_a, acc_b, acc_c, mine, *mom_parts)
    return forces.reshape(3, bx, by, bz, slots)


def solution(mesh):
    in_specs = (
        P(None, "gx", "gy", "gz", None),
        P(None, "gx", "gy", "gz", None),
        P(None, "gx", "gy", "gz", None),
        P("gx", "gy", "gz"),
        P(("gx", "gy", "gz")),
        P(("gx", "gy", "gz")),
    )
    out_specs = P(None, "gx", "gy", "gz", None)
    return jax.shard_map(body, mesh=mesh, in_specs=in_specs, out_specs=out_specs, check_vma=False)
```
